512 devices in a mesh: shot: 4 (over y_hi, core), gx: 16 (over x, y_lo), gy: 8 (over z).
Axes of the slice: x: 4, y: 8 (y_hi: 2, y_lo: 4; y = y_hi * 4 + y_lo), z: 8, core: 2. Of those that a mesh axis runs over, the one named last changes fastest.
Arguments:
- mean_velocity: float32 [128, 256, 128], P('gx', 'gy'), may hold values from 0.8 to 1.2
- log_scale: float32 [128, 256, 128], P('gx', 'gy'), may hold values from -4 to -2.3
- shot_noise: float32 [4, 128, 256, 128], P('shot', 'gx', 'gy'), may hold values from -4 to 4
- checkpoint_prev: float32 [4, 128, 256, 128], P('shot', 'gx', 'gy'), may hold values from -6 to 6
- checkpoint_now: float32 [4, 128, 256, 128], P('shot', 'gx', 'gy'), may hold values from -6 to 6
- adjoint_next: float32 [4, 128, 256, 128], P('shot', 'gx', 'gy'), may hold values from -6 to 6
- adjoint_now: float32 [4, 128, 256, 128], P('shot', 'gx', 'gy'), may hold values from -6 to 6
- wavelet: float32 [4, 64], P('shot'), may hold values from -1200 to 1200
- source_column: int32 [4], P('shot'), may hold values from 0 to 32767
- receiver_column: int32 [4, 8192], P('shot'), may hold values from 0 to 32767
- observed: float32 [4, 4, 8192], P('shot', None, ('gx', 'gy')), may hold values from -10 to 10
- start_step: int32 [1], replicated, may hold values from 0 to 60
Outputs:
- grad_mean: float32 [128, 256, 128], P('gx', 'gy')
- grad_log_scale: float32 [128, 256, 128], P('gx', 'gy')
The draws below stay inside these ranges and needn't reach their ends.
Inputs may be any that keep to these rules, and one draw needn't show every extreme that they name: `receiver_column`: column x * 256 + y of the cell column holding each receiver; receivers sit at depth 3; several receivers may share a cell. `source_column`: column x * 256 + y of each shot's source, at depth 6. The window reads wavelet samples start_step to start_step + 3.
All inputs are finite; a program needn't handle non-finite values.
Results may differ from the reference program's by a relative error of at most 0.0003.
Values sent between devices are 32-bit elements; how exact they have to be, the bound alone decides.
No kernel may reach another device: no remote copies, remote signals or barrier semaphores. Data moves between devices by JAX's collectives and lax.ppermute only.
A program may use at most 64 MiB of HBM per device.

```python
import jax
import jax.numpy as jnp
from jax import lax

STEPS = 4
WAVE_LEN = 64
SRC_DEPTH = 6
REC_DEPTH = 3
SHOTS = 4
NX = 128
NY = 256
NZ = 128
NREC = 8192


def place_ends(array, stream_key, least, high):
    dims = array.shape
    place = [jax.random.randint(jax.random.fold_in(stream_key, axis), (), 0, dims[axis]) for axis in range(len(dims))]
    array = array.at[tuple(place)].set(least)
    longest = dims.index(max(dims))
    place[longest] = (place[longest] + 1) % dims[longest]
    return array.at[tuple(place)].set(high)


def levels(stream_key, extent, shards, smallest, high):
    level = 1.0
    for dim, blocks in shards:
        heights = jax.random.uniform(jax.random.fold_in(jax.random.fold_in(stream_key, 6), dim), (blocks,), jnp.float32, smallest / len(shards), high / len(shards))
        level = level * jnp.repeat(jnp.exp(heights), extent[dim] // blocks).reshape((-1,) + (1,) * (len(extent) - 1 - dim))
    return level


def gaussian(key, shape, scale, bound, split=(), kind=jnp.bfloat16):
    result = jax.random.normal(key, shape, jnp.float32) * scale
    if len(split) > 0:
        result = levels(key, shape, split, -0.22, 0.18) * result
    return jnp.clip(result, min=-bound, max=bound).astype(kind)


def setup_inputs(seed: int = 0) -> dict:
    key_of = jax.random.split(jax.random.key(seed), 13)
    mean_velocity = jnp.clip(0.8 + 0.40000004 * jax.random.uniform(key_of[0], (NX, NY, NZ), jnp.float32) ** levels(key_of[0], (NX, NY, NZ), ((0, 16), (1, 8)), -0.2, 0.2), 0.8, 1.2)
    log_scale = jnp.clip(-4.0 + 1.7 * jax.random.uniform(key_of[1], (NX, NY, NZ), jnp.float32) ** levels(key_of[1], (NX, NY, NZ), ((0, 16), (1, 8)), -0.2, 0.2), -4.0, -2.3)
    shot_noise = gaussian(key_of[2], (SHOTS, NX, NY, NZ), 1.0, 4.0, ((0, 4), (1, 16), (2, 8)), jnp.float32)
    checkpoint_prev = gaussian(key_of[3], (SHOTS, NX, NY, NZ), 1.0, 6.0, ((0, 4), (1, 16), (2, 8)), jnp.float32)
    checkpoint_now = gaussian(key_of[4], (SHOTS, NX, NY, NZ), 1.0, 6.0, ((0, 4), (1, 16), (2, 8)), jnp.float32)
    adjoint_next = gaussian(key_of[5], (SHOTS, NX, NY, NZ), 1.0, 6.0, ((0, 4), (1, 16), (2, 8)), jnp.float32)
    adjoint_now = gaussian(key_of[6], (SHOTS, NX, NY, NZ), 1.0, 6.0, ((0, 4), (1, 16), (2, 8)), jnp.float32)
    wavelet = gaussian(key_of[7], (SHOTS, WAVE_LEN), 300.0, 1200.0, ((0, 4),), jnp.float32)
    source_column = place_ends(jax.random.randint(key_of[8], (SHOTS,), 0, NX * NY), jax.random.fold_in(key_of[8], 1), 0, (NX * NY) - 1).astype(jnp.int32)
    receiver_column = place_ends(jax.random.randint(key_of[9], (SHOTS, NREC), 0, NX * NY), jax.random.fold_in(key_of[9], 1), 0, (NX * NY) - 1).astype(jnp.int32)
    observed = gaussian(key_of[10], (SHOTS, STEPS, NREC), 2.0, 10.0, ((0, 4), (2, 128)), jnp.float32)
    start_step = jax.random.randint(key_of[11], (1,), 0, WAVE_LEN - STEPS + 1).astype(jnp.int32)
    return dict(mean_velocity=mean_velocity, log_scale=log_scale, shot_noise=shot_noise, checkpoint_prev=checkpoint_prev, checkpoint_now=checkpoint_now, adjoint_next=adjoint_next, adjoint_now=adjoint_now, wavelet=wavelet, source_column=source_column, receiver_column=receiver_column, observed=observed, start_step=start_step)


stencil_weights = (-205.0 / 72.0, 8.0 / 5.0, -1.0 / 5.0, 8.0 / 315.0, -1.0 / 560.0)
courant_sq = 0.0625
prior_var = 0.01


def stencil(padded, size_x, size_y):
    center = padded[4:4 + size_x, 4:4 + size_y]
    size_z = center.shape[2]
    padded_z = jnp.pad(center, ((0, 0), (0, 0), (4, 4)))
    running = 3.0 * stencil_weights[0] * center
    for offset in range(1, 5):
        beside = padded[4 + offset:4 + offset + size_x, 4:4 + size_y] + padded[4 - offset:4 - offset + size_x, 4:4 + size_y]
        beside = beside + padded[4:4 + size_x, 4 + offset:4 + offset + size_y] + padded[4:4 + size_x, 4 - offset:4 - offset + size_y]
        beside = beside + padded_z[:, :, 4 + offset:4 + offset + size_z] + padded_z[:, :, 4 - offset:4 - offset + size_z]
        running = running + stencil_weights[offset] * beside
    return running


def laplace(wavefield):
    padded = jnp.pad(wavefield, ((4, 4), (4, 4), (0, 0)))
    return stencil(padded, wavefield.shape[0], wavefield.shape[1])


def reference(mean_velocity, log_scale, shot_noise, checkpoint_prev, checkpoint_now, adjoint_next, adjoint_now, wavelet, source_column, receiver_column, observed, start_step):
    width_y = mean_velocity.shape[1]
    spread = jnp.exp(log_scale)
    first = start_step[0].astype(jnp.int32)

    def one_shot(shot_args):
        noise_here, wave_prev, wave_now, adj_later, adj_now, wave_shot, src_cell, rec_cols, obs_shot = shot_args
        velocity = mean_velocity + spread * noise_here
        coefficient = courant_sq * velocity * velocity
        src_x = src_cell // width_y
        src_y = src_cell % width_y
        rec_x = rec_cols // width_y
        rec_y = rec_cols % width_y
        samples = lax.dynamic_slice_in_dim(wave_shot, first, STEPS)
        stored_laps = []
        traces = []
        for step in range(STEPS):
            laplacian = laplace(wave_now)
            stored_laps.append(laplacian)
            wave_next = 2.0 * wave_now - wave_prev + coefficient * laplacian
            wave_next = wave_next.at[src_x, src_y, SRC_DEPTH].add(samples[step])
            wave_prev, wave_now = wave_now, wave_next
            traces.append(wave_now[rec_x, rec_y, REC_DEPTH])
        residual = jnp.stack(traces) - obs_shot
        imaging = jnp.zeros_like(mean_velocity)
        for step in range(STEPS, 0, -1):
            earlier = 2.0 * adj_now - adj_later + laplace(coefficient * adj_now)
            earlier = earlier.at[rec_x, rec_y, REC_DEPTH].add(residual[step - 1])
            imaging = imaging + earlier * stored_laps[step - 1]
            adj_later, adj_now = adj_now, earlier
        velocity_grad = 2.0 * courant_sq * velocity * imaging
        return velocity_grad, velocity_grad * noise_here

    grads, weighted = lax.map(one_shot, (shot_noise, checkpoint_prev, checkpoint_now, adjoint_next, adjoint_now, wavelet, source_column, receiver_column, observed))
    grad_mean = jnp.sum(grads, axis=0)
    grad_log_scale = spread * jnp.sum(weighted, axis=0) + jnp.exp(2.0 * log_scale) / prior_var - 1.0
    return grad_mean, grad_log_scale
```

```python
import jax
import jax.numpy as jnp
from jax import lax
from jax.sharding import PartitionSpec as P

STEPS = 4
SRC_DEPTH = 6
REC_DEPTH = 3
W = 4
SLAB = 16

stencil_weights = (-205.0 / 72.0, 8.0 / 5.0, -1.0 / 5.0, 8.0 / 315.0, -1.0 / 560.0)
courant_sq = 0.0625
prior_var = 0.01


def shift(x, axis, k):
    n = lax.axis_size(axis)
    return lax.ppermute(x, axis, [(i, i + k) for i in range(n) if 0 <= i + k < n])


def swap_x(low, high):
    return shift(high, "gx", 1), shift(low, "gx", -1)


def swap_y(low, high):
    return shift(high, "gy", 1), shift(low, "gy", -1)


def star(center, pad_x, pad_y):
    nx, ny, nz = center.shape
    pad_z = jnp.pad(center, ((0, 0), (0, 0), (W, W)))
    out = 3.0 * stencil_weights[0] * center
    for k in range(1, W + 1):
        beside = pad_x[W + k : W + k + nx] + pad_x[W - k : W - k + nx]
        beside = beside + pad_y[:, W + k : W + k + ny] + pad_y[:, W - k : W - k + ny]
        beside = beside + pad_z[:, :, W + k : W + k + nz] + pad_z[:, :, W - k : W - k + nz]
        out = out + stencil_weights[k] * beside
    return out


def star_inner(block):
    return star(block[W:-W, W:-W], block[:, W:-W], block[W:-W])


def local(
    mean_velocity,
    log_scale,
    shot_noise,
    checkpoint_prev,
    checkpoint_now,
    adjoint_next,
    adjoint_now,
    wavelet,
    source_column,
    receiver_column,
    observed,
    start_step,
):
    sx, sy, sz = mean_velocity.shape
    ngx, ngy, nshot = lax.axis_size("gx"), lax.axis_size("gy"), lax.axis_size("shot")
    width_y = sy * ngy
    ix, iy = lax.axis_index("gx"), lax.axis_index("gy")
    ax, ay = ix * sx, iy * sy
    noise = shot_noise[0]
    spread = jnp.exp(log_scale)
    velocity = mean_velocity + spread * noise
    coef = courant_sq * velocity * velocity

    row = lax.broadcasted_iota(jnp.int32, (sx, sy, sz), 0)
    col = lax.broadcasted_iota(jnp.int32, (sx, sy, sz), 1)
    dep = lax.broadcasted_iota(jnp.int32, (sx, sy, sz), 2)
    src = source_column[0]
    at_source = (row == src // width_y - ax) & (col == src % width_y - ay) & (dep == SRC_DEPTH)
    samples = lax.dynamic_slice_in_dim(wavelet[0], start_step[0], STEPS)

    p_prev, p = checkpoint_prev[0], checkpoint_now[0]
    q_later, q = adjoint_next[0], adjoint_now[0]
    laps, planes, free = [], [], []

    cslab = coef[:, :, :SLAB]
    for n in range(STEPS):
        s = coef * q
        xl = [p[:W], s[:W]]
        xh = [p[sx - W :], s[sx - W :]]
        yl = [p[:, :W], s[:, :W]]
        yh = [p[:, sy - W :], s[:, sy - W :]]
        from_l, from_r = swap_x(jnp.concatenate(xl, 0), jnp.concatenate(xh, 0))
        from_d, from_u = swap_y(jnp.concatenate(yl, 1), jnp.concatenate(yh, 1))
        if n == 0:
            cd, cu = swap_y(cslab[:, :8].reshape(sx, 128), cslab[:, sy - 8 :].reshape(sx, 128))
            cd, cu = cd.reshape(sx, 8, SLAB), cu.reshape(sx, 8, SLAB)
            cy = jnp.concatenate([cd, cslab, cu], 1)
        if n == 1:
            cflat = cy.reshape(sx, -1, 128)
            cl, cr = swap_x(cflat, cflat)
            cext = jnp.concatenate([cl.reshape(cy.shape), cy, cr.reshape(cy.shape)], 0)
        lap = star(
            p,
            jnp.concatenate([from_l[:W], p, from_r[:W]], 0),
            jnp.concatenate([from_d[:, :W], p, from_u[:, :W]], 1),
        )
        lap_s = star(
            s,
            jnp.concatenate([from_l[W:], s, from_r[W:]], 0),
            jnp.concatenate([from_d[:, W:], s, from_u[:, W:]], 1),
        )
        p_next = 2.0 * p - p_prev + coef * lap + jnp.where(at_source, samples[n], 0.0)
        q_next = 2.0 * q - q_later + lap_s
        p_prev, p = p, p_next
        q_later, q = q, q_next
        laps.append(lap)
        planes.append(p[:, :, REC_DEPTH])
        free.append(q)

    mine = jnp.concatenate(
        [
            planes[3].reshape(-1),
            planes[2].reshape(-1),
            planes[1].reshape(-1),
            coef[:, :, REC_DEPTH].reshape(-1),
            observed[0].reshape(-1),
        ]
    )
    ncell = sx * sy
    everyone = lax.all_to_all(
        jnp.broadcast_to(mine[None], (ngx * ngy, mine.size)), ("gx", "gy"), 0, 0
    )
    grid = everyone[:, : 4 * ncell].reshape(ngx, ngy, 4, sx, sy)
    grid = jnp.pad(grid, ((2, 2), (1, 1), (0, 0), (0, 0), (0, 0)))
    near = lax.dynamic_slice(grid, (ix, iy, 0, 0, 0), (5, 3, 4, sx, sy))
    near = near.transpose(2, 0, 3, 1, 4).reshape(4, 5 * sx, 3 * sy)
    hx, hy = 2 * sx - 12, sy - 12
    near = near[:, hx : hx + sx + 24, hy : hy + sy + 24]
    traces = everyone[:, 4 * ncell :].reshape(ngx * ngy, STEPS, -1).transpose(1, 0, 2)
    traces = traces.reshape(STEPS, -1)
    ex, ey = sx + 24, sy + 24
    rec = receiver_column[0]
    rx = rec // width_y - ax + 12
    ry = rec % width_y - ay + 12
    hot_x = (lax.broadcasted_iota(jnp.int32, (ex, rec.size), 0) == rx[None]).astype(jnp.float32)
    hot_y = (lax.broadcasted_iota(jnp.int32, (ey, rec.size), 0) == ry[None]).astype(jnp.float32)
    values = jnp.concatenate([traces, jnp.ones((1, rec.size), jnp.float32)], 0)
    table = (values[:, None, :] * hot_x[None]).reshape(-1, rec.size)
    sums = lax.dot_general(
        table, hot_y, (((1,), (1,)), ((), ())), precision=lax.Precision.HIGHEST
    ).reshape(STEPS + 1, ex, ey)
    count = sums[STEPS]

    def lift(plane):
        return jnp.pad(plane[:, :, None], ((0, 0), (0, 0), (REC_DEPTH, SLAB - 1 - REC_DEPTH)))

    r3 = count * near[0] - sums[3]
    in2 = (count * near[1] - sums[2])[4:-4, 4:-4]
    in1 = (count * near[2] - sums[1])[8:-8, 8:-8]
    in0 = count[12:-12, 12:-12] * planes[0] - sums[0][12:-12, 12:-12]
    r3 = lift(r3)
    c3 = lift(near[3])
    r2 = 2.0 * r3[4:-4, 4:-4] + star_inner(c3 * r3) + lift(in2)
    r1 = 2.0 * r2[4:-4, 4:-4] - r3[8:-8, 8:-8] + star_inner(cext * r2) + lift(in1)
    r0 = (
        2.0 * r1[4:-4, 4:-4]
        - r2[8:-8, 8:-8]
        + star_inner(cext[4:-4, 4:-4] * r1)
        + lift(in0)
    )
    r = [r0, r1[4:-4, 4:-4], r2[8:-8, 8:-8], r3[12:-12, 12:-12]]
    imaging = jnp.zeros_like(mean_velocity)
    for n in range(STEPS):
        adj = free[STEPS - 1 - n] + jnp.pad(r[n], ((0, 0), (0, 0), (0, sz - SLAB)))
        imaging = imaging + adj * laps[n]
    velocity_grad = 2.0 * courant_sq * velocity * imaging
    both = jnp.stack([velocity_grad, velocity_grad * noise])
    parts = both.reshape(2, nshot, sx // nshot, sy, sz).transpose(1, 0, 2, 3, 4)
    quarter = lax.all_to_all(parts, "shot", 0, 0).sum(0)
    total = lax.all_gather(quarter, "shot", axis=0)
    total_grad = total[:, 0].reshape(sx, sy, sz)
    total_weighted = total[:, 1].reshape(sx, sy, sz)
    grad_log_scale = spread * total_weighted + jnp.exp(2.0 * log_scale) / prior_var - 1.0
    return (total_grad, grad_log_scale)


def solution(mesh):
    return jax.shard_map(
        local,
        mesh=mesh,
        in_specs=(
            P("gx", "gy", None),
            P("gx", "gy", None),
            P("shot", "gx", "gy", None),
            P("shot", "gx", "gy", None),
            P("shot", "gx", "gy", None),
            P("shot", "gx", "gy", None),
            P("shot", "gx", "gy", None),
            P("shot", None),
            P("shot"),
            P("shot", None),
            P("shot", None, ("gx", "gy")),
            P(),
        ),
        out_specs=(P("gx", "gy", None), P("gx", "gy", None)),
        check_vma=False,
    )
```

```python
import functools

import jax
import jax.numpy as jnp
from jax import lax
from jax.experimental import pallas as pl
from jax.experimental.pallas import tpu as pltpu
from jax.sharding import PartitionSpec as P

STEPS = 4
SRC_DEPTH = 6
REC_DEPTH = 3
NX, NY, NZ = 8, 32, 128
W = 4
SLAB = 16

C0, C1, C2, C3, C4 = (-205.0 / 72.0, 8.0 / 5.0, -1.0 / 5.0, 8.0 / 315.0, -1.0 / 560.0)
CK = (C0, C1, C2, C3, C4)
courant_sq = 0.0625
prior_var = 0.01

f32 = jnp.float32
VM = pl.BlockSpec(memory_space=pltpu.VMEM)
SM = pl.BlockSpec(memory_space=pltpu.SMEM)


def sds(*shape):
    return jax.ShapeDtypeStruct(shape, f32)


def lanes(rows=1):
    return lax.broadcasted_iota(jnp.int32, (rows, 128), 1)


def roll(x, k):
    k = k % 128
    return x if k == 0 else pltpu.roll(x, k, 1)


def pack(rows):
    part = lanes() // SLAB
    out = jnp.where(part == 0, rows[0], 0.0)
    for x in range(1, NX):
        out = jnp.where(part == x, roll(rows[x], SLAB * x), out)
    return out


def put_strips(i, p, s, xlo, xhi, ylo, yhi):
    out, j = (xlo, i) if i < W else (xhi, i - W)
    out[NY * j : NY * (j + 1)] = p
    out[NY * (W + j) : NY * (W + j + 1)] = s
    ylo[8 * i : 8 * i + 4] = p[:W]
    ylo[8 * i + 4 : 8 * i + 8] = s[:W]
    yhi[8 * i : 8 * i + 4] = p[NY - W :]
    yhi[8 * i + 4 : 8 * i + 8] = s[NY - W :]


def first_kernel(mean, logs, noise, p, q, obs, c_out, xlo, xhi, ylo, yhi, cpk):
    rows = []
    for i in range(NX):
        vel = mean[i] + jnp.exp(logs[i]) * noise[i]
        c = courant_sq * vel * vel
        c_out[i] = c
        put_strips(i, p[i], c * q[i], xlo, xhi, ylo, yhi)
        rows.append(c)
    slab = pack(rows)
    cpk[...] = slab
    ylo[64:80] = slab[:16]
    yhi[64:80] = slab[16:]
    ylo[80:88] = obs[...]
    yhi[80:88] = obs[...]


def fill(buf, field, rows_l, rows_r, md, mu, at, keep_d, keep_u):
    for i in range(NX):
        buf[W + i, 8:40] = field[i]
        buf[W + i, 4:8] = jnp.where(keep_d, md[8 * i + at : 8 * i + at + 4], 0.0)
        buf[W + i, 40:44] = jnp.where(keep_u, mu[8 * i + at : 8 * i + at + 4], 0.0)
    for j in range(W):
        buf[j, 8:40] = rows_l[j]
        buf[W + NX + j, 8:40] = rows_r[j]


def laplace(buf, i, wz):
    here = buf[W + i, 8:40]
    out = (3.0 * C0) * here
    for k in range(1, W + 1):
        beside = buf[W + i + k, 8:40] + buf[W + i - k, 8:40]
        beside = beside + buf[W + i, 8 + k : 40 + k] + buf[W + i, 8 - k : 40 - k]
        out = out + CK[k] * beside
        out = out + wz[k][0] * roll(here, -k) + wz[k][1] * roll(here, k)
    return out


def step_kernel(n, meta, samples, c, p, pp, q, ql, ml, mr, md, mu, oc, *rest):
    rest = list(rest)
    bufp, bufs = rest[-2:]
    rest = rest[:-2]
    take = lambda: rest.pop(0)
    cpk = cl = cr = lap_other = q3 = img = None
    if n == 1:
        cext = take()
    if n == 2:
        lap_other = take()
    if n == 3:
        lap_other, q3, img = take(), take(), take()
    lpk, oc_out, qn = take(), take(), take()
    if n < 3:
        pn, xlo, xhi, ylo, yhi = take(), take(), take(), take(), take()
    else:
        pn = take()
    if n == 0:
        lap_out, cext = take(), take()
    if n == 1:
        lap_out = take()
    if n == 2:
        img_out = take()
    if n == 3:
        img_out, mat = take(), take()

    keep_d, keep_u = meta[3] > 0, meta[4] > 0
    lane = lanes()
    wz = [None] + [
        (jnp.where(lane < NZ - k, CK[k], 0.0), jnp.where(lane >= k, CK[k], 0.0))
        for k in range(1, W + 1)
    ]

    def strip(m, at):
        return [m[at + NY * j : at + NY * (j + 1)] for j in range(W)]

    fill(bufp, p, strip(ml, 0), strip(mr, 0), md, mu, 0, keep_d, keep_u)
    s = [c[i] * q[i] for i in range(NX)]
    fill(bufs, s, strip(ml, 128), strip(mr, 128), md, mu, 4, keep_d, keep_u)
    slab = jnp.zeros((NY, NZ), f32)
    for i in range(NX):
        lap = laplace(bufp, i, wz)
        slab = jnp.where(lane // SLAB == i, roll(lap, SLAB * i), slab)
        pn[i] = 2.0 * p[i] - pp[i] + c[i] * lap
        q_new = 2.0 * q[i] - ql[i] + laplace(bufs, i, wz)
        qn[i] = q_new
        if n < 2:
            lap_out[i] = lap
        if n == 2:
            img_out[i] = lap * q[i] + q_new * lap_other[i]
        if n == 3:
            img_out[i] = img[i] + lap * q3[i] + q_new * lap_other[i]
    lpk[...] = slab

    sx, sy = meta[0], meta[1]

    @pl.when((sx >= 0) & (sx < NX) & (sy >= 0) & (sy < NY))
    def _():
        row = pn[sx, pl.ds(sy, 1), :]
        pn[sx, pl.ds(sy, 1), :] = row + jnp.where(lane == SRC_DEPTH, samples[n], 0.0)

    at = 80 if n == 0 else 64
    got_d, got_u = md[at : at + 8], mu[at : at + 8]
    oc_out[...] = oc[...]
    up, turn_u, down, turn_d = ((0, 64, 12, 64), (4, 0, 12, 0), (4, 64, 8, 64), (8, 0, None, 0))[n]
    oc_out[up : up + 4] = oc_out[up : up + 4] + roll(got_u, turn_u)[:4]
    if down is not None:
        oc_out[down : down + 4] = oc_out[down : down + 4] + roll(got_d, turn_d)[:4]

    if n < 3:
        for i in range(NX):
            put_strips(i, pn[i], c[i] * qn[i], xlo, xhi, ylo, yhi)
        ylo[64:72] = got_u
        yhi[64:72] = got_d
    if n == 0:
        cext[0:16] = jnp.where(keep_d, md[64:80], 0.0)
        cext[16:48] = pack([c[i] for i in range(NX)])
        cext[48:64] = jnp.where(keep_u, mu[64:80], 0.0)
        xlo[256:320] = cext[...]
        xhi[256:320] = cext[...]
    if n == 1:
        xlo[256:288] = mr[272:304]
        xhi[256:288] = ml[272:304]
    if n == 3:
        out = jnp.zeros((NY, NZ), f32)
        for i in range(NX):
            for t, row in ((1, None), (2, pp[i]), (3, p[i]), (4, pn[i])):
                if row is not None:
                    to = 4 * i + t - 1
                    out = jnp.where(lane == to, roll(row, to - REC_DEPTH), out)
        mat[...] = out


def chunk_kernel(mat, got_d, got_u, p1, oc, out):
    m = mat[...]
    lane = lanes()
    for i in range(NX):
        m = jnp.where(lane == 4 * i, roll(p1[i], 4 * i - REC_DEPTH), m)
    packed = got_d[...] + roll(m[:16], 32) + roll(m[16:], 64) + roll(got_u[...], 96)
    for g in range(out.shape[0]):
        out[g, 0:16] = oc[...]
        out[g, 16:32] = packed


def lap_packed(buf, g, lo, hi, wz):
    lane = lanes()
    here = buf[g, lo:hi]
    before, after = buf[g - 1, lo:hi], buf[g + 1, lo:hi]
    out = (3.0 * C0) * here
    for k in range(1, W + 1):
        t = SLAB * k
        beside = jnp.where(lane < 128 - t, roll(here, -t), roll(after, -t))
        beside = beside + jnp.where(lane >= t, roll(here, t), roll(before, t))
        beside = beside + buf[g, lo + k : hi + k] + buf[g, lo - k : hi - k]
        out = out + CK[k] * beside
        out = out + wz[k][0] * roll(here, -k) + wz[k][1] * roll(here, k)
    return out


def last_kernel(
    meta, got, keyx, keyy, cext, c1l, c1r, c2l, c2r, lp0, lp1, lp2, lp3, img, mean, logs, noise,
    out, table, hoty, x, r3, r2, r1, inj,
):
    ngx = got.shape[0]
    lane = lanes()
    ix = meta[2]
    bf = jnp.bfloat16

    row4 = lax.broadcasted_iota(jnp.int32, (160, 128), 0) // 4
    coly = lax.broadcasted_iota(jnp.int32, (64, 128), 0)

    def build(g, carry):
        for rp in range(4):
            kx = keyx[pl.ds(4 * g + rp, 1), :]
            ky = keyy[pl.ds(4 * g + rp, 1), :]
            at = pl.ds(pl.multiple_of((4 * g + rp) * 128, 128), 128)
            val = got[g, 4 * rp : 4 * rp + 4, :]
            hi = val.astype(bf).astype(f32)
            mid = (val - hi).astype(bf).astype(f32)
            low = val - hi - mid
            hot = row4 == kx
            for part, v in enumerate((hi, mid, low)):
                v8 = jnp.concatenate([v, v], 0)
                v160 = jnp.concatenate([v8] * 20, 0)
                table[160 * part : 160 * (part + 1), at] = jnp.where(hot, v160, 0.0).astype(bf)
            table[480:640, at] = jnp.where(hot, 1.0, 0.0).astype(bf)
            hoty[:, at] = jnp.where(coly == ky, 1.0, 0.0).astype(bf)
        return carry

    lax.fori_loop(0, ngx, build, 0)
    sums = lax.dot_general(
        table[...], hoty[...], (((1,), (1,)), ((), ())), preferred_element_type=f32
    )
    seen = sums[0:160] + sums[160:320] + sums[320:480]
    count = sums[480:640]
    zero = jnp.zeros((96, 64), f32)
    seen = jnp.concatenate([seen, zero], 0)
    count = jnp.concatenate([count, zero], 0)
    both = jnp.concatenate([seen, count], 1)
    tr = [both[:128].T, both[128:].T]

    k_in = lax.broadcasted_iota(jnp.int32, (128, 512), 0)
    k_out = lax.broadcasted_iota(jnp.int32, (128, 512), 1)
    spread_to = jnp.where(
        (k_in < 32) & (k_out == (k_in % 4) * 128 + (k_in // 4) * SLAB + REC_DEPTH), 1.0, 0.0
    )
    dense = []
    for g in range(5):
        src = ix + (g - 2)
        ok = (src >= 0) & (src < ngx)
        blk = got[jnp.clip(src, 0, ngx - 1), 16:32, :]
        m = jnp.concatenate([roll(blk, -32 * t) for t in range(4)], 0)
        m = jnp.where(ok, m, 0.0)
        t = tr[g // 4]
        s_g = roll(t[:64], -32 * (g % 4))
        n_g = roll(t[64:], -32 * (g % 4))
        dense.append(n_g * m - s_g)
    inj[...] = jnp.dot(
        jnp.concatenate(dense, 0), spread_to,
        precision=lax.Precision.HIGHEST, preferred_element_type=f32,
    )

    def j(n, g, lo, hi):
        return inj[64 * g + lo : 64 * g + hi, 128 * n : 128 * (n + 1)]

    d = lane % SLAB
    wz = [None] + [
        (jnp.where(d < SLAB - k, CK[k], 0.0), jnp.where(d >= k, CK[k], 0.0))
        for k in range(1, W + 1)
    ]
    coef = {1: c1l, 2: cext, 3: c1r}
    pad = jnp.zeros((16, 128), f32)
    for g in range(5):
        r3[g] = j(3, g, 0, 64)
        if g in coef:
            x[g] = coef[g][...] * r3[g]
    for g, far in ((0, c2l), (4, c2r)):
        x[g, 0:16] = pad
        x[g, 16:48] = far[...] * r3[g, 16:48]
        x[g, 48:64] = pad
    for g in (1, 2, 3):
        r2[g] = 2.0 * r3[g, 8:56] + lap_packed(x, g, 8, 56, wz) + j(2, g, 8, 56)
    x[0] = jnp.zeros((64, 128), f32)
    x[4] = jnp.zeros((64, 128), f32)
    for g in (1, 2, 3):
        x[g, 0:8] = pad[:8]
        x[g, 8:56] = coef[g][8:56] * r2[g]
        x[g, 56:64] = pad[:8]
    for g in (1, 2, 3):
        r1[g] = 2.0 * r2[g] - r3[g, 8:56] + lap_packed(x, g, 8, 56, wz) + j(1, g, 8, 56)
    for g in (1, 2, 3):
        x[g, 8:56] = coef[g][8:56] * r1[g]
    r0 = 2.0 * r1[2, 8:40] - r2[2, 8:40] + lap_packed(x, 2, 16, 48, wz) + j(0, 2, 16, 48)
    corr = r0 * lp0[...] + r1[2, 8:40] * lp1[...] + r2[2, 8:40] * lp2[...]
    corr = corr + r3[2, 16:48] * lp3[...]

    per = NX // out.shape[0]
    for i in range(NX):
        image = img[i] + jnp.where(lane < SLAB, roll(corr, -SLAB * i), 0.0)
        z = noise[i]
        vel = mean[i] + jnp.exp(logs[i]) * z
        grad = (2.0 * courant_sq) * vel * image
        out[i // per, 0, i % per] = grad
        out[i // per, 1, i % per] = grad * z


def call(kernel, outs, scratch=(), smem=0):
    def go(*args):
        return pl.pallas_call(
            kernel,
            out_shape=outs,
            in_specs=[SM] * smem + [VM] * (len(args) - smem),
            out_specs=jax.tree.map(lambda _: VM, outs),
            scratch_shapes=list(scratch),
            compiler_params=pltpu.CompilerParams(vmem_limit_bytes=48 * 2**20),
        )(*args)

    return go


def shift(x, axis, k, wrap=False):
    n = lax.axis_size(axis)
    return lax.ppermute(x, axis, [(i, (i + k) % n) for i in range(n) if wrap or 0 <= i + k < n])


def local(
    mean_velocity,
    log_scale,
    shot_noise,
    checkpoint_prev,
    checkpoint_now,
    adjoint_next,
    adjoint_now,
    wavelet,
    source_column,
    receiver_column,
    observed,
    start_step,
):
    ngx, ngy, nshot = lax.axis_size("gx"), lax.axis_size("gy"), lax.axis_size("shot")
    width_y = NY * ngy
    ix, iy = lax.axis_index("gx"), lax.axis_index("gy")
    noise = shot_noise[0]
    src = source_column[0]
    meta = jnp.stack(
        [
            src // width_y - ix * NX,
            src % width_y - iy * NY,
            ix,
            (iy > 0).astype(jnp.int32),
            (iy < ngy - 1).astype(jnp.int32),
        ]
    ).astype(jnp.int32)
    samples = lax.dynamic_slice_in_dim(wavelet[0], start_step[0], STEPS)
    obs = jnp.pad(observed[0], ((0, 4), (0, 64)))
    rec = receiver_column[0].reshape(ngx, ngy, -1)
    rec = lax.dynamic_slice_in_dim(jnp.concatenate([rec, rec], 1), iy, ngy, 1).reshape(-1, 128)
    keyx = rec // width_y - ix * NX + 16
    keyy = rec % width_y - iy * NY + 16

    p_prev, p = checkpoint_prev[0], checkpoint_now[0]
    q_later, q = adjoint_next[0], adjoint_now[0]
    F = sds(NX, NY, NZ)
    coef, xlo, xhi, ylo, yhi, cpk = call(
        first_kernel, (F, sds(256, 128), sds(256, 128), sds(88, 128), sds(88, 128), sds(NY, NZ))
    )(mean_velocity, log_scale, noise, p, q, obs)
    oc = jnp.pad(observed[0], ((0, 12), (0, 64)))
    buf = pltpu.VMEM((NX + 2 * W, 48, NZ), f32)
    slabs, keep = [], {}
    for n in range(STEPS):
        ml, mr = shift(xhi, "gx", 1), shift(xlo, "gx", -1)
        md, mu = shift(yhi, "gy", 1, True), shift(ylo, "gy", -1, True)
        extra = ()
        if n == 1:
            extra = (keep["cext"],)
        if n == 2:
            extra = (keep["lap1"],)
        if n == 3:
            extra = (keep["lap0"], keep["q3"], keep["img"])
        outs = [sds(NY, NZ), sds(16, 128), F, F]
        if n < 3:
            rows = (320, 288, 256)[n]
            outs += [sds(rows, 128), sds(rows, 128), sds(72, 128), sds(72, 128)]
        outs += {0: [F, sds(64, 128)], 1: [F], 2: [F], 3: [F, sds(NY, NZ)]}[n]
        res = call(functools.partial(step_kernel, n), tuple(outs), (buf, buf), smem=2)(
            meta, samples, coef, p, p_prev, q, q_later, ml, mr, md, mu, oc, *extra
        )
        lpk, oc, q_next, p_next = res[:4]
        slabs.append(lpk)
        if n < 3:
            xlo, xhi, ylo, yhi = res[4:8]
        if n == 0:
            keep["lap0"], keep["cext"], keep["q3"], keep["p1"] = res[8], res[9], q_next, p_next
        if n == 1:
            keep["lap1"] = res[8]
            c1l, c1r = ml[256:320], mr[256:320]
        if n == 2:
            keep["img"] = res[8]
            c2l, c2r = ml[256:288], mr[256:288]
        if n == 3:
            img, mat = res[4], res[5]
        p_prev, p = p, p_next
        q_later, q = q, q_next

    mat_d, mat_u = shift(mat[16:], "gy", 1), shift(mat[:16], "gy", -1)
    chunk = call(chunk_kernel, sds(ngx, 32, 128))(mat, mat_d, mat_u, keep["p1"], oc)
    got = lax.all_to_all(chunk, "gx", 0, 0)
    nrec = receiver_column.shape[1]
    g5 = pltpu.VMEM((5, 64, 128), f32)
    g48 = pltpu.VMEM((5, 48, 128), f32)
    parts = call(
        last_kernel,
        sds(nshot, 2, NX // nshot, NY, NZ),
        (
            pltpu.VMEM((640, nrec), jnp.bfloat16),
            pltpu.VMEM((64, nrec), jnp.bfloat16),
            g5,
            g5,
            g48,
            g48,
            pltpu.VMEM((320, 512), f32),
        ),
        smem=1,
    )(
        meta, got, keyx, keyy, keep["cext"], c1l, c1r, c2l, c2r, *slabs, img,
        mean_velocity, log_scale, noise,
    )
    quarter = lax.all_to_all(parts, "shot", 0, 0).sum(0)
    total = lax.all_gather(quarter, "shot", axis=0)
    total_grad = total[:, 0].reshape(NX, NY, NZ)
    total_weighted = total[:, 1].reshape(NX, NY, NZ)
    spread = jnp.exp(log_scale)
    grad_log_scale = spread * total_weighted + jnp.exp(2.0 * log_scale) / prior_var - 1.0
    return (total_grad, grad_log_scale)


def solution(mesh):
    return jax.shard_map(
        local,
        mesh=mesh,
        in_specs=(
            P("gx", "gy", None),
            P("gx", "gy", None),
            P("shot", "gx", "gy", None),
            P("shot", "gx", "gy", None),
            P("shot", "gx", "gy", None),
            P("shot", "gx", "gy", None),
            P("shot", "gx", "gy", None),
            P("shot", None),
            P("shot"),
            P("shot", None),
            P("shot", None, ("gx", "gy")),
            P(),
        ),
        out_specs=(P("gx", "gy", None), P("gx", "gy", None)),
        check_vma=False,
    )
```

```python
import functools

import jax
import jax.numpy as jnp
from jax import lax
from jax.experimental import pallas as pl
from jax.experimental.pallas import tpu as pltpu
from jax.sharding import PartitionSpec as P

STEPS = 4
SRC_DEPTH = 6
REC_DEPTH = 3
NX, NY, NZ = 8, 32, 128
W = 4
SLAB = 16

C0, C1, C2, C3, C4 = (-205.0 / 72.0, 8.0 / 5.0, -1.0 / 5.0, 8.0 / 315.0, -1.0 / 560.0)
CK = (C0, C1, C2, C3, C4)
courant_sq = 0.0625
prior_var = 0.01

f32 = jnp.float32
VM = pl.BlockSpec(memory_space=pltpu.VMEM)
SM = pl.BlockSpec(memory_space=pltpu.SMEM)


def sds(*shape):
    return jax.ShapeDtypeStruct(shape, f32)


def lanes(rows=1):
    return lax.broadcasted_iota(jnp.int32, (rows, 128), 1)


def roll(x, k):
    k = k % 128
    return x if k == 0 else pltpu.roll(x, k, 1)


def pack(rows):
    part = lanes() // SLAB
    out = jnp.where(part == 0, rows[0], 0.0)
    for x in range(1, NX):
        out = jnp.where(part == x, roll(rows[x], SLAB * x), out)
    return out


def put_strips(i, p, s, xlo, xhi, ylo, yhi):
    out, j = (xlo, i) if i < W else (xhi, i - W)
    out[NY * j : NY * (j + 1)] = p
    out[NY * (W + j) : NY * (W + j + 1)] = s
    ylo[8 * i : 8 * i + 4] = p[:W]
    ylo[8 * i + 4 : 8 * i + 8] = s[:W]
    yhi[8 * i : 8 * i + 4] = p[NY - W :]
    yhi[8 * i + 4 : 8 * i + 8] = s[NY - W :]


def first_kernel(
    mean, logs, noise, p, q, obs, c_out, v_out, xlo, xhi, ylo, yhi, cpk, oc
):
    oc[...] = jnp.zeros((16, 128), f32)
    oc[0:4, 0:64] = obs[...]
    for y in (ylo, yhi):
        y[80:88] = jnp.zeros((8, 128), f32)
        y[80:84, 0:64] = obs[...]
    rows = []
    for i in range(NX):
        vel = mean[i] + jnp.exp(logs[i]) * noise[i]
        c = courant_sq * vel * vel
        v_out[i] = vel
        c_out[i] = c
        put_strips(i, p[i], c * q[i], xlo, xhi, ylo, yhi)
        rows.append(c)
    slab = pack(rows)
    cpk[...] = slab
    ylo[64:80] = slab[:16]
    yhi[64:80] = slab[16:]


def fill(buf, field, rows_l, rows_r, md, mu, at, keep_d, keep_u):
    for i in range(NX):
        buf[W + i, 8:40] = field[i]
        buf[W + i, 4:8] = jnp.where(keep_d, md[8 * i + at : 8 * i + at + 4], 0.0)
        buf[W + i, 40:44] = jnp.where(keep_u, mu[8 * i + at : 8 * i + at + 4], 0.0)
    for j in range(W):
        buf[j, 8:40] = rows_l[j]
        buf[W + NX + j, 8:40] = rows_r[j]


def laplace(buf, i, wz):
    here = buf[W + i, 8:40]
    out = (3.0 * C0) * here
    for k in range(1, W + 1):
        beside = buf[W + i + k, 8:40] + buf[W + i - k, 8:40]
        beside = beside + buf[W + i, 8 + k : 40 + k] + buf[W + i, 8 - k : 40 - k]
        out = out + CK[k] * beside
        out = out + wz[k][0] * roll(here, -k) + wz[k][1] * roll(here, k)
    return out


def step_kernel(n, source, start, wavelet, c, p, pp, q, ql, ml, mr, md, mu, oc, *rest):
    ix, iy, ngy = lax.axis_index("gx"), lax.axis_index("gy"), lax.axis_size("gy")
    rest = list(rest)
    bufp, bufs = rest[-2:]
    rest = rest[:-2]
    take = lambda: rest.pop(0)
    if n == 1:
        cext = take()
    if n == 2:
        lap_other = take()
    if n == 3:
        lap_other, q3, img, vel, noise = take(), take(), take(), take(), take()
    lpk, oc_out, qn = take(), take(), take()
    if n < 3:
        pn, xlo, xhi, ylo, yhi = take(), take(), take(), take(), take()
    else:
        pn = take()
    if n == 0:
        lap_out, cext = take(), take()
    if n == 1:
        lap_out = take()
    if n == 2:
        img_out = take()
    if n == 3:
        mat, mat_lo, mat_hi, own, sent = take(), take(), take(), take(), take()

    keep_d, keep_u = iy > 0, iy < ngy - 1
    lane = lanes()
    wz = [None] + [
        (jnp.where(lane < NZ - k, CK[k], 0.0), jnp.where(lane >= k, CK[k], 0.0))
        for k in range(1, W + 1)
    ]

    def strip(m, at):
        return [m[at + NY * j : at + NY * (j + 1)] for j in range(W)]

    fill(bufp, p, strip(ml, 0), strip(mr, 0), md, mu, 0, keep_d, keep_u)
    s = [c[i] * q[i] for i in range(NX)]
    fill(bufs, s, strip(ml, 128), strip(mr, 128), md, mu, 4, keep_d, keep_u)
    slab = jnp.zeros((NY, NZ), f32)
    for i in range(NX):
        lap = laplace(bufp, i, wz)
        slab = jnp.where(lane // SLAB == i, roll(lap, SLAB * i), slab)
        pn[i] = 2.0 * p[i] - pp[i] + c[i] * lap
        q_new = 2.0 * q[i] - ql[i] + laplace(bufs, i, wz)
        qn[i] = q_new
        if n < 2:
            lap_out[i] = lap
        if n == 2:
            img_out[i] = lap * q[i] + q_new * lap_other[i]
        if n == 3:
            image = img[i] + lap * q3[i] + q_new * lap_other[i]
            grad = (2.0 * courant_sq) * vel[i] * image
            weighted = grad * noise[i]
            first = lax.axis_index("shot") % 2 == 0
            own[i] = jnp.where(first, grad, weighted)
            sent[i] = jnp.where(first, weighted, grad)
    lpk[...] = slab

    sx = source[0] // (NY * ngy) - ix * NX
    sy = source[0] % (NY * ngy) - iy * NY

    @pl.when((sx >= 0) & (sx < NX) & (sy >= 0) & (sy < NY))
    def _():
        row = pn[sx, pl.ds(sy, 1), :]
        pn[sx, pl.ds(sy, 1), :] = row + jnp.where(lane == SRC_DEPTH, wavelet[0, start[0] + n], 0.0)

    at = 80 if n == 0 else 64
    got_d, got_u = md[at : at + 8], mu[at : at + 8]
    oc_out[...] = oc[...]
    up, turn_u, down, turn_d = ((0, 64, 12, 64), (4, 0, 12, 0), (4, 64, 8, 64), (8, 0, None, 0))[n]
    oc_out[up : up + 4] = oc_out[up : up + 4] + roll(got_u, turn_u)[:4]
    if down is not None:
        oc_out[down : down + 4] = oc_out[down : down + 4] + roll(got_d, turn_d)[:4]

    if n < 3:
        for i in range(NX):
            put_strips(i, pn[i], c[i] * qn[i], xlo, xhi, ylo, yhi)
        ylo[64:72] = got_u
        yhi[64:72] = got_d
    if n == 0:
        cext[0:16] = jnp.where(keep_d, md[64:80], 0.0)
        cext[16:48] = pack([c[i] for i in range(NX)])
        cext[48:64] = jnp.where(keep_u, mu[64:80], 0.0)
        xlo[256:320] = cext[...]
        xhi[256:320] = cext[...]
    if n == 1:
        xlo[256:288] = mr[272:304]
        xhi[256:288] = ml[272:304]
    if n == 3:
        out = jnp.zeros((NY, NZ), f32)
        for i in range(NX):
            for t, row in ((2, pp[i]), (3, p[i]), (4, pn[i])):
                to = 4 * i + t - 1
                out = jnp.where(lane == to, roll(row, to - REC_DEPTH), out)
        mat[...] = out
        mat_lo[...] = out[:16]
        mat_hi[...] = out[16:]


def chunk_kernel(mat, got_d, got_u, p1, oc, out):
    m = mat[...]
    lane = lanes()
    for i in range(NX):
        m = jnp.where(lane == 4 * i, roll(p1[i], 4 * i - REC_DEPTH), m)
    packed = got_d[...] + roll(m[:16], 32) + roll(m[16:], 64) + roll(got_u[...], 96)
    for g in range(out.shape[0]):
        out[g, 0:16] = oc[...]
        out[g, 16:32] = packed


def lap_packed(buf, g, lo, hi, wz):
    lane = lanes()
    here = buf[g, lo:hi]
    before, after = buf[g - 1, lo:hi], buf[g + 1, lo:hi]
    out = (3.0 * C0) * here
    for k in range(1, W + 1):
        t = SLAB * k
        beside = jnp.where(lane < 128 - t, roll(here, -t), roll(after, -t))
        beside = beside + jnp.where(lane >= t, roll(here, t), roll(before, t))
        beside = beside + buf[g, lo + k : hi + k] + buf[g, lo - k : hi - k]
        out = out + CK[k] * beside
        out = out + wz[k][0] * roll(here, -k) + wz[k][1] * roll(here, k)
    return out


def table_kernel(rec, vel, noise, keyx, hoty, count, vpk, zpk, hot):
    ix, iy, ngy = lax.axis_index("gx"), lax.axis_index("gy"), lax.axis_size("gy")
    half = ngy // 2
    odd = iy % 2 == 1
    lane = lanes()
    bf = jnp.bfloat16
    row4 = lax.broadcasted_iota(jnp.int32, (160, 128), 0) // 4
    coly = lax.broadcasted_iota(jnp.int32, (64, 128), 0)

    def build(g, carry):
        at = pl.ds(pl.multiple_of(g * 128, 128), 128)
        first = (iy + 2 * (g % half)) % ngy
        second = (first + 1) % ngy
        row_a = rec[pl.ds((g // half) * half + first // 2, 1), :]
        row_b = rec[pl.ds((g // half) * half + second // 2, 1), :]
        row = jnp.where(odd, jnp.where(lane < 64, roll(row_a, 64), roll(row_b, 64)), row_a)
        kx = row // (NY * ngy) - ix * NX + 16
        ky = row % (NY * ngy) - iy * NY + 16
        keyx[pl.ds(g, 1), :] = kx
        hot[:, at] = jnp.where(row4 == kx, 1.0, 0.0).astype(bf)
        hoty[:, at] = jnp.where(coly == ky, 1.0, 0.0).astype(bf)
        return carry

    lax.fori_loop(0, rec.shape[0], build, 0)
    count[...] = lax.dot_general(
        hot[...], hoty[...], (((1,), (1,)), ((), ())), preferred_element_type=f32
    )
    vpk[...] = pack([vel[i] for i in range(NX)])
    zpk[...] = pack([noise[i] for i in range(NX)])


def last_kernel(
    got, keyx, hoty, cnt, cext, ml1, mr1, ml2, mr2, lp0, lp1, lp2, lp3, vpk, zpk, own, other,
    out, table, x, r3, r2, r1, inj,
):
    ngx = got.shape[0]
    lane = lanes()
    ix = lax.axis_index("gx")
    c1l, c1r = ml1.at[256:320], mr1.at[256:320]
    c2l, c2r = ml2.at[256:288], mr2.at[256:288]
    bf = jnp.bfloat16
    row4 = (lax.broadcasted_iota(jnp.int32, (160, 128), 0) // 4).astype(f32).astype(bf)
    none = jnp.zeros((), bf)

    def build(g, carry):
        for rp in range(4):
            at = pl.ds(pl.multiple_of((4 * g + rp) * 128, 128), 128)
            val = got[g, 4 * rp : 4 * rp + 4, :]
            hi = val.astype(bf).astype(f32)
            mid = (val - hi).astype(bf).astype(f32)
            low = val - hi - mid
            kx = jnp.clip(keyx[pl.ds(4 * g + rp, 1), :], -1, 40).astype(f32).astype(bf)
            here = row4 == kx
            for part, v in enumerate((hi, mid, low)):
                v16 = jnp.concatenate([v, v, v, v], 0).astype(bf)
                v160 = jnp.concatenate([v16] * 10, 0)
                table[160 * part : 160 * (part + 1), at] = jnp.where(here, v160, none)
        return carry

    lax.fori_loop(0, ngx, build, 0)
    sums = lax.dot_general(
        table[...], hoty[...], (((1,), (1,)), ((), ())), preferred_element_type=f32
    )
    seen = sums[0:160] + sums[160:320] + sums[320:480]
    zero = jnp.zeros((96, 64), f32)
    seen = jnp.concatenate([seen, zero], 0)
    count = jnp.concatenate([cnt[...], zero], 0)
    both = jnp.concatenate([seen, count], 1)
    tr = [both[:128].T, both[128:].T]

    k_in = lax.broadcasted_iota(jnp.int32, (128, 512), 0)
    k_out = lax.broadcasted_iota(jnp.int32, (128, 512), 1)
    spread_to = jnp.where(
        (k_in < 32) & (k_out == (k_in % 4) * 128 + (k_in // 4) * SLAB + REC_DEPTH), 1.0, 0.0
    )
    dense = []
    for g in range(5):
        src = ix + (g - 2)
        ok = (src >= 0) & (src < ngx)
        blk = got[jnp.clip(src, 0, ngx - 1), 16:32, :]
        m = jnp.concatenate([roll(blk, -32 * t) for t in range(4)], 0)
        m = jnp.where(ok, m, 0.0)
        t = tr[g // 4]
        s_g = roll(t[:64], -32 * (g % 4))
        n_g = roll(t[64:], -32 * (g % 4))
        dense.append(n_g * m - s_g)
    inj[...] = jnp.dot(
        jnp.concatenate(dense, 0), spread_to,
        precision=lax.Precision.HIGHEST, preferred_element_type=f32,
    )

    def j(n, g, lo, hi):
        return inj[64 * g + lo : 64 * g + hi, 128 * n : 128 * (n + 1)]

    d = lane % SLAB
    wz = [None] + [
        (jnp.where(d < SLAB - k, CK[k], 0.0), jnp.where(d >= k, CK[k], 0.0))
        for k in range(1, W + 1)
    ]
    coef = {1: c1l, 2: cext, 3: c1r}
    pad = jnp.zeros((16, 128), f32)
    for g in range(5):
        r3[g] = j(3, g, 0, 64)
        if g in coef:
            x[g] = coef[g][...] * r3[g]
    for g, far in ((0, c2l), (4, c2r)):
        x[g, 0:16] = pad
        x[g, 16:48] = far[...] * r3[g, 16:48]
        x[g, 48:64] = pad
    for g in (1, 2, 3):
        r2[g] = 2.0 * r3[g, 8:56] + lap_packed(x, g, 8, 56, wz) + j(2, g, 8, 56)
    x[0] = jnp.zeros((64, 128), f32)
    x[4] = jnp.zeros((64, 128), f32)
    for g in (1, 2, 3):
        x[g, 0:8] = pad[:8]
        x[g, 8:56] = coef[g][8:56] * r2[g]
        x[g, 56:64] = pad[:8]
    for g in (1, 2, 3):
        r1[g] = 2.0 * r2[g] - r3[g, 8:56] + lap_packed(x, g, 8, 56, wz) + j(1, g, 8, 56)
    for g in (1, 2, 3):
        x[g, 8:56] = coef[g][8:56] * r1[g]
    r0 = 2.0 * r1[2, 8:40] - r2[2, 8:40] + lap_packed(x, 2, 16, 48, wz) + j(0, 2, 16, 48)
    corr = r0 * lp0[...] + r1[2, 8:40] * lp1[...] + r2[2, 8:40] * lp2[...]
    corr = corr + r3[2, 16:48] * lp3[...]

    cells = NX * NY
    for i in range(NX):
        out[NY * i : NY * (i + 1)] = own[i] + other[i]
    grad = (2.0 * courant_sq) * vpk[...] * corr
    out[cells : cells + NY] = grad
    out[cells + NY : cells + 2 * NY] = grad * zpk[...]


def sum_kernel(every, logs, grad_mean, grad_logs):
    lane = lanes()
    cells = NX * NY

    def packed(at):
        rows = slice(at, at + NY)
        return (every[0, rows] + every[1, rows]) + (every[2, rows] + every[3, rows])

    grad_in, weighted_in = packed(cells), packed(cells + NY)
    for i in range(NX):
        rows = slice(NY * i, NY * (i + 1))
        grad = every[0, rows] + every[2, rows]
        grad_mean[i] = grad + jnp.where(lane < SLAB, roll(grad_in, -SLAB * i), 0.0)
        weighted = every[1, rows] + every[3, rows]
        weighted = weighted + jnp.where(lane < SLAB, roll(weighted_in, -SLAB * i), 0.0)
        spread = jnp.exp(logs[i])
        grad_logs[i] = spread * weighted + jnp.exp(2.0 * logs[i]) / prior_var - 1.0


def call(kernel, outs, scratch=(), smem=0, mib=4):
    def go(*args):
        return pl.pallas_call(
            kernel,
            out_shape=outs,
            in_specs=[SM] * smem + [VM] * (len(args) - smem),
            out_specs=jax.tree.map(lambda _: VM, outs),
            scratch_shapes=list(scratch),
            compiler_params=pltpu.CompilerParams(vmem_limit_bytes=mib * 2**20),
        )(*args)

    return go


def shift(x, axis, k, wrap=False):
    n = lax.axis_size(axis)
    return lax.ppermute(x, axis, [(i, (i + k) % n) for i in range(n) if wrap or 0 <= i + k < n])


def local(
    mean_velocity,
    log_scale,
    shot_noise,
    checkpoint_prev,
    checkpoint_now,
    adjoint_next,
    adjoint_now,
    wavelet,
    source_column,
    receiver_column,
    observed,
    start_step,
):
    ngx, ngy, nshot = lax.axis_size("gx"), lax.axis_size("gy"), lax.axis_size("shot")
    noise = shot_noise[0]
    p_prev, p = checkpoint_prev[0], checkpoint_now[0]
    q_later, q = adjoint_next[0], adjoint_now[0]
    F = sds(NX, NY, NZ)
    coef, vel, xlo, xhi, ylo, yhi, _, oc = call(
        first_kernel,
        (
            F, F, sds(256, 128), sds(256, 128), sds(88, 128), sds(88, 128), sds(NY, NZ),
            sds(16, 128),
        ),
    )(mean_velocity, log_scale, noise, p, q, observed[0])
    buf = pltpu.VMEM((NX + 2 * W, 48, NZ), f32)
    slabs, keep = [], {}
    for n in range(STEPS):
        ml, mr = shift(xhi, "gx", 1), shift(xlo, "gx", -1)
        md, mu = shift(yhi, "gy", 1, True), shift(ylo, "gy", -1, True)
        extra = ()
        if n == 1:
            extra = (keep["cext"],)
        if n == 2:
            extra = (keep["lap1"],)
        if n == 3:
            extra = (keep["lap0"], keep["q3"], keep["img"], vel, noise)
        outs = [sds(NY, NZ), sds(16, 128), F, F]
        if n < 3:
            rows = (320, 288, 256)[n]
            outs += [sds(rows, 128), sds(rows, 128), sds(72, 128), sds(72, 128)]
        outs += {0: [F, sds(64, 128)], 1: [F], 2: [F], 3: [sds(NY, NZ), sds(16, NZ), sds(16, NZ), F, F]}[n]
        res = call(functools.partial(step_kernel, n), tuple(outs), (buf, buf), smem=3)(
            source_column, start_step, wavelet, coef, p, p_prev, q, q_later, ml, mr, md, mu, oc, *extra
        )
        lpk, oc, q_next, p_next = res[:4]
        slabs.append(lpk)
        if n < 3:
            xlo, xhi, ylo, yhi = res[4:8]
        if n == 0:
            keep["lap0"], keep["cext"], keep["q3"], keep["p1"] = res[8], res[9], q_next, p_next
        if n == 1:
            keep["lap1"] = res[8]
            keep["c"] = [ml, mr]
        if n == 2:
            keep["img"] = res[8]
            keep["c"] += [ml, mr]
        if n == 3:
            mat, mat_lo, mat_hi, own, sent = res[4:9]
        p_prev, p = p, p_next
        q_later, q = q, q_next

    mat_d, mat_u = shift(mat_hi, "gy", 1), shift(mat_lo, "gy", -1)
    other = lax.ppermute(sent, "shot", [(i, i ^ 1) for i in range(nshot)])
    nrec = receiver_column.shape[1]
    bf = jnp.bfloat16
    keyx, hoty, count, vpk, zpk = call(
        table_kernel,
        (
            jax.ShapeDtypeStruct((nrec // 128, 128), jnp.int32),
            jax.ShapeDtypeStruct((64, nrec), bf),
            sds(160, 64),
            sds(NY, NZ),
            sds(NY, NZ),
        ),
        [pltpu.VMEM((160, nrec), bf)],
        mib=16,
    )(receiver_column.reshape(-1, 128), vel, noise)
    chunk = call(chunk_kernel, sds(ngx, 32, 128))(mat, mat_d, mat_u, keep["p1"], oc)
    got = lax.all_to_all(chunk, "gx", 0, 0)
    g5 = pltpu.VMEM((5, 64, 128), f32)
    g48 = pltpu.VMEM((5, 48, 128), f32)
    part = call(
        last_kernel,
        sds(NX * NY + 2 * NY, NZ),
        (pltpu.VMEM((480, nrec), bf), g5, g5, g48, g48, pltpu.VMEM((320, 512), f32)),
        mib=24,
    )(got, keyx, hoty, count, keep["cext"], *keep["c"], *slabs, vpk, zpk, own, other)
    every = lax.all_gather(part, "shot", axis=0)
    return call(sum_kernel, (F, F))(every, log_scale)


def solution(mesh):
    return jax.shard_map(
        local,
        mesh=mesh,
        in_specs=(
            P("gx", "gy", None),
            P("gx", "gy", None),
            P("shot", "gx", "gy", None),
            P("shot", "gx", "gy", None),
            P("shot", "gx", "gy", None),
            P("shot", "gx", "gy", None),
            P("shot", "gx", "gy", None),
            P("shot", None),
            P("shot"),
            P("shot", None),
            P("shot", None, ("gx", "gy")),
            P(),
        ),
        out_specs=(P("gx", "gy", None), P("gx", "gy", None)),
        check_vma=False,
    )
```

```python
import functools

import jax
import jax.numpy as jnp
from jax import lax
from jax.experimental import pallas as pl
from jax.experimental.pallas import tpu as pltpu
from jax.sharding import PartitionSpec as P

STEPS = 4
SRC_DEPTH = 6
REC_DEPTH = 3
NX, NY, NZ = 8, 32, 128
W = 4
SLAB = 16

C0, C1, C2, C3, C4 = (-205.0 / 72.0, 8.0 / 5.0, -1.0 / 5.0, 8.0 / 315.0, -1.0 / 560.0)
CK = (C0, C1, C2, C3, C4)
courant_sq = 0.0625
prior_var = 0.01

f32 = jnp.float32
VM = pl.BlockSpec(memory_space=pltpu.VMEM)
SM = pl.BlockSpec(memory_space=pltpu.SMEM)


def sds(*shape):
    return jax.ShapeDtypeStruct(shape, f32)


def lanes(rows=1):
    return lax.broadcasted_iota(jnp.int32, (rows, 128), 1)


def roll(x, k):
    k = k % 128
    return x if k == 0 else pltpu.roll(x, k, 1)


def pack(rows):
    part = lanes() // SLAB
    out = jnp.where(part == 0, rows[0], 0.0)
    for x in range(1, NX):
        out = jnp.where(part == x, roll(rows[x], SLAB * x), out)
    return out


def put_rows(i, p, s, xlo, xhi):
    out, j = (xlo, i) if i < W else (xhi, i - W)
    out[NY * j : NY * (j + 1)] = p
    out[NY * (W + j) : NY * (W + j + 1)] = s


def put_pair(i, section, a, b, ylo, yhi, far=0):
    at = 64 * section + 8 * i
    lo, hi = slice(far, far + W), slice(NY - W - far, NY - far)
    if a is not None:
        ylo[at : at + 4] = a[lo]
        yhi[at : at + 4] = a[hi]
    ylo[at + 4 : at + 8] = b[lo]
    yhi[at + 4 : at + 8] = b[hi]


def put_columns(i, p, s, ylo, yhi):
    put_pair(i, 0, p, s, ylo, yhi)
    put_pair(i, 1, p, s, ylo, yhi, W)


def first_kernel(mean, logs, noise, p, q, pp, ql, obs, c_out, v_out, xlo, xhi, ylo, yhi, oc, ob):
    oc[...] = jnp.zeros((16, 128), f32)
    oc[0:4, 0:64] = obs[...]
    ob[...] = jnp.zeros((8, 128), f32)
    ob[0:4, 0:64] = obs[...]
    rows = []
    for i in range(NX):
        vel = mean[i] + jnp.exp(logs[i]) * noise[i]
        c = courant_sq * vel * vel
        s = c * q[i]
        v_out[i] = vel
        c_out[i] = c
        put_rows(i, p[i], s, xlo, xhi)
        put_columns(i, p[i], s, ylo, yhi)
        put_pair(i, 2, pp[i], q[i], ylo, yhi)
        put_pair(i, 3, ql[i], c, ylo, yhi)
        rows.append(c)
    slab = pack(rows)
    ylo[256:272] = slab[:16]
    yhi[256:272] = slab[16:]
    for y in (ylo, yhi):
        y[272:280] = ob[...]


def join_kernel(xlo, xhi, md, mu, lo, hi):
    n = xlo.shape[0]
    lo[:n] = xlo[...]
    lo[n : n + 32] = md[:32]
    lo[n + 32 :] = mu[:32]
    hi[:n] = xhi[...]
    hi[n : n + 32] = md[32:64]
    hi[n + 32 :] = mu[32:64]


def edges():
    iy = lax.axis_index("gy")
    return iy > 0, iy < lax.axis_size("gy") - 1


def depth_weights():
    lane = lanes()
    return [None] + [
        (jnp.where(lane < NZ - k, CK[k], 0.0), jnp.where(lane >= k, CK[k], 0.0))
        for k in range(1, W + 1)
    ]


def laplace(buf, i, lo, hi, wz):
    here = buf[W + i, lo:hi]
    out = (3.0 * C0) * here
    for k in range(1, W + 1):
        beside = buf[W + i + k, lo:hi] + buf[W + i - k, lo:hi]
        beside = beside + buf[W + i, lo + k : hi + k] + buf[W + i, lo - k : hi - k]
        out = out + CK[k] * beside
        out = out + wz[k][0] * roll(here, -k) + wz[k][1] * roll(here, k)
    return out


def add_source(n, source, start, wavelet, field, margin, reach):
    ix, iy, width = lax.axis_index("gx"), lax.axis_index("gy"), NY * lax.axis_size("gy")
    sx = source[0] // width - ix * NX
    sy = source[0] % width - iy * NY

    @pl.when((sx >= 0) & (sx < NX) & (sy >= -reach) & (sy < NY + reach))
    def _():
        at = pl.ds(sy + margin, 1)
        row = field[sx, at, :]
        field[sx, at, :] = row + jnp.where(lanes() == SRC_DEPTH, wavelet[0, start[0] + n], 0.0)


def even_kernel(n, source, start, wavelet, c, p, pp, q, ql, ml, mr, md, mu, oc, *rest):
    if n == 0:
        lpk, oc_out, fwd, pe, qe, xlo, xhi, lap_out, ce, cext, bufp, bufs, qn, ppe, qle = rest
    else:
        lap1, lpk, oc_out, fwd, pe, qe, xlo, xhi, img, bufp, bufs, qn = rest
    keep_d, keep_u = edges()
    lane = lanes()
    wz = depth_weights()

    def part(m, keep, at):
        return jnp.where(keep, m[at : at + 4], 0.0)

    def extend(ext, field, section, half):
        for i in range(NX):
            at = 64 * section + 8 * i + half
            ext[i, 8:40] = field[i]
            ext[i, 4:8] = part(md, keep_d, at)
            ext[i, 40:44] = part(mu, keep_u, at)

    extend(qn, q, 2, 4)
    if n == 0:
        extend(ppe, pp, 2, 0)
        extend(qle, ql, 3, 0)
        extend(ce, c, 3, 4)
    else:
        ce, ppe, qle = c, pp, ql
    corner = 256 if n == 0 else 288
    for buf, half in ((bufp, 0), (bufs, 4)):
        for i in range(NX):
            row = p[i] if half == 0 else ce[i, 8:40] * q[i]
            buf[W + i, 16:48] = row
            near, far = 8 * i + half, 64 + 8 * i + half
            buf[W + i, 8:12] = part(md, keep_d, far)
            buf[W + i, 12:16] = part(md, keep_d, near)
            buf[W + i, 48:52] = part(mu, keep_u, near)
            buf[W + i, 52:56] = part(mu, keep_u, far)
        for j in range(W):
            at = 32 * half + NY * j
            for m, row in ((ml, j), (mr, W + NX + j)):
                buf[row, 16:48] = m[at : at + NY]
                buf[row, 12:16] = part(m, keep_d, corner + 8 * j + half)
                buf[row, 48:52] = part(m, keep_u, corner + 32 + 8 * j + half)
    slab = jnp.zeros((NY, NZ), f32)
    for i in range(NX):
        lap_e = laplace(bufp, i, 8, 56, wz)
        lap = lap_e[8:40]
        slab = jnp.where(lane // SLAB == i, roll(lap, SLAB * i), slab)
        pe[i] = 2.0 * bufp[W + i, 8:56] - ppe[i] + ce[i] * lap_e
        q_new = 2.0 * qn[i] - qle[i] + laplace(bufs, i, 8, 56, wz)
        qe[i] = q_new
        if n == 0:
            lap_out[i] = lap
        else:
            img[i] = lap * q[i] + q_new[8:40] * lap1[i]
    lpk[...] = slab
    add_source(n, source, start, wavelet, pe, 8, W)

    at = 272 if n == 0 else 192
    got_d, got_u = md[at : at + 8], mu[at : at + 8]
    fwd[0:8] = got_d
    fwd[8:16] = got_u
    oc_out[...] = oc[...]
    up, turn = (0, 64) if n == 0 else (4, 0)
    oc_out[up : up + 4] = oc_out[up : up + 4] + roll(got_u, turn)[:4]
    oc_out[12:16] = oc_out[12:16] + roll(got_d, turn)[:4]

    for i in range(NX):
        put_rows(i, pe[i, 8:40], ce[i, 8:40] * qe[i, 8:40], xlo, xhi)
    if n == 0:
        cext[0:16] = jnp.where(keep_d, md[256:272], 0.0)
        cext[16:48] = pack([c[i] for i in range(NX)])
        cext[48:64] = jnp.where(keep_u, mu[256:272], 0.0)
        xlo[256:320] = cext[...]
        xhi[256:320] = cext[...]


def odd_kernel(n, source, start, wavelet, ce, pe, pp, qe, ql, ml, mr, fwd, *rest):
    if n == 1:
        lpk, qn, pn, xlo, xhi, ylo, yhi, lap_out, bufp, bufs = rest
    else:
        (lap0, q3, img, vel, noise, lpk, mat, mat_lo, mat_hi, own, sent, bufp, bufs, pn) = rest
    lane = lanes()
    wz = depth_weights()
    for i in range(NX):
        bufp[W + i, 12:52] = pe[i, 4:44]
        bufs[W + i, 12:52] = ce[i, 4:44] * qe[i, 4:44]
    for j in range(W):
        for m, row in ((ml, j), (mr, W + NX + j)):
            bufp[row, 16:48] = m[NY * j : NY * (j + 1)]
            bufs[row, 16:48] = m[128 + NY * j : 128 + NY * (j + 1)]
    slab = jnp.zeros((NY, NZ), f32)
    for i in range(NX):
        lap = laplace(bufp, i, 16, 48, wz)
        slab = jnp.where(lane // SLAB == i, roll(lap, SLAB * i), slab)
        pn[i] = 2.0 * pe[i, 8:40] - pp[i] + ce[i, 8:40] * lap
        q_new = 2.0 * qe[i, 8:40] - ql[i] + laplace(bufs, i, 16, 48, wz)
        if n == 1:
            qn[i] = q_new
            lap_out[i] = lap
        else:
            image = img[i] + lap * q3[i, 8:40] + q_new * lap0[i]
            grad = (2.0 * courant_sq) * vel[i] * image
            weighted = grad * noise[i]
            first = lax.axis_index("shot") % 2 == 0
            own[i] = jnp.where(first, grad, weighted)
            sent[i] = jnp.where(first, weighted, grad)
    lpk[...] = slab
    add_source(n, source, start, wavelet, pn, 0, 0)
    if n == 1:
        for i in range(NX):
            s = ce[i, 8:40] * qn[i]
            put_rows(i, pn[i], s, xlo, xhi)
            put_columns(i, pn[i], s, ylo, yhi)
            put_pair(i, 2, None, qn[i], ylo, yhi)
        xlo[256:288] = mr[272:304]
        xhi[256:288] = ml[272:304]
        ylo[192:200] = fwd[8:16]
        yhi[192:200] = fwd[0:8]
    else:
        out = jnp.zeros((NY, NZ), f32)
        for i in range(NX):
            for t, row in ((2, pp[i]), (3, pe[i, 8:40]), (4, pn[i])):
                to = 4 * i + t - 1
                out = jnp.where(lane == to, roll(row, to - REC_DEPTH), out)
        mat[...] = out
        mat_lo[0:16] = out[:16]
        mat_hi[0:16] = out[16:]
        mat_lo[16:24] = fwd[8:16]
        mat_hi[16:24] = fwd[0:8]


def chunk_kernel(mat, got_d, got_u, far, p1, oc, out):
    m = mat[...]
    lane = lanes()
    for i in range(NX):
        m = jnp.where(lane == 4 * i, roll(p1[i, 8:40], 4 * i - REC_DEPTH), m)
    packed = got_d[:16] + roll(m[:16], 32) + roll(m[16:], 64) + roll(got_u[:16], 96)
    third_u, third_d = roll(got_u[16:24], 64)[:4], roll(got_d[16:24], 64)[:4]
    for g in range(out.shape[0]):
        out[g, 0:4] = oc[0:4]
        out[g, 4:8] = oc[4:8] + third_u
        out[g, 8:12] = oc[8:12] + third_d + far[:4]
        out[g, 12:16] = oc[12:16]
        out[g, 16:32] = packed


def lap_packed(buf, g, lo, hi, wz):
    lane = lanes()
    here = buf[g, lo:hi]
    before, after = buf[g - 1, lo:hi], buf[g + 1, lo:hi]
    out = (3.0 * C0) * here
    for k in range(1, W + 1):
        t = SLAB * k
        beside = jnp.where(lane < 128 - t, roll(here, -t), roll(after, -t))
        beside = beside + jnp.where(lane >= t, roll(here, t), roll(before, t))
        beside = beside + buf[g, lo + k : hi + k] + buf[g, lo - k : hi - k]
        out = out + CK[k] * beside
        out = out + wz[k][0] * roll(here, -k) + wz[k][1] * roll(here, k)
    return out


def table_kernel(rec, vel, noise, keyx, hoty, count, vpk, zpk, hot):
    ix, iy, ngy = lax.axis_index("gx"), lax.axis_index("gy"), lax.axis_size("gy")
    half = ngy // 2
    odd = iy % 2 == 1
    bits = (NY * ngy).bit_length() - 1
    assert 2**bits == NY * ngy
    lane = lanes()
    bf = jnp.bfloat16
    row4 = lax.broadcasted_iota(jnp.int32, (160, 128), 0) // 4
    coly = lax.broadcasted_iota(jnp.int32, (64, 128), 0)

    def build(g, carry):
        at = pl.ds(pl.multiple_of(g * 128, 128), 128)
        first = (iy + 2 * (g % half)) % ngy
        second = (first + 1) % ngy
        row_a = rec[pl.ds((g // half) * half + first // 2, 1), :]
        row_b = rec[pl.ds((g // half) * half + second // 2, 1), :]
        row = jnp.where(odd, jnp.where(lane < 64, roll(row_a, 64), roll(row_b, 64)), row_a)
        kx = (row >> bits) - ix * NX + 16
        ky = (row & (NY * ngy - 1)) - iy * NY + 16
        keyx[pl.ds(g, 1), :] = kx
        hot[:, at] = jnp.where(row4 == kx, 1.0, 0.0).astype(bf)
        hoty[:, at] = jnp.where(coly == ky, 1.0, 0.0).astype(bf)
        return carry

    lax.fori_loop(0, rec.shape[0], build, 0)
    count[...] = lax.dot_general(
        hot[...], hoty[...], (((1,), (1,)), ((), ())), preferred_element_type=f32
    )
    vpk[...] = pack([vel[i] for i in range(NX)])
    zpk[...] = pack([noise[i] for i in range(NX)])


def last_kernel(
    got, keyx, hoty, cnt, cext, ml1, mr1, ml2, mr2, lp0, lp1, lp2, lp3, vpk, zpk, own, other,
    out, table, x, r3, r2, r1, inj,
):
    ngx = got.shape[0]
    lane = lanes()
    ix = lax.axis_index("gx")
    c1l, c1r = ml1.at[256:320], mr1.at[256:320]
    c2l, c2r = ml2.at[256:288], mr2.at[256:288]
    bf = jnp.bfloat16
    row4 = (lax.broadcasted_iota(jnp.int32, (160, 128), 0) // 4).astype(f32).astype(bf)
    none = jnp.zeros((), bf)

    def build(g, carry):
        for rp in range(4):
            at = pl.ds(pl.multiple_of((4 * g + rp) * 128, 128), 128)
            val = got[g, 4 * rp : 4 * rp + 4, :]
            hi = val.astype(bf).astype(f32)
            mid = (val - hi).astype(bf).astype(f32)
            low = val - hi - mid
            kx = jnp.clip(keyx[pl.ds(4 * g + rp, 1), :], -1, 40).astype(f32).astype(bf)
            here = row4 == kx
            for part, v in enumerate((hi, mid, low)):
                v16 = jnp.concatenate([v, v, v, v], 0).astype(bf)
                v160 = jnp.concatenate([v16] * 10, 0)
                table[160 * part : 160 * (part + 1), at] = jnp.where(here, v160, none)
        return carry

    lax.fori_loop(0, ngx, build, 0)
    sums = lax.dot_general(
        table[...], hoty[...], (((1,), (1,)), ((), ())), preferred_element_type=f32
    )
    seen = sums[0:160] + sums[160:320] + sums[320:480]
    zero = jnp.zeros((96, 64), f32)
    seen = jnp.concatenate([seen, zero], 0)
    count = jnp.concatenate([cnt[...], zero], 0)
    both = jnp.concatenate([seen, count], 1)
    tr = [both[:128].T, both[128:].T]

    k_in = lax.broadcasted_iota(jnp.int32, (128, 512), 0)
    k_out = lax.broadcasted_iota(jnp.int32, (128, 512), 1)
    spread_to = jnp.where(
        (k_in < 32) & (k_out == (k_in % 4) * 128 + (k_in // 4) * SLAB + REC_DEPTH), 1.0, 0.0
    )
    dense = []
    for g in range(5):
        src = ix + (g - 2)
        ok = (src >= 0) & (src < ngx)
        blk = got[jnp.clip(src, 0, ngx - 1), 16:32, :]
        m = jnp.concatenate([roll(blk, -32 * t) for t in range(4)], 0)
        m = jnp.where(ok, m, 0.0)
        t = tr[g // 4]
        s_g = roll(t[:64], -32 * (g % 4))
        n_g = roll(t[64:], -32 * (g % 4))
        dense.append(n_g * m - s_g)
    inj[...] = jnp.dot(
        jnp.concatenate(dense, 0), spread_to,
        precision=lax.Precision.HIGHEST, preferred_element_type=f32,
    )

    def j(n, g, lo, hi):
        return inj[64 * g + lo : 64 * g + hi, 128 * n : 128 * (n + 1)]

    d = lane % SLAB
    wz = [None] + [
        (jnp.where(d < SLAB - k, CK[k], 0.0), jnp.where(d >= k, CK[k], 0.0))
        for k in range(1, W + 1)
    ]
    coef = {1: c1l, 2: cext, 3: c1r}
    pad = jnp.zeros((16, 128), f32)
    for g in range(5):
        r3[g] = j(3, g, 0, 64)
        if g in coef:
            x[g] = coef[g][...] * r3[g]
    for g, far in ((0, c2l), (4, c2r)):
        x[g, 0:16] = pad
        x[g, 16:48] = far[...] * r3[g, 16:48]
        x[g, 48:64] = pad
    for g in (1, 2, 3):
        r2[g] = 2.0 * r3[g, 8:56] + lap_packed(x, g, 8, 56, wz) + j(2, g, 8, 56)
    x[0] = jnp.zeros((64, 128), f32)
    x[4] = jnp.zeros((64, 128), f32)
    for g in (1, 2, 3):
        x[g, 0:8] = pad[:8]
        x[g, 8:56] = coef[g][8:56] * r2[g]
        x[g, 56:64] = pad[:8]
    for g in (1, 2, 3):
        r1[g] = 2.0 * r2[g] - r3[g, 8:56] + lap_packed(x, g, 8, 56, wz) + j(1, g, 8, 56)
    for g in (1, 2, 3):
        x[g, 8:56] = coef[g][8:56] * r1[g]
    r0 = 2.0 * r1[2, 8:40] - r2[2, 8:40] + lap_packed(x, 2, 16, 48, wz) + j(0, 2, 16, 48)
    corr = r0 * lp0[...] + r1[2, 8:40] * lp1[...] + r2[2, 8:40] * lp2[...]
    corr = corr + r3[2, 16:48] * lp3[...]

    cells = NX * NY
    for i in range(NX):
        out[NY * i : NY * (i + 1)] = own[i] + other[i]
    grad = (2.0 * courant_sq) * vpk[...] * corr
    out[cells : cells + NY] = grad
    out[cells + NY : cells + 2 * NY] = grad * zpk[...]


def sum_kernel(every, logs, grad_mean, grad_logs):
    lane = lanes()
    cells = NX * NY

    def packed(at):
        rows = slice(at, at + NY)
        return (every[0, rows] + every[1, rows]) + (every[2, rows] + every[3, rows])

    grad_in, weighted_in = packed(cells), packed(cells + NY)
    for i in range(NX):
        rows = slice(NY * i, NY * (i + 1))
        grad = every[0, rows] + every[2, rows]
        grad_mean[i] = grad + jnp.where(lane < SLAB, roll(grad_in, -SLAB * i), 0.0)
        weighted = every[1, rows] + every[3, rows]
        weighted = weighted + jnp.where(lane < SLAB, roll(weighted_in, -SLAB * i), 0.0)
        spread = jnp.exp(logs[i])
        grad_logs[i] = spread * weighted + jnp.exp(2.0 * logs[i]) / prior_var - 1.0


def call(kernel, outs, scratch=(), smem=0, mib=4):
    def go(*args):
        return pl.pallas_call(
            kernel,
            out_shape=outs,
            in_specs=[SM] * smem + [VM] * (len(args) - smem),
            out_specs=jax.tree.map(lambda _: VM, outs),
            scratch_shapes=list(scratch),
            compiler_params=pltpu.CompilerParams(vmem_limit_bytes=mib * 2**20),
        )(*args)

    return go


def shift(x, axis, k, wrap=False):
    n = lax.axis_size(axis)
    return lax.ppermute(x, axis, [(i, (i + k) % n) for i in range(n) if wrap or 0 <= i + k < n])


def local(
    mean_velocity,
    log_scale,
    shot_noise,
    checkpoint_prev,
    checkpoint_now,
    adjoint_next,
    adjoint_now,
    wavelet,
    source_column,
    receiver_column,
    observed,
    start_step,
):
    ngx, ngy, nshot = lax.axis_size("gx"), lax.axis_size("gy"), lax.axis_size("shot")
    noise = shot_noise[0]
    p_prev, p = checkpoint_prev[0], checkpoint_now[0]
    q_later, q = adjoint_next[0], adjoint_now[0]
    F = sds(NX, NY, NZ)
    E = sds(NX, NY + 16, NZ)
    coef, vel, xlo, xhi, ylo, yhi, oc, ob = call(
        first_kernel,
        (
            F, F, sds(256, 128), sds(256, 128), sds(280, 128), sds(280, 128), sds(16, 128),
            sds(8, 128),
        ),
    )(mean_velocity, log_scale, noise, p, q, p_prev, q_later, observed[0])
    buf = pltpu.VMEM((NX + 2 * W, 64, NZ), f32)
    ext = pltpu.VMEM((NX, NY + 16, NZ), f32)
    own_block = pltpu.VMEM((NX, NY, NZ), f32)
    scalars = (source_column, start_step, wavelet)

    def to_y(lo, hi):
        return shift(hi, "gy", 1, True), shift(lo, "gy", -1, True)

    def to_x(lo, hi):
        return shift(hi, "gx", 1), shift(lo, "gx", -1)

    def join(xlo, xhi, md, mu):
        out = sds(xlo.shape[0] + 64, 128)
        return call(join_kernel, (out, out))(xlo, xhi, md, mu)

    step = lambda kernel, n, outs, scratch: call(
        functools.partial(kernel, n), tuple(outs), scratch, smem=3
    )
    head = [sds(NY, NZ), sds(16, 128), sds(16, 128), E, E]

    md, mu = to_y(ylo, yhi)
    far = shift(ob, "gy", ngy // 2, True)
    ml, mr = to_x(*join(xlo, xhi, md, mu))
    lp0, oc, fwd, p1, q3, xlo, xhi, lap0, cext_f, cext = step(
        even_kernel, 0, head + [sds(320, 128), sds(320, 128), F, E, sds(64, 128)],
        (buf, buf, ext, ext, ext),
    )(*scalars, coef, p, p_prev, q, q_later, ml, mr, md, mu, oc)

    ml1, mr1 = to_x(xlo, xhi)
    lp1, q2, p2, xlo, xhi, ylo, yhi, lap1 = step(
        odd_kernel, 1,
        [sds(NY, NZ), F, F, sds(288, 128), sds(288, 128), sds(200, 128), sds(200, 128), F],
        (buf, buf),
    )(*scalars, cext_f, p1, p, q3, q, ml1, mr1, fwd)

    md, mu = to_y(ylo, yhi)
    ml2, mr2 = to_x(*join(xlo, xhi, md, mu))
    lp2, oc, fwd, p3, q1, xlo, xhi, img = step(
        even_kernel, 2, head + [sds(256, 128), sds(256, 128), F], (buf, buf, ext)
    )(*scalars, cext_f, p2, p1, q2, q3, ml2, mr2, md, mu, oc, lap1)

    ml, mr = to_x(xlo, xhi)
    lp3, mat, mat_lo, mat_hi, own, sent = step(
        odd_kernel, 3, [sds(NY, NZ), sds(NY, NZ), sds(24, NZ), sds(24, NZ), F, F],
        (buf, buf, own_block),
    )(*scalars, cext_f, p3, p2, q1, q2, ml, mr, fwd, lap0, q3, img, vel, noise)

    mat_d, mat_u = shift(mat_hi, "gy", 1, True), shift(mat_lo, "gy", -1, True)
    other = lax.ppermute(sent, "shot", [(i, i ^ 1) for i in range(nshot)])
    nrec = receiver_column.shape[1]
    bf = jnp.bfloat16
    keyx, hoty, count, vpk, zpk = call(
        table_kernel,
        (
            jax.ShapeDtypeStruct((nrec // 128, 128), jnp.int32),
            jax.ShapeDtypeStruct((64, nrec), bf),
            sds(160, 64),
            sds(NY, NZ),
            sds(NY, NZ),
        ),
        [pltpu.VMEM((160, nrec), bf)],
        mib=16,
    )(receiver_column.reshape(-1, 128), vel, noise)
    chunk = call(chunk_kernel, sds(ngx, 32, 128))(mat, mat_d, mat_u, far, p1, oc)
    got = lax.all_to_all(chunk, "gx", 0, 0)
    g5 = pltpu.VMEM((5, 64, 128), f32)
    g48 = pltpu.VMEM((5, 48, 128), f32)
    part = call(
        last_kernel,
        sds(NX * NY + 2 * NY, NZ),
        (pltpu.VMEM((480, nrec), bf), g5, g5, g48, g48, pltpu.VMEM((320, 512), f32)),
        mib=24,
    )(
        got, keyx, hoty, count, cext, ml1, mr1, ml2, mr2, lp0, lp1, lp2, lp3, vpk, zpk, own, other
    )
    every = lax.all_gather(part, "shot", axis=0)
    return call(sum_kernel, (F, F))(every, log_scale)


def solution(mesh):
    return jax.shard_map(
        local,
        mesh=mesh,
        in_specs=(
            P("gx", "gy", None),
            P("gx", "gy", None),
            P("shot", "gx", "gy", None),
            P("shot", "gx", "gy", None),
            P("shot", "gx", "gy", None),
            P("shot", "gx", "gy", None),
            P("shot", "gx", "gy", None),
            P("shot", None),
            P("shot"),
            P("shot", None),
            P("shot", None, ("gx", "gy")),
            P(),
        ),
        out_specs=(P("gx", "gy", None), P("gx", "gy", None)),
        check_vma=False,
    )
```

```python
import functools

import jax
import jax.numpy as jnp
from jax import lax
from jax.experimental import pallas as pl
from jax.experimental.pallas import tpu as pltpu
from jax.sharding import PartitionSpec as P

STEPS = 4
SRC_DEPTH = 6
REC_DEPTH = 3
NX, NY, NZ = 8, 32, 128
W = 4
SLAB = 16

C0, C1, C2, C3, C4 = (-205.0 / 72.0, 8.0 / 5.0, -1.0 / 5.0, 8.0 / 315.0, -1.0 / 560.0)
CK = (C0, C1, C2, C3, C4)
courant_sq = 0.0625
prior_var = 0.01

f32 = jnp.float32
VM = pl.BlockSpec(memory_space=pltpu.VMEM)
SM = pl.BlockSpec(memory_space=pltpu.SMEM)


def sds(*shape):
    return jax.ShapeDtypeStruct(shape, f32)


def lanes(rows=1):
    return lax.broadcasted_iota(jnp.int32, (rows, 128), 1)


def roll(x, k):
    k = k % 128
    return x if k == 0 else pltpu.roll(x, k, 1)


def pack(rows):
    part = lanes() // SLAB
    out = jnp.where(part == 0, rows[0], 0.0)
    for x in range(1, NX):
        out = jnp.where(part == x, roll(rows[x], SLAB * x), out)
    return out


def put_strips(i, p, s, xlo, xhi, ylo, yhi):
    out, j = (xlo, i) if i < W else (xhi, i - W)
    out[NY * j : NY * (j + 1)] = p
    out[NY * (W + j) : NY * (W + j + 1)] = s
    ylo[8 * i : 8 * i + 4] = p[:W]
    ylo[8 * i + 4 : 8 * i + 8] = s[:W]
    yhi[8 * i : 8 * i + 4] = p[NY - W :]
    yhi[8 * i + 4 : 8 * i + 8] = s[NY - W :]


def first_kernel(c, s, p, obs, xlo, xhi, ylo, yhi, oc):
    oc[...] = jnp.zeros((16, 128), f32)
    oc[0:4, 0:64] = obs[...]
    for y in (ylo, yhi):
        y[80:88] = jnp.zeros((8, 128), f32)
        y[80:84, 0:64] = obs[...]
    for i in range(NX):
        put_strips(i, p[i], s[i], xlo, xhi, ylo, yhi)
    slab = pack([c[i] for i in range(NX)])
    ylo[64:80] = slab[:16]
    yhi[64:80] = slab[16:]


def fill(buf, field, rows_l, rows_r, md, mu, at, keep_d, keep_u):
    for i in range(NX):
        buf[W + i, 8:40] = field[i]
        buf[W + i, 4:8] = jnp.where(keep_d, md[8 * i + at : 8 * i + at + 4], 0.0)
        buf[W + i, 40:44] = jnp.where(keep_u, mu[8 * i + at : 8 * i + at + 4], 0.0)
    for j in range(W):
        buf[j, 8:40] = rows_l[j]
        buf[W + NX + j, 8:40] = rows_r[j]


def laplace(buf, i, wz):
    here = buf[W + i, 8:40]
    out = (3.0 * C0) * here
    for k in range(1, W + 1):
        beside = buf[W + i + k, 8:40] + buf[W + i - k, 8:40]
        beside = beside + buf[W + i, 8 + k : 40 + k] + buf[W + i, 8 - k : 40 - k]
        out = out + CK[k] * beside
        out = out + wz[k][0] * roll(here, -k) + wz[k][1] * roll(here, k)
    return out


def step_kernel(n, source, start, wavelet, c, p, pp, q, ql, ml, mr, md, mu, oc, *rest):
    ix, iy, ngy = lax.axis_index("gx"), lax.axis_index("gy"), lax.axis_size("gy")
    rest = list(rest)
    bufp, bufs = rest[-2:]
    rest = rest[:-2]
    take = lambda: rest.pop(0)
    if n == 1:
        cext = take()
    if n == 2:
        lap_other = take()
    if n == 3:
        lap_other, q3, img, vel, noise = take(), take(), take(), take(), take()
    lpk, oc_out, qn = take(), take(), take()
    if n < 3:
        pn, xlo, xhi, ylo, yhi = take(), take(), take(), take(), take()
    else:
        pn = take()
    if n == 0:
        lap_out, cext = take(), take()
    if n == 1:
        lap_out = take()
    if n == 2:
        img_out = take()
    if n == 3:
        mat, mat_lo, mat_hi, own, sent = take(), take(), take(), take(), take()

    keep_d, keep_u = iy > 0, iy < ngy - 1
    lane = lanes()
    wz = [None] + [
        (jnp.where(lane < NZ - k, CK[k], 0.0), jnp.where(lane >= k, CK[k], 0.0))
        for k in range(1, W + 1)
    ]

    def strip(m, at):
        return [m[at + NY * j : at + NY * (j + 1)] for j in range(W)]

    fill(bufp, p, strip(ml, 0), strip(mr, 0), md, mu, 0, keep_d, keep_u)
    s = [c[i] * q[i] for i in range(NX)]
    fill(bufs, s, strip(ml, 128), strip(mr, 128), md, mu, 4, keep_d, keep_u)
    slab = jnp.zeros((NY, NZ), f32)
    for i in range(NX):
        lap = laplace(bufp, i, wz)
        slab = jnp.where(lane // SLAB == i, roll(lap, SLAB * i), slab)
        pn[i] = 2.0 * p[i] - pp[i] + c[i] * lap
        q_new = 2.0 * q[i] - ql[i] + laplace(bufs, i, wz)
        qn[i] = q_new
        if n < 2:
            lap_out[i] = lap
        if n == 2:
            img_out[i] = lap * q[i] + q_new * lap_other[i]
        if n == 3:
            image = img[i] + lap * q3[i] + q_new * lap_other[i]
            grad = (2.0 * courant_sq) * vel[i] * image
            weighted = grad * noise[i]
            first = lax.axis_index("shot") % 2 == 0
            own[i] = jnp.where(first, grad, weighted)
            sent[i] = jnp.where(first, weighted, grad)
    lpk[...] = slab

    sx = source[0] // (NY * ngy) - ix * NX
    sy = source[0] % (NY * ngy) - iy * NY

    @pl.when((sx >= 0) & (sx < NX) & (sy >= 0) & (sy < NY))
    def _():
        row = pn[sx, pl.ds(sy, 1), :]
        pn[sx, pl.ds(sy, 1), :] = row + jnp.where(lane == SRC_DEPTH, wavelet[0, start[0] + n], 0.0)

    at = 80 if n == 0 else 64
    got_d, got_u = md[at : at + 8], mu[at : at + 8]
    oc_out[...] = oc[...]
    up, turn_u, down, turn_d = ((0, 64, 12, 64), (4, 0, 12, 0), (4, 64, 8, 64), (8, 0, None, 0))[n]
    oc_out[up : up + 4] = oc_out[up : up + 4] + roll(got_u, turn_u)[:4]
    if down is not None:
        oc_out[down : down + 4] = oc_out[down : down + 4] + roll(got_d, turn_d)[:4]

    if n < 3:
        for i in range(NX):
            put_strips(i, pn[i], c[i] * qn[i], xlo, xhi, ylo, yhi)
        ylo[64:72] = got_u
        yhi[64:72] = got_d
    if n == 0:
        cext[0:16] = jnp.where(keep_d, md[64:80], 0.0)
        cext[16:48] = pack([c[i] for i in range(NX)])
        cext[48:64] = jnp.where(keep_u, mu[64:80], 0.0)
        xlo[256:320] = cext[...]
        xhi[256:320] = cext[...]
    if n == 1:
        xlo[256:288] = mr[272:304]
        xhi[256:288] = ml[272:304]
    if n == 3:
        out = jnp.zeros((NY, NZ), f32)
        for i in range(NX):
            for t, row in ((2, pp[i]), (3, p[i]), (4, pn[i])):
                to = 4 * i + t - 1
                out = jnp.where(lane == to, roll(row, to - REC_DEPTH), out)
        mat[...] = out
        mat_lo[...] = out[:16]
        mat_hi[...] = out[16:]


def chunk_kernel(mat, got_d, got_u, p1, oc, out):
    m = mat[...]
    lane = lanes()
    for i in range(NX):
        m = jnp.where(lane == 4 * i, roll(p1[i], 4 * i - REC_DEPTH), m)
    packed = got_d[...] + roll(m[:16], 32) + roll(m[16:], 64) + roll(got_u[...], 96)
    for g in range(out.shape[0]):
        out[g, 0:16] = oc[...]
        out[g, 16:32] = packed


def lap_packed(buf, g, lo, hi, wz):
    lane = lanes()
    here = buf[g, lo:hi]
    before, after = buf[g - 1, lo:hi], buf[g + 1, lo:hi]
    out = (3.0 * C0) * here
    for k in range(1, W + 1):
        t = SLAB * k
        beside = jnp.where(lane < 128 - t, roll(here, -t), roll(after, -t))
        beside = beside + jnp.where(lane >= t, roll(here, t), roll(before, t))
        beside = beside + buf[g, lo + k : hi + k] + buf[g, lo - k : hi - k]
        out = out + CK[k] * beside
        out = out + wz[k][0] * roll(here, -k) + wz[k][1] * roll(here, k)
    return out


def table_kernel(rec, vel, noise, keyx, hoty, vpk, zpk, cols, rows):
    ix, iy, ngy = lax.axis_index("gx"), lax.axis_index("gy"), lax.axis_size("gy")
    half = ngy // 2
    bits = (NY * ngy).bit_length() - 1
    assert 2**bits == NY * ngy
    odd = iy % 2 == 1
    low = lanes() < 64
    bf = jnp.bfloat16
    coly = lax.broadcasted_iota(jnp.int32, (64, 128), 0).astype(f32).astype(bf)
    one, none = jnp.ones((), bf), jnp.zeros((), bf)
    kx = jnp.clip((rec[...] >> bits) - ix * NX + 16, -1, 40).astype(f32)
    ky = jnp.clip((rec[...] & (NY * ngy - 1)) - iy * NY + 16, -1, 64).astype(f32)
    for ref, k in ((rows, kx), (cols, ky)):
        ref[0] = jnp.where(odd, roll(k, 64), k)
    for g in range(rec.shape[0]):
        first = (iy + 2 * (g % half)) % ngy
        a = pl.ds((g // half) * half + first // 2, 1)
        b = pl.ds((g // half) * half + ((first + 1) % ngy) // 2, 1)
        keyx[g : g + 1] = jnp.where(low, rows[0, a, :], rows[0, b, :])
        here = jnp.where(low, cols[0, a, :], cols[0, b, :]).astype(bf)
        hoty[:, 128 * g : 128 * (g + 1)] = jnp.where(coly == here, one, none)
    vpk[...] = pack([vel[i] for i in range(NX)])
    zpk[...] = pack([noise[i] for i in range(NX)])


def last_kernel(
    got, keyx, hoty, cext, ml1, mr1, ml2, mr2, lp0, lp1, lp2, lp3, vpk, zpk, own, other,
    out, table, x, r3, r2, r1, inj,
):
    ngx = got.shape[0]
    lane = lanes()
    ix = lax.axis_index("gx")
    c1l, c1r = ml1.at[256:320], mr1.at[256:320]
    c2l, c2r = ml2.at[256:288], mr2.at[256:288]
    bf = jnp.bfloat16
    row4 = (lax.broadcasted_iota(jnp.int32, (160, 128), 0) // 4).astype(f32).astype(bf)
    one, none = jnp.ones((), bf), jnp.zeros((), bf)

    def build(g, carry):
        for rp in range(4):
            at = pl.ds(pl.multiple_of((4 * g + rp) * 128, 128), 128)
            val = got[g, 4 * rp : 4 * rp + 4, :]
            hi = val.astype(bf).astype(f32)
            mid = (val - hi).astype(bf).astype(f32)
            low = val - hi - mid
            here = row4 == keyx[pl.ds(4 * g + rp, 1), :].astype(bf)
            for part, v in enumerate((hi, mid, low)):
                v16 = jnp.concatenate([v, v, v, v], 0).astype(bf)
                v160 = jnp.concatenate([v16] * 10, 0)
                table[160 * part : 160 * (part + 1), at] = jnp.where(here, v160, none)
            table[480:640, at] = jnp.where(here, one, none)
        return carry

    lax.fori_loop(0, ngx, build, 0, unroll=2)
    sums = lax.dot_general(
        table[...], hoty[...], (((1,), (1,)), ((), ())), preferred_element_type=f32
    )
    seen = sums[0:160] + sums[160:320] + sums[320:480]
    zero = jnp.zeros((96, 64), f32)
    seen = jnp.concatenate([seen, zero], 0)
    count = jnp.concatenate([sums[480:640], zero], 0)
    both = jnp.concatenate([seen, count], 1)
    tr = [both[:128].T, both[128:].T]

    k_in = lax.broadcasted_iota(jnp.int32, (128, 512), 0)
    k_out = lax.broadcasted_iota(jnp.int32, (128, 512), 1)
    spread_to = jnp.where(
        (k_in < 32) & (k_out == (k_in % 4) * 128 + (k_in // 4) * SLAB + REC_DEPTH), 1.0, 0.0
    )
    dense = []
    for g in range(5):
        src = ix + (g - 2)
        ok = (src >= 0) & (src < ngx)
        blk = got[jnp.clip(src, 0, ngx - 1), 16:32, :]
        m = jnp.concatenate([roll(blk, -32 * t) for t in range(4)], 0)
        m = jnp.where(ok, m, 0.0)
        t = tr[g // 4]
        s_g = roll(t[:64], -32 * (g % 4))
        n_g = roll(t[64:], -32 * (g % 4))
        dense.append(n_g * m - s_g)
    inj[...] = jnp.dot(
        jnp.concatenate(dense, 0), spread_to,
        precision=lax.Precision.HIGHEST, preferred_element_type=f32,
    )

    def j(n, g, lo, hi):
        return inj[64 * g + lo : 64 * g + hi, 128 * n : 128 * (n + 1)]

    d = lane % SLAB
    wz = [None] + [
        (jnp.where(d < SLAB - k, CK[k], 0.0), jnp.where(d >= k, CK[k], 0.0))
        for k in range(1, W + 1)
    ]
    coef = {1: c1l, 2: cext, 3: c1r}
    pad = jnp.zeros((16, 128), f32)
    for g in range(5):
        r3[g] = j(3, g, 0, 64)
        if g in coef:
            x[g] = coef[g][...] * r3[g]
    for g, far in ((0, c2l), (4, c2r)):
        x[g, 0:16] = pad
        x[g, 16:48] = far[...] * r3[g, 16:48]
        x[g, 48:64] = pad
    for g in (1, 2, 3):
        r2[g] = 2.0 * r3[g, 8:56] + lap_packed(x, g, 8, 56, wz) + j(2, g, 8, 56)
    x[0] = jnp.zeros((64, 128), f32)
    x[4] = jnp.zeros((64, 128), f32)
    for g in (1, 2, 3):
        x[g, 0:8] = pad[:8]
        x[g, 8:56] = coef[g][8:56] * r2[g]
        x[g, 56:64] = pad[:8]
    for g in (1, 2, 3):
        r1[g] = 2.0 * r2[g] - r3[g, 8:56] + lap_packed(x, g, 8, 56, wz) + j(1, g, 8, 56)
    for g in (1, 2, 3):
        x[g, 8:56] = coef[g][8:56] * r1[g]
    r0 = 2.0 * r1[2, 8:40] - r2[2, 8:40] + lap_packed(x, 2, 16, 48, wz) + j(0, 2, 16, 48)
    corr = r0 * lp0[...] + r1[2, 8:40] * lp1[...] + r2[2, 8:40] * lp2[...]
    corr = corr + r3[2, 16:48] * lp3[...]

    cells = NX * NY
    for i in range(NX):
        out[NY * i : NY * (i + 1)] = own[i] + other[i]
    grad = (2.0 * courant_sq) * vpk[...] * corr
    out[cells : cells + NY] = grad
    out[cells + NY : cells + 2 * NY] = grad * zpk[...]


def sum_kernel(every, logs, grad_mean, grad_logs):
    lane = lanes()
    cells = NX * NY

    def packed(at):
        rows = slice(at, at + NY)
        return (every[0, rows] + every[1, rows]) + (every[2, rows] + every[3, rows])

    grad_in, weighted_in = packed(cells), packed(cells + NY)
    for i in range(NX):
        rows = slice(NY * i, NY * (i + 1))
        grad = every[0, rows] + every[2, rows]
        grad_mean[i] = grad + jnp.where(lane < SLAB, roll(grad_in, -SLAB * i), 0.0)
        weighted = every[1, rows] + every[3, rows]
        weighted = weighted + jnp.where(lane < SLAB, roll(weighted_in, -SLAB * i), 0.0)
        spread = jnp.exp(logs[i])
        grad_logs[i] = spread * weighted + jnp.exp(2.0 * logs[i]) / prior_var - 1.0


def call(kernel, outs, scratch=(), smem=0, mib=4):
    def go(*args):
        return pl.pallas_call(
            kernel,
            out_shape=outs,
            in_specs=[SM] * smem + [VM] * (len(args) - smem),
            out_specs=jax.tree.map(lambda _: VM, outs),
            scratch_shapes=list(scratch),
            compiler_params=pltpu.CompilerParams(vmem_limit_bytes=mib * 2**20),
        )(*args)

    return go


def shift(x, axis, k, wrap=False):
    n = lax.axis_size(axis)
    return lax.ppermute(x, axis, [(i, (i + k) % n) for i in range(n) if wrap or 0 <= i + k < n])


def local(
    mean_velocity,
    log_scale,
    shot_noise,
    checkpoint_prev,
    checkpoint_now,
    adjoint_next,
    adjoint_now,
    wavelet,
    source_column,
    receiver_column,
    observed,
    start_step,
):
    ngx, ngy, nshot = lax.axis_size("gx"), lax.axis_size("gy"), lax.axis_size("shot")
    noise = shot_noise[0]
    p_prev, p = checkpoint_prev[0], checkpoint_now[0]
    q_later, q = adjoint_next[0], adjoint_now[0]
    F = sds(NX, NY, NZ)
    vel = mean_velocity + jnp.exp(log_scale) * noise
    coef = courant_sq * vel * vel
    xlo, xhi, ylo, yhi, oc = call(
        first_kernel,
        (sds(256, 128), sds(256, 128), sds(88, 128), sds(88, 128), sds(16, 128)),
    )(coef, coef * q, p, observed[0])
    buf = pltpu.VMEM((NX + 2 * W, 48, NZ), f32)
    slabs, keep = [], {}
    for n in range(STEPS):
        ml, mr = shift(xhi, "gx", 1), shift(xlo, "gx", -1)
        md, mu = shift(yhi, "gy", 1, True), shift(ylo, "gy", -1, True)
        extra = ()
        if n == 1:
            extra = (keep["cext"],)
        if n == 2:
            extra = (keep["lap1"],)
        if n == 3:
            extra = (keep["lap0"], keep["q3"], keep["img"], vel, noise)
        outs = [sds(NY, NZ), sds(16, 128), F, F]
        if n < 3:
            rows = (320, 288, 256)[n]
            outs += [sds(rows, 128), sds(rows, 128), sds(72, 128), sds(72, 128)]
        outs += {0: [F, sds(64, 128)], 1: [F], 2: [F], 3: [sds(NY, NZ), sds(16, NZ), sds(16, NZ), F, F]}[n]
        res = call(functools.partial(step_kernel, n), tuple(outs), (buf, buf), smem=3)(
            source_column, start_step, wavelet, coef, p, p_prev, q, q_later, ml, mr, md, mu, oc, *extra
        )
        lpk, oc, q_next, p_next = res[:4]
        slabs.append(lpk)
        if n < 3:
            xlo, xhi, ylo, yhi = res[4:8]
        if n == 0:
            keep["lap0"], keep["cext"], keep["q3"], keep["p1"] = res[8], res[9], q_next, p_next
        if n == 1:
            keep["lap1"] = res[8]
            keep["c"] = [ml, mr]
        if n == 2:
            keep["img"] = res[8]
            keep["c"] += [ml, mr]
        if n == 3:
            mat, mat_lo, mat_hi, own, sent = res[4:9]
        p_prev, p = p, p_next
        q_later, q = q, q_next

    mat_d, mat_u = shift(mat_hi, "gy", 1), shift(mat_lo, "gy", -1)
    other = lax.ppermute(sent, "shot", [(i, i ^ 1) for i in range(nshot)])
    nrec = receiver_column.shape[1]
    bf = jnp.bfloat16
    keyx, hoty, vpk, zpk = call(
        table_kernel,
        (
            sds(nrec // 128, 128),
            jax.ShapeDtypeStruct((64, nrec), bf),
            sds(NY, NZ),
            sds(NY, NZ),
        ),
        [pltpu.VMEM((1, nrec // 128, 128), f32)] * 2,
        mib=8,
    )(receiver_column.reshape(-1, 128), vel, noise)
    chunk = call(chunk_kernel, sds(ngx, 32, 128))(mat, mat_d, mat_u, keep["p1"], oc)
    got = lax.all_to_all(chunk, "gx", 0, 0)
    g5 = pltpu.VMEM((5, 64, 128), f32)
    g48 = pltpu.VMEM((5, 48, 128), f32)
    part = call(
        last_kernel,
        sds(NX * NY + 2 * NY, NZ),
        (pltpu.VMEM((640, nrec), bf), g5, g5, g48, g48, pltpu.VMEM((320, 512), f32)),
        mib=24,
    )(got, keyx, hoty, keep["cext"], *keep["c"], *slabs, vpk, zpk, own, other)
    every = lax.all_gather(part, "shot", axis=0)
    return call(sum_kernel, (F, F))(every, log_scale)


def solution(mesh):
    return jax.shard_map(
        local,
        mesh=mesh,
        in_specs=(
            P("gx", "gy", None),
            P("gx", "gy", None),
            P("shot", "gx", "gy", None),
            P("shot", "gx", "gy", None),
            P("shot", "gx", "gy", None),
            P("shot", "gx", "gy", None),
            P("shot", "gx", "gy", None),
            P("shot", None),
            P("shot"),
            P("shot", None),
            P("shot", None, ("gx", "gy")),
            P(),
        ),
        out_specs=(P("gx", "gy", None), P("gx", "gy", None)),
        check_vma=False,
    )
```

```python
import functools

import jax
import jax.numpy as jnp
from jax import lax
from jax.experimental import pallas as pl
from jax.experimental.pallas import tpu as pltpu
from jax.sharding import PartitionSpec as P

STEPS = 4
SRC_DEPTH = 6
REC_DEPTH = 3
NX, NY, NZ = 8, 32, 128
W = 4
SLAB = 16

C0, C1, C2, C3, C4 = (-205.0 / 72.0, 8.0 / 5.0, -1.0 / 5.0, 8.0 / 315.0, -1.0 / 560.0)
CK = (C0, C1, C2, C3, C4)
courant_sq = 0.0625
prior_var = 0.01

f32 = jnp.float32
VM = pl.BlockSpec(memory_space=pltpu.VMEM)
SM = pl.BlockSpec(memory_space=pltpu.SMEM)


def sds(*shape):
    return jax.ShapeDtypeStruct(shape, f32)


def lanes(rows=1):
    return lax.broadcasted_iota(jnp.int32, (rows, 128), 1)


def roll(x, k):
    k = k % 128
    return x if k == 0 else pltpu.roll(x, k, 1)


def pack(rows):
    part = lanes() // SLAB
    out = jnp.where(part == 0, rows[0], 0.0)
    for x in range(1, NX):
        out = jnp.where(part == x, roll(rows[x], SLAB * x), out)
    return out


def put_strips(i, p, s, xlo, xhi, ylo, yhi):
    out, j = (xlo, i) if i < W else (xhi, i - W)
    out[NY * j : NY * (j + 1)] = p
    out[NY * (W + j) : NY * (W + j + 1)] = s
    ylo[8 * i : 8 * i + 4] = p[:W]
    ylo[8 * i + 4 : 8 * i + 8] = s[:W]
    yhi[8 * i : 8 * i + 4] = p[NY - W :]
    yhi[8 * i + 4 : 8 * i + 8] = s[NY - W :]


def first_kernel(c, s, p, obs, xlo, xhi, ylo, yhi, oc):
    oc[...] = jnp.zeros((16, 128), f32)
    oc[0:4, 0:64] = obs[...]
    for y in (ylo, yhi):
        y[80:88] = jnp.zeros((8, 128), f32)
        y[80:84, 0:64] = obs[...]
    for i in range(NX):
        put_strips(i, p[i], s[i], xlo, xhi, ylo, yhi)
    slab = pack([c[i] for i in range(NX)])
    ylo[64:80] = slab[:16]
    yhi[64:80] = slab[16:]


def fill(buf, field, rows_l, rows_r, md, mu, at, keep_d, keep_u):
    for i in range(NX):
        buf[W + i, 8:40] = field[i]
        buf[W + i, 4:8] = jnp.where(keep_d, md[8 * i + at : 8 * i + at + 4], 0.0)
        buf[W + i, 40:44] = jnp.where(keep_u, mu[8 * i + at : 8 * i + at + 4], 0.0)
    for j in range(W):
        buf[j, 8:40] = rows_l[j]
        buf[W + NX + j, 8:40] = rows_r[j]


def laplace(buf, i, wz):
    here = buf[W + i, 8:40]
    out = (3.0 * C0) * here
    for k in range(1, W + 1):
        beside = buf[W + i + k, 8:40] + buf[W + i - k, 8:40]
        beside = beside + buf[W + i, 8 + k : 40 + k] + buf[W + i, 8 - k : 40 - k]
        out = out + CK[k] * beside
        out = out + wz[k][0] * roll(here, -k) + wz[k][1] * roll(here, k)
    return out


def depth_weights():
    lane = lanes()
    return [None] + [
        (jnp.where(lane < NZ - k, CK[k], 0.0), jnp.where(lane >= k, CK[k], 0.0))
        for k in range(1, W + 1)
    ]


def edges():
    iy = lax.axis_index("gy")
    return iy > 0, iy < lax.axis_size("gy") - 1


def strip(m, at):
    return [m[at + NY * j : at + NY * (j + 1)] for j in range(W)]


def add_source(n, source, start, wavelet, field):
    width = NY * lax.axis_size("gy")
    sx = source[0] // width - lax.axis_index("gx") * NX
    sy = source[0] % width - lax.axis_index("gy") * NY

    @pl.when((sx >= 0) & (sx < NX) & (sy >= 0) & (sy < NY))
    def _():
        row = field[sx, pl.ds(sy, 1), :]
        add = jnp.where(lanes() == SRC_DEPTH, wavelet[0, start[0] + n], 0.0)
        field[sx, pl.ds(sy, 1), :] = row + add


def collect(n, md, mu, oc, oc_out):
    at = 80 if n == 0 else 64
    got_d, got_u = md[at : at + 8], mu[at : at + 8]
    oc_out[...] = oc[...]
    up, turn_u, down, turn_d = ((0, 64, 12, 64), (4, 0, 12, 0), (4, 64, 8, 64), (8, 0, None, 0))[n]
    oc_out[up : up + 4] = oc_out[up : up + 4] + roll(got_u, turn_u)[:4]
    if down is not None:
        oc_out[down : down + 4] = oc_out[down : down + 4] + roll(got_d, turn_d)[:4]
    return got_d, got_u


def step_kernel(n, source, start, wavelet, c, p, pp, q, ql, ml, mr, md, mu, oc, *rest):
    if n == 0:
        lpk, oc_out, qn, pn, xlo, xhi, ylo, yhi, lap_out, cext, bufp, bufs = rest
    if n == 1:
        cext, lpk, oc_out, qn, pn, xlo, xhi, ylo, yhi, lap_out, bufp, bufs = rest
    if n == 2:
        lap_other, lpk, oc_out, qn, pn, xlo, xhi, ylo, yhi, img_out, bufp, bufs = rest
    keep_d, keep_u = edges()
    lane = lanes()
    wz = depth_weights()
    fill(bufp, p, strip(ml, 0), strip(mr, 0), md, mu, 0, keep_d, keep_u)
    s = [c[i] * q[i] for i in range(NX)]
    fill(bufs, s, strip(ml, 128), strip(mr, 128), md, mu, 4, keep_d, keep_u)
    slab = jnp.zeros((NY, NZ), f32)
    for i in range(NX):
        lap = laplace(bufp, i, wz)
        slab = jnp.where(lane // SLAB == i, roll(lap, SLAB * i), slab)
        pn[i] = 2.0 * p[i] - pp[i] + c[i] * lap
        q_new = 2.0 * q[i] - ql[i] + laplace(bufs, i, wz)
        qn[i] = q_new
        if n < 2:
            lap_out[i] = lap
        else:
            img_out[i] = lap * q[i] + q_new * lap_other[i]
    lpk[...] = slab
    add_source(n, source, start, wavelet, pn)
    got_d, got_u = collect(n, md, mu, oc, oc_out)
    for i in range(NX):
        put_strips(i, pn[i], c[i] * qn[i], xlo, xhi, ylo, yhi)
    ylo[64:72] = got_u
    yhi[64:72] = got_d
    if n == 0:
        cext[0:16] = jnp.where(keep_d, md[64:80], 0.0)
        cext[16:48] = pack([c[i] for i in range(NX)])
        cext[48:64] = jnp.where(keep_u, mu[64:80], 0.0)
        xlo[256:320] = cext[...]
        xhi[256:320] = cext[...]
    if n == 1:
        xlo[256:288] = mr[272:304]
        xhi[256:288] = ml[272:304]


def plane_kernel(
    source, start, wavelet, c, p, pp, ml, mr, md, mu, oc,
    lpk, oc_out, lap_out, mat, mat_lo, mat_hi, bufp, pn,
):
    keep_d, keep_u = edges()
    lane = lanes()
    wz = depth_weights()
    fill(bufp, p, strip(ml, 0), strip(mr, 0), md, mu, 0, keep_d, keep_u)
    slab = jnp.zeros((NY, NZ), f32)
    for i in range(NX):
        lap = laplace(bufp, i, wz)
        slab = jnp.where(lane // SLAB == i, roll(lap, SLAB * i), slab)
        lap_out[i] = lap
        pn[i] = 2.0 * p[i] - pp[i] + c[i] * lap
    lpk[...] = slab
    add_source(3, source, start, wavelet, pn)
    collect(3, md, mu, oc, oc_out)
    out = jnp.zeros((NY, NZ), f32)
    for i in range(NX):
        for t, row in ((2, pp[i]), (3, p[i]), (4, pn[i])):
            to = 4 * i + t - 1
            out = jnp.where(lane == to, roll(row, to - REC_DEPTH), out)
    mat[...] = out
    mat_lo[...] = out[:16]
    mat_hi[...] = out[16:]


def adjoint_kernel(
    c, q, ql, ml, mr, md, mu, lap3, lap0, q3, img, vel, noise, mat, p1, own, sent, base, bufs
):
    keep_d, keep_u = edges()
    lane = lanes()
    wz = depth_weights()
    first = lax.axis_index("shot") % 2 == 0
    s = [c[i] * q[i] for i in range(NX)]
    fill(bufs, s, strip(ml, 128), strip(mr, 128), md, mu, 4, keep_d, keep_u)
    m = mat[...]
    for i in range(NX):
        q_new = 2.0 * q[i] - ql[i] + laplace(bufs, i, wz)
        image = img[i] + lap3[i] * q3[i] + q_new * lap0[i]
        grad = (2.0 * courant_sq) * vel[i] * image
        weighted = grad * noise[i]
        own[i] = jnp.where(first, grad, weighted)
        sent[i] = jnp.where(first, weighted, grad)
        m = jnp.where(lane == 4 * i, roll(p1[i], 4 * i - REC_DEPTH), m)
    base[...] = roll(m[:16], 32) + roll(m[16:], 64)


def chunk_kernel(base, got_d, got_u, oc, out):
    packed = base[...] + got_d[...] + roll(got_u[...], 96)
    for g in range(out.shape[0]):
        out[g, 0:16] = oc[...]
        out[g, 16:32] = packed


def lap_packed(buf, g, lo, hi, wz):
    lane = lanes()
    here = buf[g, lo:hi]
    before, after = buf[g - 1, lo:hi], buf[g + 1, lo:hi]
    out = (3.0 * C0) * here
    for k in range(1, W + 1):
        t = SLAB * k
        beside = jnp.where(lane < 128 - t, roll(here, -t), roll(after, -t))
        beside = beside + jnp.where(lane >= t, roll(here, t), roll(before, t))
        beside = beside + buf[g, lo + k : hi + k] + buf[g, lo - k : hi - k]
        out = out + CK[k] * beside
        out = out + wz[k][0] * roll(here, -k) + wz[k][1] * roll(here, k)
    return out


def table_kernel(rec, vel, noise, keyx, hoty, count, vpk, zpk, cols, rows, hot):
    ix, iy, ngy = lax.axis_index("gx"), lax.axis_index("gy"), lax.axis_size("gy")
    half = ngy // 2
    bits = (NY * ngy).bit_length() - 1
    assert 2**bits == NY * ngy
    odd = iy % 2 == 1
    low = lanes() < 64
    bf = jnp.bfloat16
    coly = lax.broadcasted_iota(jnp.int32, (64, 128), 0).astype(f32).astype(bf)
    row4 = (lax.broadcasted_iota(jnp.int32, (128, 128), 0) // 4).astype(f32).astype(bf)
    one, none = jnp.ones((), bf), jnp.zeros((), bf)
    kx = jnp.clip((rec[...] >> bits) - ix * NX + 12, -1, 32).astype(f32)
    ky = jnp.clip((rec[...] & (NY * ngy - 1)) - iy * NY + 16, -1, 64).astype(f32)
    for ref, k in ((rows, kx), (cols, ky)):
        ref[0] = jnp.where(odd, roll(k, 64), k)
    for g in range(rec.shape[0]):
        first = (iy + 2 * (g % half)) % ngy
        a = pl.ds((g // half) * half + first // 2, 1)
        b = pl.ds((g // half) * half + ((first + 1) % ngy) // 2, 1)
        key = jnp.where(low, rows[0, a, :], rows[0, b, :])
        keyx[g : g + 1] = key
        hot[:, 128 * g : 128 * (g + 1)] = jnp.where(row4 == key.astype(bf), one, none)
        here = jnp.where(low, cols[0, a, :], cols[0, b, :]).astype(bf)
        hoty[:, 128 * g : 128 * (g + 1)] = jnp.where(coly == here, one, none)
    count[...] = lax.dot_general(
        hot[...], hoty[...], (((1,), (1,)), ((), ())), preferred_element_type=f32
    )
    vpk[...] = pack([vel[i] for i in range(NX)])
    zpk[...] = pack([noise[i] for i in range(NX)])


def last_kernel(
    got, keyx, hoty, count, cext, ml1, mr1, ml2, mr2, lp0, lp1, lp2, lp3, vpk, zpk, own, other,
    out, table, x, r3, r2, r1, inj,
):
    ngx = got.shape[0]
    lane = lanes()
    ix = lax.axis_index("gx")
    c1l, c1r = ml1.at[256:320], mr1.at[256:320]
    c2l, c2r = ml2.at[256:288], mr2.at[256:288]
    bf = jnp.bfloat16
    row4 = (lax.broadcasted_iota(jnp.int32, (128, 128), 0) // 4).astype(f32).astype(bf)
    none = jnp.zeros((), bf)

    def build(g, carry):
        for rp in range(4):
            at = pl.ds(pl.multiple_of((4 * g + rp) * 128, 128), 128)
            val = got[g, 4 * rp : 4 * rp + 4, :]
            hi = val.astype(bf).astype(f32)
            mid = (val - hi).astype(bf).astype(f32)
            low = val - hi - mid
            here = row4 == keyx[pl.ds(4 * g + rp, 1), :].astype(bf)
            for part, v in enumerate((hi, mid, low)):
                v16 = jnp.concatenate([v, v, v, v], 0).astype(bf)
                v128 = jnp.concatenate([v16] * 8, 0)
                table[128 * part : 128 * (part + 1), at] = jnp.where(here, v128, none)
        return carry

    lax.fori_loop(0, ngx, build, 0, unroll=2)
    sums = lax.dot_general(
        table[...], hoty[...], (((1,), (1,)), ((), ())), preferred_element_type=f32
    )
    seen = sums[0:128] + sums[128:256] + sums[256:384]
    tr = jnp.concatenate([seen, count[...]], 1).T

    k_in = lax.broadcasted_iota(jnp.int32, (128, 512), 0)
    k_out = lax.broadcasted_iota(jnp.int32, (128, 512), 1)
    spread_to = jnp.where(
        (k_in < 32) & (k_out == (k_in % 4) * 128 + (k_in // 4) * SLAB + REC_DEPTH), 1.0, 0.0
    )
    dense = []
    for g in range(5):
        src = ix + (g - 2)
        ok = (src >= 0) & (src < ngx)
        blk = got[jnp.clip(src, 0, ngx - 1), 16:32, :]
        m = jnp.concatenate([roll(blk, -32 * t) for t in range(4)], 0)
        m = jnp.where(ok, m, 0.0)
        s_g = roll(tr[:64], 16 - 32 * g)
        n_g = roll(tr[64:], 16 - 32 * g)
        dense.append(n_g * m - s_g)
    inj[...] = jnp.dot(
        jnp.concatenate(dense, 0), spread_to,
        precision=lax.Precision.HIGHEST, preferred_element_type=f32,
    )

    def j(n, g, lo, hi):
        return inj[64 * g + lo : 64 * g + hi, 128 * n : 128 * (n + 1)]

    d = lane % SLAB
    wz = [None] + [
        (jnp.where(d < SLAB - k, CK[k], 0.0), jnp.where(d >= k, CK[k], 0.0))
        for k in range(1, W + 1)
    ]
    coef = {1: c1l, 2: cext, 3: c1r}
    pad = jnp.zeros((16, 128), f32)
    for g in range(5):
        r3[g] = j(3, g, 0, 64)
        if g in coef:
            x[g] = coef[g][...] * r3[g]
    for g, far in ((0, c2l), (4, c2r)):
        x[g, 0:16] = pad
        x[g, 16:48] = far[...] * r3[g, 16:48]
        x[g, 48:64] = pad
    for g in (1, 2, 3):
        r2[g] = 2.0 * r3[g, 8:56] + lap_packed(x, g, 8, 56, wz) + j(2, g, 8, 56)
    x[0] = jnp.zeros((64, 128), f32)
    x[4] = jnp.zeros((64, 128), f32)
    for g in (1, 2, 3):
        x[g, 0:8] = pad[:8]
        x[g, 8:56] = coef[g][8:56] * r2[g]
        x[g, 56:64] = pad[:8]
    for g in (1, 2, 3):
        r1[g] = 2.0 * r2[g] - r3[g, 8:56] + lap_packed(x, g, 8, 56, wz) + j(1, g, 8, 56)
    for g in (1, 2, 3):
        x[g, 8:56] = coef[g][8:56] * r1[g]
    r0 = 2.0 * r1[2, 8:40] - r2[2, 8:40] + lap_packed(x, 2, 16, 48, wz) + j(0, 2, 16, 48)
    corr = r0 * lp0[...] + r1[2, 8:40] * lp1[...] + r2[2, 8:40] * lp2[...]
    corr = corr + r3[2, 16:48] * lp3[...]

    cells = NX * NY
    for i in range(NX):
        out[NY * i : NY * (i + 1)] = own[i] + other[i]
    grad = (2.0 * courant_sq) * vpk[...] * corr
    out[cells : cells + NY] = grad
    out[cells + NY : cells + 2 * NY] = grad * zpk[...]


def sum_kernel(every, logs, grad_mean, grad_logs):
    lane = lanes()
    cells = NX * NY

    def packed(at):
        rows = slice(at, at + NY)
        return (every[0, rows] + every[1, rows]) + (every[2, rows] + every[3, rows])

    grad_in, weighted_in = packed(cells), packed(cells + NY)
    for i in range(NX):
        rows = slice(NY * i, NY * (i + 1))
        grad = every[0, rows] + every[2, rows]
        grad_mean[i] = grad + jnp.where(lane < SLAB, roll(grad_in, -SLAB * i), 0.0)
        weighted = every[1, rows] + every[3, rows]
        weighted = weighted + jnp.where(lane < SLAB, roll(weighted_in, -SLAB * i), 0.0)
        spread = jnp.exp(logs[i])
        grad_logs[i] = spread * weighted + jnp.exp(2.0 * logs[i]) / prior_var - 1.0


def call(kernel, outs, scratch=(), smem=0, mib=4, cost=None):
    def go(*args):
        return pl.pallas_call(
            kernel,
            out_shape=outs,
            in_specs=[SM] * smem + [VM] * (len(args) - smem),
            out_specs=jax.tree.map(lambda _: VM, outs),
            scratch_shapes=list(scratch),
            cost_estimate=cost and pl.CostEstimate(
                flops=cost[0], bytes_accessed=cost[1], transcendentals=0
            ),
            compiler_params=pltpu.CompilerParams(vmem_limit_bytes=mib * 2**20),
        )(*args)

    return go


def shift(x, axis, k, wrap=False):
    n = lax.axis_size(axis)
    return lax.ppermute(x, axis, [(i, (i + k) % n) for i in range(n) if wrap or 0 <= i + k < n])


def local(
    mean_velocity,
    log_scale,
    shot_noise,
    checkpoint_prev,
    checkpoint_now,
    adjoint_next,
    adjoint_now,
    wavelet,
    source_column,
    receiver_column,
    observed,
    start_step,
):
    ngx, ngy, nshot = lax.axis_size("gx"), lax.axis_size("gy"), lax.axis_size("shot")
    noise = shot_noise[0]
    p_prev, p = checkpoint_prev[0], checkpoint_now[0]
    q_later, q = adjoint_next[0], adjoint_now[0]
    F = sds(NX, NY, NZ)
    vel = mean_velocity + jnp.exp(log_scale) * noise
    coef = courant_sq * vel * vel
    xlo, xhi, ylo, yhi, oc = call(
        first_kernel,
        (sds(256, 128), sds(256, 128), sds(88, 128), sds(88, 128), sds(16, 128)),
    )(coef, coef * q, p, observed[0])
    buf = pltpu.VMEM((NX + 2 * W, 48, NZ), f32)
    slabs, keep = [], {}
    for n in range(STEPS):
        ml, mr = shift(xhi, "gx", 1), shift(xlo, "gx", -1)
        md, mu = shift(yhi, "gy", 1, True), shift(ylo, "gy", -1, True)
        halos = (ml, mr, md, mu)
        if n == STEPS - 1:
            break
        extra = {1: (keep.get("cext"),), 2: (keep.get("lap1"),)}.get(n, ())
        rows = (320, 288, 256)[n]
        outs = [sds(NY, NZ), sds(16, 128), F, F]
        outs += [sds(rows, 128), sds(rows, 128), sds(72, 128), sds(72, 128), F]
        if n == 0:
            outs.append(sds(64, 128))
        res = call(functools.partial(step_kernel, n), tuple(outs), (buf, buf), smem=3)(
            source_column, start_step, wavelet, coef, p, p_prev, q, q_later, *halos, oc, *extra
        )
        lpk, oc, q_next, p_next, xlo, xhi, ylo, yhi = res[:8]
        slabs.append(lpk)
        if n == 0:
            keep["lap0"], keep["cext"], keep["q3"], keep["p1"] = res[8], res[9], q_next, p_next
        if n == 1:
            keep["lap1"], keep["c"] = res[8], [ml, mr]
        if n == 2:
            img = res[8]
            keep["c"] += [ml, mr]
        p_prev, p = p, p_next
        q_later, q = q, q_next

    lpk, oc, lap3, mat, mat_lo, mat_hi = call(
        plane_kernel,
        (sds(NY, NZ), sds(16, 128), F, sds(NY, NZ), sds(16, NZ), sds(16, NZ)),
        (buf, pltpu.VMEM((NX, NY, NZ), f32)),
        smem=3,
    )(source_column, start_step, wavelet, coef, p, p_prev, *halos, oc)
    slabs.append(lpk)
    mat_d, mat_u = shift(mat_hi, "gy", 1), shift(mat_lo, "gy", -1)
    own, sent, base = call(
        adjoint_kernel, (F, F, sds(16, NZ)), (buf,), cost=(2_000_000, 2_000_000)
    )(
        coef, q, q_later, *halos, lap3, keep["lap0"], keep["q3"], img, vel, noise, mat, keep["p1"]
    )
    other = lax.ppermute(sent, "shot", [(i, i ^ 1) for i in range(nshot)])
    nrec = receiver_column.shape[1]
    bf = jnp.bfloat16
    keyx, hoty, count, vpk, zpk = call(
        table_kernel,
        (
            sds(nrec // 128, 128),
            jax.ShapeDtypeStruct((64, nrec), bf),
            sds(128, 64),
            sds(NY, NZ),
            sds(NY, NZ),
        ),
        [pltpu.VMEM((1, nrec // 128, 128), f32)] * 2 + [pltpu.VMEM((128, nrec), bf)],
        mib=12,
    )(receiver_column.reshape(-1, 128), vel, noise)
    chunk = call(chunk_kernel, sds(ngx, 32, 128))(base, mat_d, mat_u, oc)
    got = lax.all_to_all(chunk, "gx", 0, 0)
    g5 = pltpu.VMEM((5, 64, 128), f32)
    g48 = pltpu.VMEM((5, 48, 128), f32)
    part = call(
        last_kernel,
        sds(NX * NY + 2 * NY, NZ),
        (pltpu.VMEM((384, nrec), bf), g5, g5, g48, g48, pltpu.VMEM((320, 512), f32)),
        mib=24,
    )(got, keyx, hoty, count, keep["cext"], *keep["c"], *slabs, vpk, zpk, own, other)
    every = lax.all_gather(part, "shot", axis=0)
    return call(sum_kernel, (F, F))(every, log_scale)


def solution(mesh):
    return jax.shard_map(
        local,
        mesh=mesh,
        in_specs=(
            P("gx", "gy", None),
            P("gx", "gy", None),
            P("shot", "gx", "gy", None),
            P("shot", "gx", "gy", None),
            P("shot", "gx", "gy", None),
            P("shot", "gx", "gy", None),
            P("shot", "gx", "gy", None),
            P("shot", None),
            P("shot"),
            P("shot", None),
            P("shot", None, ("gx", "gy")),
            P(),
        ),
        out_specs=(P("gx", "gy", None), P("gx", "gy", None)),
        check_vma=False,
    )
```

```python
import functools

import jax
import jax.numpy as jnp
from jax import lax
from jax.experimental import pallas as pl
from jax.experimental.pallas import tpu as pltpu
from jax.sharding import PartitionSpec as P

STEPS = 4
SRC_DEPTH = 6
REC_DEPTH = 3
NX, NY, NZ = 8, 32, 128
W = 4
SLAB = 16

C0, C1, C2, C3, C4 = (-205.0 / 72.0, 8.0 / 5.0, -1.0 / 5.0, 8.0 / 315.0, -1.0 / 560.0)
CK = (C0, C1, C2, C3, C4)
courant_sq = 0.0625
prior_var = 0.01

f32 = jnp.float32
VM = pl.BlockSpec(memory_space=pltpu.VMEM)
SM = pl.BlockSpec(memory_space=pltpu.SMEM)


def sds(*shape):
    return jax.ShapeDtypeStruct(shape, f32)


def lanes(rows=1):
    return lax.broadcasted_iota(jnp.int32, (rows, 128), 1)


def roll(x, k):
    k = k % 128
    return x if k == 0 else pltpu.roll(x, k, 1)


def pack(rows):
    part = lanes() // SLAB
    out = jnp.where(part == 0, rows[0], 0.0)
    for x in range(1, NX):
        out = jnp.where(part == x, roll(rows[x], SLAB * x), out)
    return out


def put_strips(i, p, s, xlo, xhi, ylo, yhi):
    out, j = (xlo, i) if i < W else (xhi, i - W)
    out[NY * j : NY * (j + 1)] = p
    out[NY * (W + j) : NY * (W + j + 1)] = s
    ylo[8 * i : 8 * i + 4] = p[:W]
    ylo[8 * i + 4 : 8 * i + 8] = s[:W]
    yhi[8 * i : 8 * i + 4] = p[NY - W :]
    yhi[8 * i + 4 : 8 * i + 8] = s[NY - W :]


def first_kernel(c, s, p, obs, xlo, xhi, ylo, yhi, oc):
    oc[...] = jnp.zeros((16, 128), f32)
    oc[0:4, 0:64] = obs[...]
    for y in (ylo, yhi):
        y[80:88] = jnp.zeros((8, 128), f32)
        y[80:84, 0:64] = obs[...]
    for i in range(NX):
        put_strips(i, p[i], s[i], xlo, xhi, ylo, yhi)
    slab = pack([c[i] for i in range(NX)])
    ylo[64:80] = slab[:16]
    yhi[64:80] = slab[16:]


def fill(buf, field, rows_l, rows_r, md, mu, at, keep_d, keep_u):
    for i in range(NX):
        buf[W + i, 8:40] = field[i]
        buf[W + i, 4:8] = jnp.where(keep_d, md[8 * i + at : 8 * i + at + 4], 0.0)
        buf[W + i, 40:44] = jnp.where(keep_u, mu[8 * i + at : 8 * i + at + 4], 0.0)
    for j in range(W):
        buf[j, 8:40] = rows_l[j]
        buf[W + NX + j, 8:40] = rows_r[j]


def laplace(buf, i, wz):
    here = buf[W + i, 8:40]
    out = (3.0 * C0) * here
    for k in range(1, W + 1):
        beside = buf[W + i + k, 8:40] + buf[W + i - k, 8:40]
        beside = beside + buf[W + i, 8 + k : 40 + k] + buf[W + i, 8 - k : 40 - k]
        out = out + CK[k] * beside
        out = out + wz[k][0] * roll(here, -k) + wz[k][1] * roll(here, k)
    return out


def depth_weights():
    lane = lanes()
    return [None] + [
        (jnp.where(lane < NZ - k, CK[k], 0.0), jnp.where(lane >= k, CK[k], 0.0))
        for k in range(1, W + 1)
    ]


def edges():
    iy = lax.axis_index("gy")
    return iy > 0, iy < lax.axis_size("gy") - 1


def strip(m, at):
    return [m[at + NY * j : at + NY * (j + 1)] for j in range(W)]


def add_source(n, source, start, wavelet, field):
    width = NY * lax.axis_size("gy")
    sx = source[0] // width - lax.axis_index("gx") * NX
    sy = source[0] % width - lax.axis_index("gy") * NY

    @pl.when((sx >= 0) & (sx < NX) & (sy >= 0) & (sy < NY))
    def _():
        row = field[sx, pl.ds(sy, 1), :]
        add = jnp.where(lanes() == SRC_DEPTH, wavelet[0, start[0] + n], 0.0)
        field[sx, pl.ds(sy, 1), :] = row + add


def collect(n, md, mu, oc, oc_out):
    at = 80 if n == 0 else 64
    got_d, got_u = md[at : at + 8], mu[at : at + 8]
    oc_out[...] = oc[...]
    up, turn_u, down, turn_d = ((0, 64, 12, 64), (4, 0, 12, 0), (4, 64, 8, 64), (8, 0, None, 0))[n]
    oc_out[up : up + 4] = oc_out[up : up + 4] + roll(got_u, turn_u)[:4]
    if down is not None:
        oc_out[down : down + 4] = oc_out[down : down + 4] + roll(got_d, turn_d)[:4]
    return got_d, got_u


def step_kernel(n, source, start, wavelet, c, p, pp, q, ql, ml, mr, md, mu, oc, *rest):
    if n == 0:
        lpk, oc_out, qn, pn, xlo, xhi, ylo, yhi, lap_out, cext, bufp, bufs = rest
    if n == 1:
        cext, lpk, oc_out, qn, pn, xlo, xhi, ylo, yhi, lap_out, bufp, bufs = rest
    if n == 2:
        lap_other, lpk, oc_out, qn, pn, xlo, xhi, ylo, yhi, img_out, mat, bufp, bufs = rest
    keep_d, keep_u = edges()
    lane = lanes()
    wz = depth_weights()
    fill(bufp, p, strip(ml, 0), strip(mr, 0), md, mu, 0, keep_d, keep_u)
    s = [c[i] * q[i] for i in range(NX)]
    fill(bufs, s, strip(ml, 128), strip(mr, 128), md, mu, 4, keep_d, keep_u)
    slab = jnp.zeros((NY, NZ), f32)
    for i in range(NX):
        lap = laplace(bufp, i, wz)
        slab = jnp.where(lane // SLAB == i, roll(lap, SLAB * i), slab)
        pn[i] = 2.0 * p[i] - pp[i] + c[i] * lap
        q_new = 2.0 * q[i] - ql[i] + laplace(bufs, i, wz)
        qn[i] = q_new
        if n < 2:
            lap_out[i] = lap
        else:
            img_out[i] = lap * q[i] + q_new * lap_other[i]
    lpk[...] = slab
    add_source(n, source, start, wavelet, pn)
    got_d, got_u = collect(n, md, mu, oc, oc_out)
    for i in range(NX):
        put_strips(i, pn[i], c[i] * qn[i], xlo, xhi, ylo, yhi)
    ylo[64:72] = got_u
    yhi[64:72] = got_d
    if n == 0:
        cext[0:16] = jnp.where(keep_d, md[64:80], 0.0)
        cext[16:48] = pack([c[i] for i in range(NX)])
        cext[48:64] = jnp.where(keep_u, mu[64:80], 0.0)
        xlo[256:320] = cext[...]
        xhi[256:320] = cext[...]
    if n == 2:
        new = [pn[i] for i in range(NX)]
        slab = pack(new)
        d = lane % SLAB
        deep = (3.0 * C0) * slab
        for k in range(1, W + 1):
            deep = deep + jnp.where(d < SLAB - k, CK[k], 0.0) * roll(slab, -k)
            deep = deep + jnp.where(d >= k, CK[k], 0.0) * roll(slab, k)
        out = jnp.zeros((NY, NZ), f32)
        for i in range(NX):
            for t, row, at in (
                (0, pp[i], REC_DEPTH),
                (1, p[i], REC_DEPTH),
                (2, new[i], REC_DEPTH),
                (3, deep, SLAB * i + REC_DEPTH),
            ):
                out = jnp.where(lane == 4 * i + t, roll(row, 4 * i + t - at), out)
        mat[...] = out
        ylo[72:88] = out[:16]
        yhi[72:88] = out[16:]
    if n == 1:
        xlo[256:288] = mr[272:304]
        xhi[256:288] = ml[272:304]


def final_kernel(
    c, p, q, ql, ml, mr, md, mu, lap0, q3, img, vel, noise, lpk, own, sent, bufp, bufs
):
    keep_d, keep_u = edges()
    lane = lanes()
    wz = depth_weights()
    first = lax.axis_index("shot") % 2 == 0
    fill(bufp, p, strip(ml, 0), strip(mr, 0), md, mu, 0, keep_d, keep_u)
    s = [c[i] * q[i] for i in range(NX)]
    fill(bufs, s, strip(ml, 128), strip(mr, 128), md, mu, 4, keep_d, keep_u)
    slab = jnp.zeros((NY, NZ), f32)
    for i in range(NX):
        lap = laplace(bufp, i, wz)
        slab = jnp.where(lane // SLAB == i, roll(lap, SLAB * i), slab)
        q_new = 2.0 * q[i] - ql[i] + laplace(bufs, i, wz)
        image = img[i] + lap * q3[i] + q_new * lap0[i]
        grad = (2.0 * courant_sq) * vel[i] * image
        weighted = grad * noise[i]
        own[i] = jnp.where(first, grad, weighted)
        sent[i] = jnp.where(first, weighted, grad)
    lpk[...] = slab


def chunk_kernel(mat, md, mu, oc, out, traces):
    keep_d, keep_u = edges()
    collect(3, md, mu, oc, traces)
    packed = jnp.where(keep_d, md[72:88], 0.0) + roll(jnp.where(keep_u, mu[72:88], 0.0), 96)
    packed = packed + roll(mat[0:16], 32) + roll(mat[16:32], 64)
    for g in range(out.shape[0]):
        out[g, 0:16] = traces[...]
        out[g, 16:32] = packed


def lap_packed(buf, g, lo, hi, wz):
    lane = lanes()
    here = buf[g, lo:hi]
    before, after = buf[g - 1, lo:hi], buf[g + 1, lo:hi]
    out = (3.0 * C0) * here
    for k in range(1, W + 1):
        t = SLAB * k
        beside = jnp.where(lane < 128 - t, roll(here, -t), roll(after, -t))
        beside = beside + jnp.where(lane >= t, roll(here, t), roll(before, t))
        beside = beside + buf[g, lo + k : hi + k] + buf[g, lo - k : hi - k]
        out = out + CK[k] * beside
        out = out + wz[k][0] * roll(here, -k) + wz[k][1] * roll(here, k)
    return out


def table_kernel(rec, vel, noise, keyx, hoty, count, vpk, zpk, cols, rows, hot):
    ix, iy, ngy = lax.axis_index("gx"), lax.axis_index("gy"), lax.axis_size("gy")
    half = ngy // 2
    bits = (NY * ngy).bit_length() - 1
    assert 2**bits == NY * ngy
    odd = iy % 2 == 1
    low = lanes() < 64
    bf = jnp.bfloat16
    coly = lax.broadcasted_iota(jnp.int32, (64, 128), 0).astype(f32).astype(bf)
    row4 = (lax.broadcasted_iota(jnp.int32, (128, 128), 0) // 4).astype(f32).astype(bf)
    one, none = jnp.ones((), bf), jnp.zeros((), bf)
    kx = jnp.clip((rec[...] >> bits) - ix * NX + 12, -1, 32).astype(f32)
    ky = jnp.clip((rec[...] & (NY * ngy - 1)) - iy * NY + 16, -1, 64).astype(f32)
    for ref, k in ((rows, kx), (cols, ky)):
        ref[0] = jnp.where(odd, roll(k, 64), k)
    for g in range(rec.shape[0]):
        first = (iy + 2 * (g % half)) % ngy
        a = pl.ds((g // half) * half + first // 2, 1)
        b = pl.ds((g // half) * half + ((first + 1) % ngy) // 2, 1)
        key = jnp.where(low, rows[0, a, :], rows[0, b, :])
        keyx[g : g + 1] = key
        hot[:, 128 * g : 128 * (g + 1)] = jnp.where(row4 == key.astype(bf), one, none)
        here = jnp.where(low, cols[0, a, :], cols[0, b, :]).astype(bf)
        hoty[:, 128 * g : 128 * (g + 1)] = jnp.where(coly == here, one, none)
    count[...] = lax.dot_general(
        hot[...], hoty[...], (((1,), (1,)), ((), ())), preferred_element_type=f32
    )
    vpk[...] = pack([vel[i] for i in range(NX)])
    zpk[...] = pack([noise[i] for i in range(NX)])


def last_kernel(
    got, keyx, hoty, count, cext, ml1, mr1, ml2, mr2, lp0, lp1, lp2, lp3, vpk, zpk, own, other,
    out, table, x, r3, r2, r1, inj,
):
    ngx = got.shape[0]
    lane = lanes()
    ix = lax.axis_index("gx")
    c1l, c1r = ml1.at[256:320], mr1.at[256:320]
    c2l, c2r = ml2.at[256:288], mr2.at[256:288]
    bf = jnp.bfloat16
    row4 = (lax.broadcasted_iota(jnp.int32, (128, 128), 0) // 4).astype(f32).astype(bf)
    none = jnp.zeros((), bf)

    def build(g, carry):
        for rp in range(4):
            at = pl.ds(pl.multiple_of((4 * g + rp) * 128, 128), 128)
            val = got[g, 4 * rp : 4 * rp + 4, :]
            hi = val.astype(bf).astype(f32)
            mid = (val - hi).astype(bf).astype(f32)
            low = val - hi - mid
            here = row4 == keyx[pl.ds(4 * g + rp, 1), :].astype(bf)
            for part, v in enumerate((hi, mid, low)):
                v16 = jnp.concatenate([v, v, v, v], 0).astype(bf)
                v128 = jnp.concatenate([v16] * 8, 0)
                table[128 * part : 128 * (part + 1), at] = jnp.where(here, v128, none)
        at = pl.ds(pl.multiple_of(g * 512, 512), 512)
        return carry + lax.dot_general(
            table[:, at], hoty[:, at], (((1,), (1,)), ((), ())), preferred_element_type=f32
        )

    sums = lax.fori_loop(0, ngx, build, jnp.zeros((384, 64), f32), unroll=ngx)
    seen = sums[0:128] + sums[128:256] + sums[256:384]
    tr = jnp.concatenate([seen, count[...]], 1).T

    k_in = lax.broadcasted_iota(jnp.int32, (128, 512), 0)
    k_out = lax.broadcasted_iota(jnp.int32, (128, 512), 1)
    spread_to = jnp.where(
        (k_in < 32) & (k_out == (k_in % 4) * 128 + (k_in // 4) * SLAB + REC_DEPTH), 1.0, 0.0
    )
    dense, raw = [], []
    for g in range(5):
        src = ix + (g - 2)
        ok = (src >= 0) & (src < ngx)
        blk = got[jnp.clip(src, 0, ngx - 1), 16:32, :]
        m = jnp.concatenate([roll(blk, -32 * t) for t in range(4)], 0)
        m = jnp.where(ok, m, 0.0)
        s_g = roll(tr[:64], 16 - 32 * g)
        n_g = roll(tr[64:], 16 - 32 * g)
        dense.append(jnp.where(lane % 4 == 3, 0.0, n_g * m) - s_g)
        raw.append(jnp.where(lane % 4 == 0, n_g, m))
    inj[...] = jnp.dot(
        jnp.concatenate(dense + raw, 0), spread_to,
        precision=lax.Precision.HIGHEST, preferred_element_type=f32,
    )

    def j(n, g, lo, hi):
        return inj[64 * g + lo : 64 * g + hi, 128 * n : 128 * (n + 1)]

    coef = {1: c1l, 2: cext, 3: c1r}
    pad = jnp.zeros((16, 128), f32)
    plane = [j(2, 5 + g, 0, 64) for g in range(5)]
    for g in range(5):
        x[g] = plane[g]
    for g in range(5):
        lo, hi = (16, 48) if g in (0, 4) else (4, 60)
        part = j(3, 5 + g, lo, hi)
        for k in range(1, W + 1):
            t = SLAB * k
            here = x[g, lo:hi]
            after = x[g + 1, lo:hi] if g < 4 else jnp.zeros_like(here)
            before = x[g - 1, lo:hi] if g > 0 else jnp.zeros_like(here)
            beside = jnp.where(lane < 128 - t, roll(here, -t), roll(after, -t))
            beside = beside + jnp.where(lane >= t, roll(here, t), roll(before, t))
            beside = beside + x[g, lo + k : hi + k] + x[g, lo - k : hi - k]
            part = part + CK[k] * jnp.where(lane % SLAB == REC_DEPTH, beside, 0.0)
        c_g = (c2l, c2r)[g // 4][...] if g in (0, 4) else coef[g][lo:hi]
        p4 = 2.0 * x[g, lo:hi] - j(1, 5 + g, lo, hi) + c_g * part
        r3[g] = j(3, g, 0, 64)
        r3[g, lo:hi] = r3[g, lo:hi] + j(0, 5 + g, lo, hi) * p4

    d = lane % SLAB
    wz = [None] + [
        (jnp.where(d < SLAB - k, CK[k], 0.0), jnp.where(d >= k, CK[k], 0.0))
        for k in range(1, W + 1)
    ]
    for g in coef:
        x[g] = coef[g][...] * r3[g]
    for g, far in ((0, c2l), (4, c2r)):
        x[g, 0:16] = pad
        x[g, 16:48] = far[...] * r3[g, 16:48]
        x[g, 48:64] = pad
    for g in (1, 2, 3):
        r2[g] = 2.0 * r3[g, 8:56] + lap_packed(x, g, 8, 56, wz) + j(2, g, 8, 56)
    x[0] = jnp.zeros((64, 128), f32)
    x[4] = jnp.zeros((64, 128), f32)
    for g in (1, 2, 3):
        x[g, 0:8] = pad[:8]
        x[g, 8:56] = coef[g][8:56] * r2[g]
        x[g, 56:64] = pad[:8]
    for g in (1, 2, 3):
        r1[g] = 2.0 * r2[g] - r3[g, 8:56] + lap_packed(x, g, 8, 56, wz) + j(1, g, 8, 56)
    for g in (1, 2, 3):
        x[g, 8:56] = coef[g][8:56] * r1[g]
    r0 = 2.0 * r1[2, 8:40] - r2[2, 8:40] + lap_packed(x, 2, 16, 48, wz) + j(0, 2, 16, 48)
    corr = r0 * lp0[...] + r1[2, 8:40] * lp1[...] + r2[2, 8:40] * lp2[...]
    corr = corr + r3[2, 16:48] * lp3[...]

    cells = NX * NY
    for i in range(NX):
        out[NY * i : NY * (i + 1)] = own[i] + other[i]
    grad = (2.0 * courant_sq) * vpk[...] * corr
    out[cells : cells + NY] = grad
    out[cells + NY : cells + 2 * NY] = grad * zpk[...]


def sum_kernel(every, logs, grad_mean, grad_logs):
    lane = lanes()
    cells = NX * NY

    def packed(at):
        rows = slice(at, at + NY)
        return (every[0, rows] + every[1, rows]) + (every[2, rows] + every[3, rows])

    grad_in, weighted_in = packed(cells), packed(cells + NY)
    for i in range(NX):
        rows = slice(NY * i, NY * (i + 1))
        grad = every[0, rows] + every[2, rows]
        grad_mean[i] = grad + jnp.where(lane < SLAB, roll(grad_in, -SLAB * i), 0.0)
        weighted = every[1, rows] + every[3, rows]
        weighted = weighted + jnp.where(lane < SLAB, roll(weighted_in, -SLAB * i), 0.0)
        spread = jnp.exp(logs[i])
        grad_logs[i] = spread * weighted + jnp.exp(2.0 * logs[i]) / prior_var - 1.0


def call(kernel, outs, scratch=(), smem=0, mib=4):
    def go(*args):
        return pl.pallas_call(
            kernel,
            out_shape=outs,
            in_specs=[SM] * smem + [VM] * (len(args) - smem),
            out_specs=jax.tree.map(lambda _: VM, outs),
            scratch_shapes=list(scratch),
            compiler_params=pltpu.CompilerParams(vmem_limit_bytes=mib * 2**20),
        )(*args)

    return go


def shift(x, axis, k, wrap=False):
    n = lax.axis_size(axis)
    return lax.ppermute(x, axis, [(i, (i + k) % n) for i in range(n) if wrap or 0 <= i + k < n])


def local(
    mean_velocity,
    log_scale,
    shot_noise,
    checkpoint_prev,
    checkpoint_now,
    adjoint_next,
    adjoint_now,
    wavelet,
    source_column,
    receiver_column,
    observed,
    start_step,
):
    ngx, ngy, nshot = lax.axis_size("gx"), lax.axis_size("gy"), lax.axis_size("shot")
    noise = shot_noise[0]
    p_prev, p = checkpoint_prev[0], checkpoint_now[0]
    q_later, q = adjoint_next[0], adjoint_now[0]
    F = sds(NX, NY, NZ)
    vel = mean_velocity + jnp.exp(log_scale) * noise
    coef = courant_sq * vel * vel
    xlo, xhi, ylo, yhi, oc = call(
        first_kernel,
        (sds(256, 128), sds(256, 128), sds(88, 128), sds(88, 128), sds(16, 128)),
    )(coef, coef * q, p, observed[0])
    buf = pltpu.VMEM((NX + 2 * W, 48, NZ), f32)
    slabs, keep = [], {}
    for n in range(STEPS):
        ml, mr = shift(xhi, "gx", 1), shift(xlo, "gx", -1)
        md, mu = shift(yhi, "gy", 1, True), shift(ylo, "gy", -1, True)
        halos = (ml, mr, md, mu)
        if n == STEPS - 1:
            break
        extra = {1: (keep.get("cext"),), 2: (keep.get("lap1"),)}.get(n, ())
        rows = (320, 288, 256)[n]
        outs = [sds(NY, NZ), sds(16, 128), F, F]
        cols = (72, 72, 88)[n]
        outs += [sds(rows, 128), sds(rows, 128), sds(cols, 128), sds(cols, 128), F]
        if n != 1:
            outs.append(sds(64, 128) if n == 0 else sds(NY, NZ))
        res = call(functools.partial(step_kernel, n), tuple(outs), (buf, buf), smem=3)(
            source_column, start_step, wavelet, coef, p, p_prev, q, q_later, *halos, oc, *extra
        )
        lpk, oc, q_next, p_next, xlo, xhi, ylo, yhi = res[:8]
        slabs.append(lpk)
        if n == 0:
            keep["lap0"], keep["cext"], keep["q3"] = res[8], res[9], q_next
        if n == 1:
            keep["lap1"], keep["c"] = res[8], [ml, mr]
        if n == 2:
            img, mat = res[8], res[9]
            keep["c"] += [ml, mr]
        p_prev, p = p, p_next
        q_later, q = q, q_next

    chunk = call(chunk_kernel, sds(ngx, 32, 128), (pltpu.VMEM((16, 128), f32),))(mat, md, mu, oc)
    got = lax.all_to_all(chunk, "gx", 0, 0)
    lpk, own, sent = call(final_kernel, (sds(NY, NZ), F, F), (buf, buf))(
        coef, p, q, q_later, *halos, keep["lap0"], keep["q3"], img, vel, noise
    )
    slabs.append(lpk)
    other = lax.ppermute(sent, "shot", [(i, i ^ 1) for i in range(nshot)])
    nrec = receiver_column.shape[1]
    bf = jnp.bfloat16
    keyx, hoty, count, vpk, zpk = call(
        table_kernel,
        (
            sds(nrec // 128, 128),
            jax.ShapeDtypeStruct((64, nrec), bf),
            sds(128, 64),
            sds(NY, NZ),
            sds(NY, NZ),
        ),
        [pltpu.VMEM((1, nrec // 128, 128), f32)] * 2 + [pltpu.VMEM((128, nrec), bf)],
        mib=12,
    )(receiver_column.reshape(-1, 128), vel, noise)
    g5 = pltpu.VMEM((5, 64, 128), f32)
    g48 = pltpu.VMEM((5, 48, 128), f32)
    part = call(
        last_kernel,
        sds(NX * NY + 2 * NY, NZ),
        (pltpu.VMEM((384, nrec), bf), g5, g5, g48, g48, pltpu.VMEM((640, 512), f32)),
        mib=24,
    )(got, keyx, hoty, count, keep["cext"], *keep["c"], *slabs, vpk, zpk, own, other)
    every = lax.all_gather(part, "shot", axis=0)
    return call(sum_kernel, (F, F))(every, log_scale)


def solution(mesh):
    return jax.shard_map(
        local,
        mesh=mesh,
        in_specs=(
            P("gx", "gy", None),
            P("gx", "gy", None),
            P("shot", "gx", "gy", None),
            P("shot", "gx", "gy", None),
            P("shot", "gx", "gy", None),
            P("shot", "gx", "gy", None),
            P("shot", "gx", "gy", None),
            P("shot", None),
            P("shot"),
            P("shot", None),
            P("shot", None, ("gx", "gy")),
            P(),
        ),
        out_specs=(P("gx", "gy", None), P("gx", "gy", None)),
        check_vma=False,
    )
```

```python
import functools

import jax
import jax.numpy as jnp
from jax import lax
from jax.experimental import pallas as pl
from jax.experimental.pallas import tpu as pltpu
from jax.sharding import PartitionSpec as P

STEPS = 4
SRC_DEPTH = 6
REC_DEPTH = 3
NX, NY, NZ = 8, 32, 128
W = 4
SLAB = 16

C0, C1, C2, C3, C4 = (-205.0 / 72.0, 8.0 / 5.0, -1.0 / 5.0, 8.0 / 315.0, -1.0 / 560.0)
CK = (C0, C1, C2, C3, C4)
courant_sq = 0.0625
prior_var = 0.01

f32 = jnp.float32
VM = pl.BlockSpec(memory_space=pltpu.VMEM)
SM = pl.BlockSpec(memory_space=pltpu.SMEM)


def sds(*shape):
    return jax.ShapeDtypeStruct(shape, f32)


def lanes(rows=1):
    return lax.broadcasted_iota(jnp.int32, (rows, 128), 1)


def roll(x, k):
    k = k % 128
    return x if k == 0 else pltpu.roll(x, k, 1)


def pack(rows):
    part = lanes() // SLAB
    out = jnp.where(part == 0, rows[0], 0.0)
    for x in range(1, NX):
        out = jnp.where(part == x, roll(rows[x], SLAB * x), out)
    return out


def put_strips(i, p, s, xlo, xhi, ylo, yhi):
    out, j = (xlo, i) if i < W else (xhi, i - W)
    out[NY * j : NY * (j + 1)] = p
    out[NY * (W + j) : NY * (W + j + 1)] = s
    ylo[8 * i : 8 * i + 4] = p[:W]
    ylo[8 * i + 4 : 8 * i + 8] = s[:W]
    yhi[8 * i : 8 * i + 4] = p[NY - W :]
    yhi[8 * i + 4 : 8 * i + 8] = s[NY - W :]


def first_kernel(c, s, p, obs, xlo, xhi, ylo, yhi, oc):
    oc[...] = jnp.zeros((16, 128), f32)
    oc[0:4, 0:64] = obs[...]
    for y in (ylo, yhi):
        y[80:88] = jnp.zeros((8, 128), f32)
        y[80:84, 0:64] = obs[...]
    for i in range(NX):
        put_strips(i, p[i], s[i], xlo, xhi, ylo, yhi)
    slab = pack([c[i] for i in range(NX)])
    ylo[64:80] = slab[:16]
    yhi[64:80] = slab[16:]


def fill(buf, field, rows_l, rows_r, md, mu, at, keep_d, keep_u):
    for i in range(NX):
        buf[W + i, 8:40] = field[i]
        buf[W + i, 4:8] = jnp.where(keep_d, md[8 * i + at : 8 * i + at + 4], 0.0)
        buf[W + i, 40:44] = jnp.where(keep_u, mu[8 * i + at : 8 * i + at + 4], 0.0)
    for j in range(W):
        buf[j, 8:40] = rows_l[j]
        buf[W + NX + j, 8:40] = rows_r[j]


def laplace(buf, i, wz):
    here = buf[W + i, 8:40]
    out = (3.0 * C0) * here
    for k in range(1, W + 1):
        beside = buf[W + i + k, 8:40] + buf[W + i - k, 8:40]
        beside = beside + buf[W + i, 8 + k : 40 + k] + buf[W + i, 8 - k : 40 - k]
        out = out + CK[k] * beside
        out = out + wz[k][0] * roll(here, -k) + wz[k][1] * roll(here, k)
    return out


def depth_weights():
    lane = lanes()
    return [None] + [
        (jnp.where(lane < NZ - k, CK[k], 0.0), jnp.where(lane >= k, CK[k], 0.0))
        for k in range(1, W + 1)
    ]


def edges():
    iy = lax.axis_index("gy")
    return iy > 0, iy < lax.axis_size("gy") - 1


def strip(m, at):
    return [m[at + NY * j : at + NY * (j + 1)] for j in range(W)]


def add_source(n, source, start, wavelet, field):
    width = NY * lax.axis_size("gy")
    sx = source[0] // width - lax.axis_index("gx") * NX
    sy = source[0] % width - lax.axis_index("gy") * NY

    @pl.when((sx >= 0) & (sx < NX) & (sy >= 0) & (sy < NY))
    def _():
        row = field[sx, pl.ds(sy, 1), :]
        add = jnp.where(lanes() == SRC_DEPTH, wavelet[0, start[0] + n], 0.0)
        field[sx, pl.ds(sy, 1), :] = row + add


def collect(n, md, mu, oc, oc_out):
    at = 80 if n == 0 else 64
    got_d, got_u = md[at : at + 8], mu[at : at + 8]
    oc_out[...] = oc[...]
    up, turn_u, down, turn_d = ((0, 64, 12, 64), (4, 0, 12, 0), (4, 64, 8, 64), (8, 0, None, 0))[n]
    oc_out[up : up + 4] = oc_out[up : up + 4] + roll(got_u, turn_u)[:4]
    if down is not None:
        oc_out[down : down + 4] = oc_out[down : down + 4] + roll(got_d, turn_d)[:4]
    return got_d, got_u


def step_kernel(n, source, start, wavelet, c, p, pp, q, ql, ml, mr, md, mu, oc, *rest):
    if n == 0:
        lpk, oc_out, qn, pn, xlo, xhi, ylo, yhi, lap_out, cext, bufp, bufs = rest
    if n == 1:
        cext, lpk, oc_out, qn, pn, xlo, xhi, ylo, yhi, lap_out, bufp, bufs = rest
    if n == 2:
        lap_other, lpk, oc_out, qn, pn, xlo, xhi, ylo, yhi, img_out, mat, bufp, bufs = rest
    keep_d, keep_u = edges()
    lane = lanes()
    wz = depth_weights()
    fill(bufp, p, strip(ml, 0), strip(mr, 0), md, mu, 0, keep_d, keep_u)
    s = [c[i] * q[i] for i in range(NX)]
    fill(bufs, s, strip(ml, 128), strip(mr, 128), md, mu, 4, keep_d, keep_u)
    slab = jnp.zeros((NY, NZ), f32)
    for i in range(NX):
        lap = laplace(bufp, i, wz)
        slab = jnp.where(lane // SLAB == i, roll(lap, SLAB * i), slab)
        pn[i] = 2.0 * p[i] - pp[i] + c[i] * lap
        q_new = 2.0 * q[i] - ql[i] + laplace(bufs, i, wz)
        qn[i] = q_new
        if n < 2:
            lap_out[i] = lap
        else:
            img_out[i] = lap * q[i] + q_new * lap_other[i]
    lpk[...] = slab
    add_source(n, source, start, wavelet, pn)
    got_d, got_u = collect(n, md, mu, oc, oc_out)
    for i in range(NX):
        put_strips(i, pn[i], c[i] * qn[i], xlo, xhi, ylo, yhi)
    ylo[64:72] = got_u
    yhi[64:72] = got_d
    if n == 0:
        cext[0:16] = jnp.where(keep_d, md[64:80], 0.0)
        cext[16:48] = pack([c[i] for i in range(NX)])
        cext[48:64] = jnp.where(keep_u, mu[64:80], 0.0)
        xlo[256:320] = cext[...]
        xhi[256:320] = cext[...]
    if n == 2:
        new = [pn[i] for i in range(NX)]
        slab = pack(new)
        d = lane % SLAB
        deep = (3.0 * C0) * slab
        for k in range(1, W + 1):
            deep = deep + jnp.where(d < SLAB - k, CK[k], 0.0) * roll(slab, -k)
            deep = deep + jnp.where(d >= k, CK[k], 0.0) * roll(slab, k)
        out = jnp.zeros((NY, NZ), f32)
        for i in range(NX):
            for t, row, at in (
                (0, pp[i], REC_DEPTH),
                (1, p[i], REC_DEPTH),
                (2, new[i], REC_DEPTH),
                (3, deep, SLAB * i + REC_DEPTH),
            ):
                out = jnp.where(lane == 4 * i + t, roll(row, 4 * i + t - at), out)
        mat[...] = out
        ylo[72:88] = out[:16]
        yhi[72:88] = out[16:]
    if n == 1:
        xlo[256:288] = mr[272:304]
        xhi[256:288] = ml[272:304]


def final_kernel(
    c, p, q, ql, ml, mr, md, mu, lap0, q3, img, vel, noise, image_in, driven, vpk, zpk,
    own, sent, part, bufp, bufs,
):
    keep_d, keep_u = edges()
    lane = lanes()
    wz = depth_weights()
    first = lax.axis_index("shot") % 2 == 0
    fill(bufp, p, strip(ml, 0), strip(mr, 0), md, mu, 0, keep_d, keep_u)
    s = [c[i] * q[i] for i in range(NX)]
    fill(bufs, s, strip(ml, 128), strip(mr, 128), md, mu, 4, keep_d, keep_u)
    slab = jnp.zeros((NY, NZ), f32)
    for i in range(NX):
        lap = laplace(bufp, i, wz)
        slab = jnp.where(lane // SLAB == i, roll(lap, SLAB * i), slab)
        q_new = 2.0 * q[i] - ql[i] + laplace(bufs, i, wz)
        image = img[i] + lap * q3[i] + q_new * lap0[i]
        grad = (2.0 * courant_sq) * vel[i] * image
        weighted = grad * noise[i]
        own[i] = jnp.where(first, grad, weighted)
        sent[i] = jnp.where(first, weighted, grad)
    grad = (2.0 * courant_sq) * vpk[...] * (image_in[...] + driven[...] * slab)
    part[0:NY] = grad
    part[NY : 2 * NY] = grad * zpk[...]


def chunk_kernel(mat, md, mu, oc, out, traces):
    keep_d, keep_u = edges()
    collect(3, md, mu, oc, traces)
    packed = jnp.where(keep_d, md[72:88], 0.0) + roll(jnp.where(keep_u, mu[72:88], 0.0), 96)
    packed = packed + roll(mat[0:16], 32) + roll(mat[16:32], 64)
    for g in range(out.shape[0]):
        out[g, 0:16] = traces[...]
        out[g, 16:32] = packed


def lap_packed(buf, g, lo, hi, wz):
    lane = lanes()
    here = buf[g, lo:hi]
    before, after = buf[g - 1, lo:hi], buf[g + 1, lo:hi]
    out = (3.0 * C0) * here
    for k in range(1, W + 1):
        t = SLAB * k
        beside = jnp.where(lane < 128 - t, roll(here, -t), roll(after, -t))
        beside = beside + jnp.where(lane >= t, roll(here, t), roll(before, t))
        beside = beside + buf[g, lo + k : hi + k] + buf[g, lo - k : hi - k]
        out = out + CK[k] * beside
        out = out + wz[k][0] * roll(here, -k) + wz[k][1] * roll(here, k)
    return out


def table_kernel(rec, vel, noise, keyx, keyy, count, vpk, zpk, cols, rows, hot, hoty):
    ix, iy, ngy = lax.axis_index("gx"), lax.axis_index("gy"), lax.axis_size("gy")
    half = ngy // 2
    bits = (NY * ngy).bit_length() - 1
    assert 2**bits == NY * ngy
    odd = iy % 2 == 1
    low = lanes() < 64
    bf = jnp.bfloat16
    coly = lax.broadcasted_iota(jnp.int32, (64, 128), 0).astype(f32).astype(bf)
    row4 = (lax.broadcasted_iota(jnp.int32, (128, 128), 0) // 4).astype(f32).astype(bf)
    one, none = jnp.ones((), bf), jnp.zeros((), bf)
    kx = jnp.clip((rec[...] >> bits) - ix * NX + 12, -1, 32).astype(f32)
    ky = jnp.clip((rec[...] & (NY * ngy - 1)) - iy * NY + 16, -1, 64).astype(f32)
    for ref, k in ((rows, kx), (cols, ky)):
        ref[0] = jnp.where(odd, roll(k, 64), k)
    for g in range(rec.shape[0]):
        first = (iy + 2 * (g % half)) % ngy
        a = pl.ds((g // half) * half + first // 2, 1)
        b = pl.ds((g // half) * half + ((first + 1) % ngy) // 2, 1)
        key = jnp.where(low, rows[0, a, :], rows[0, b, :])
        keyx[g : g + 1] = key
        hot[:, 128 * g : 128 * (g + 1)] = jnp.where(row4 == key.astype(bf), one, none)
        key = jnp.where(low, cols[0, a, :], cols[0, b, :])
        keyy[g : g + 1] = key
        hoty[:, 128 * g : 128 * (g + 1)] = jnp.where(coly == key.astype(bf), one, none)
    count[...] = lax.dot_general(
        hot[...], hoty[...], (((1,), (1,)), ((), ())), preferred_element_type=f32
    )
    vpk[...] = pack([vel[i] for i in range(NX)])
    zpk[...] = pack([noise[i] for i in range(NX)])


def last_kernel(
    got, keyx, keyy, count, cext, ml1, mr1, ml2, mr2, lp0, lp1, lp2, image, driven, table, hoty, x, r3, r2, r1, inj,
):
    ngx = got.shape[0]
    lane = lanes()
    ix = lax.axis_index("gx")
    c1l, c1r = ml1.at[256:320], mr1.at[256:320]
    c2l, c2r = ml2.at[256:288], mr2.at[256:288]
    bf = jnp.bfloat16
    row4 = (lax.broadcasted_iota(jnp.int32, (128, 128), 0) // 4).astype(f32).astype(bf)
    coly = lax.broadcasted_iota(jnp.int32, (64, 128), 0).astype(f32).astype(bf)
    one, none = jnp.ones((), bf), jnp.zeros((), bf)

    def build(g, carry):
        for rp in range(4):
            at = pl.ds(pl.multiple_of((4 * g + rp) * 128, 128), 128)
            val = got[g, 4 * rp : 4 * rp + 4, :]
            hi = val.astype(bf).astype(f32)
            mid = (val - hi).astype(bf).astype(f32)
            low = val - hi - mid
            here = row4 == keyx[pl.ds(4 * g + rp, 1), :].astype(bf)
            hoty[:, at] = jnp.where(coly == keyy[pl.ds(4 * g + rp, 1), :].astype(bf), one, none)
            for part, v in enumerate((hi, mid, low)):
                v16 = jnp.concatenate([v, v, v, v], 0).astype(bf)
                v128 = jnp.concatenate([v16] * 8, 0)
                table[128 * part : 128 * (part + 1), at] = jnp.where(here, v128, none)
        at = pl.ds(pl.multiple_of(g * 512, 512), 512)
        return carry + lax.dot_general(
            table[:, at], hoty[:, at], (((1,), (1,)), ((), ())), preferred_element_type=f32
        )

    sums = lax.fori_loop(0, ngx, build, jnp.zeros((384, 64), f32), unroll=ngx)
    seen = sums[0:128] + sums[128:256] + sums[256:384]
    tr = jnp.concatenate([seen, count[...]], 1).T

    k_in = lax.broadcasted_iota(jnp.int32, (128, 512), 0)
    k_out = lax.broadcasted_iota(jnp.int32, (128, 512), 1)
    spread_to = jnp.where(
        (k_in < 32) & (k_out == (k_in % 4) * 128 + (k_in // 4) * SLAB + REC_DEPTH), 1.0, 0.0
    )
    dense, raw = [], []
    for g in range(5):
        src = ix + (g - 2)
        ok = (src >= 0) & (src < ngx)
        blk = got[jnp.clip(src, 0, ngx - 1), 16:32, :]
        m = jnp.concatenate([roll(blk, -32 * t) for t in range(4)], 0)
        m = jnp.where(ok, m, 0.0)
        s_g = roll(tr[:64], 16 - 32 * g)
        n_g = roll(tr[64:], 16 - 32 * g)
        dense.append(jnp.where(lane % 4 == 3, 0.0, n_g * m) - s_g)
        raw.append(jnp.where(lane % 4 == 0, n_g, m))
    inj[...] = jnp.dot(
        jnp.concatenate(dense + raw, 0), spread_to,
        precision=lax.Precision.HIGHEST, preferred_element_type=f32,
    )

    def j(n, g, lo, hi):
        return inj[64 * g + lo : 64 * g + hi, 128 * n : 128 * (n + 1)]

    coef = {1: c1l, 2: cext, 3: c1r}
    pad = jnp.zeros((16, 128), f32)
    plane = [j(2, 5 + g, 0, 64) for g in range(5)]
    for g in range(5):
        x[g] = plane[g]
    for g in range(5):
        lo, hi = (16, 48) if g in (0, 4) else (4, 60)
        part = j(3, 5 + g, lo, hi)
        for k in range(1, W + 1):
            t = SLAB * k
            here = x[g, lo:hi]
            after = x[g + 1, lo:hi] if g < 4 else jnp.zeros_like(here)
            before = x[g - 1, lo:hi] if g > 0 else jnp.zeros_like(here)
            beside = jnp.where(lane < 128 - t, roll(here, -t), roll(after, -t))
            beside = beside + jnp.where(lane >= t, roll(here, t), roll(before, t))
            beside = beside + x[g, lo + k : hi + k] + x[g, lo - k : hi - k]
            part = part + CK[k] * jnp.where(lane % SLAB == REC_DEPTH, beside, 0.0)
        c_g = (c2l, c2r)[g // 4][...] if g in (0, 4) else coef[g][lo:hi]
        p4 = 2.0 * x[g, lo:hi] - j(1, 5 + g, lo, hi) + c_g * part
        r3[g] = j(3, g, 0, 64)
        r3[g, lo:hi] = r3[g, lo:hi] + j(0, 5 + g, lo, hi) * p4

    d = lane % SLAB
    wz = [None] + [
        (jnp.where(d < SLAB - k, CK[k], 0.0), jnp.where(d >= k, CK[k], 0.0))
        for k in range(1, W + 1)
    ]
    for g in coef:
        x[g] = coef[g][...] * r3[g]
    for g, far in ((0, c2l), (4, c2r)):
        x[g, 0:16] = pad
        x[g, 16:48] = far[...] * r3[g, 16:48]
        x[g, 48:64] = pad
    for g in (1, 2, 3):
        r2[g] = 2.0 * r3[g, 8:56] + lap_packed(x, g, 8, 56, wz) + j(2, g, 8, 56)
    x[0] = jnp.zeros((64, 128), f32)
    x[4] = jnp.zeros((64, 128), f32)
    for g in (1, 2, 3):
        x[g, 0:8] = pad[:8]
        x[g, 8:56] = coef[g][8:56] * r2[g]
        x[g, 56:64] = pad[:8]
    for g in (1, 2, 3):
        r1[g] = 2.0 * r2[g] - r3[g, 8:56] + lap_packed(x, g, 8, 56, wz) + j(1, g, 8, 56)
    for g in (1, 2, 3):
        x[g, 8:56] = coef[g][8:56] * r1[g]
    r0 = 2.0 * r1[2, 8:40] - r2[2, 8:40] + lap_packed(x, 2, 16, 48, wz) + j(0, 2, 16, 48)
    image[...] = r0 * lp0[...] + r1[2, 8:40] * lp1[...] + r2[2, 8:40] * lp2[...]
    driven[...] = r3[2, 16:48]


def tail_kernel(own, other, part, out):
    cells = NX * NY
    for i in range(NX):
        out[NY * i : NY * (i + 1)] = own[i] + other[i]
    out[cells : cells + 2 * NY] = part[...]


def sum_kernel(every, logs, grad_mean, grad_logs):
    lane = lanes()
    cells = NX * NY

    def packed(at):
        rows = slice(at, at + NY)
        return (every[0, rows] + every[1, rows]) + (every[2, rows] + every[3, rows])

    grad_in, weighted_in = packed(cells), packed(cells + NY)
    for i in range(NX):
        rows = slice(NY * i, NY * (i + 1))
        grad = every[0, rows] + every[2, rows]
        grad_mean[i] = grad + jnp.where(lane < SLAB, roll(grad_in, -SLAB * i), 0.0)
        weighted = every[1, rows] + every[3, rows]
        weighted = weighted + jnp.where(lane < SLAB, roll(weighted_in, -SLAB * i), 0.0)
        spread = jnp.exp(logs[i])
        grad_logs[i] = spread * weighted + jnp.exp(2.0 * logs[i]) / prior_var - 1.0


def call(kernel, outs, scratch=(), smem=0, mib=4):
    def go(*args):
        return pl.pallas_call(
            kernel,
            out_shape=outs,
            in_specs=[SM] * smem + [VM] * (len(args) - smem),
            out_specs=jax.tree.map(lambda _: VM, outs),
            scratch_shapes=list(scratch),
            compiler_params=pltpu.CompilerParams(vmem_limit_bytes=mib * 2**20),
        )(*args)

    return go


def shift(x, axis, k, wrap=False):
    n = lax.axis_size(axis)
    return lax.ppermute(x, axis, [(i, (i + k) % n) for i in range(n) if wrap or 0 <= i + k < n])


def local(
    mean_velocity,
    log_scale,
    shot_noise,
    checkpoint_prev,
    checkpoint_now,
    adjoint_next,
    adjoint_now,
    wavelet,
    source_column,
    receiver_column,
    observed,
    start_step,
):
    ngx, ngy, nshot = lax.axis_size("gx"), lax.axis_size("gy"), lax.axis_size("shot")
    noise = shot_noise[0]
    p_prev, p = checkpoint_prev[0], checkpoint_now[0]
    q_later, q = adjoint_next[0], adjoint_now[0]
    F = sds(NX, NY, NZ)
    vel = mean_velocity + jnp.exp(log_scale) * noise
    coef = courant_sq * vel * vel
    xlo, xhi, ylo, yhi, oc = call(
        first_kernel,
        (sds(256, 128), sds(256, 128), sds(88, 128), sds(88, 128), sds(16, 128)),
    )(coef, coef * q, p, observed[0])
    buf = pltpu.VMEM((NX + 2 * W, 48, NZ), f32)
    slabs, keep = [], {}
    for n in range(STEPS):
        ml, mr = shift(xhi, "gx", 1), shift(xlo, "gx", -1)
        md, mu = shift(yhi, "gy", 1, True), shift(ylo, "gy", -1, True)
        halos = (ml, mr, md, mu)
        if n == STEPS - 1:
            break
        extra = {1: (keep.get("cext"),), 2: (keep.get("lap1"),)}.get(n, ())
        rows = (320, 288, 256)[n]
        outs = [sds(NY, NZ), sds(16, 128), F, F]
        cols = (72, 72, 88)[n]
        outs += [sds(rows, 128), sds(rows, 128), sds(cols, 128), sds(cols, 128), F]
        if n != 1:
            outs.append(sds(64, 128) if n == 0 else sds(NY, NZ))
        res = call(functools.partial(step_kernel, n), tuple(outs), (buf, buf), smem=3)(
            source_column, start_step, wavelet, coef, p, p_prev, q, q_later, *halos, oc, *extra
        )
        lpk, oc, q_next, p_next, xlo, xhi, ylo, yhi = res[:8]
        slabs.append(lpk)
        if n == 0:
            keep["lap0"], keep["cext"], keep["q3"] = res[8], res[9], q_next
        if n == 1:
            keep["lap1"], keep["c"] = res[8], [ml, mr]
        if n == 2:
            img, mat = res[8], res[9]
            keep["c"] += [ml, mr]
        p_prev, p = p, p_next
        q_later, q = q, q_next

    chunk = call(chunk_kernel, sds(ngx, 32, 128), (pltpu.VMEM((16, 128), f32),))(mat, md, mu, oc)
    got = lax.all_to_all(chunk, "gx", 0, 0)
    nrec = receiver_column.shape[1]
    bf = jnp.bfloat16
    keyx, keyy, count, vpk, zpk = call(
        table_kernel,
        (
            sds(nrec // 128, 128),
            sds(nrec // 128, 128),
            sds(128, 64),
            sds(NY, NZ),
            sds(NY, NZ),
        ),
        [pltpu.VMEM((1, nrec // 128, 128), f32)] * 2
        + [pltpu.VMEM((128, nrec), bf), pltpu.VMEM((64, nrec), bf)],
        mib=12,
    )(receiver_column.reshape(-1, 128), vel, noise)
    g5 = pltpu.VMEM((5, 64, 128), f32)
    g48 = pltpu.VMEM((5, 48, 128), f32)
    image_in, driven = call(
        last_kernel,
        (sds(NY, NZ), sds(NY, NZ)),
        (pltpu.VMEM((384, nrec), bf), pltpu.VMEM((64, nrec), bf), g5, g5, g48, g48, pltpu.VMEM((640, 512), f32)),
        mib=24,
    )(got, keyx, keyy, count, keep["cext"], *keep["c"], *slabs)
    own, sent, part = call(final_kernel, (F, F, sds(2 * NY, NZ)), (buf, buf))(
        coef, p, q, q_later, *halos, keep["lap0"], keep["q3"], img, vel, noise,
        image_in, driven, vpk, zpk,
    )
    other = lax.ppermute(sent, "shot", [(i, i ^ 1) for i in range(nshot)])
    part = call(tail_kernel, sds(NX * NY + 2 * NY, NZ))(own, other, part)
    every = lax.all_gather(part, "shot", axis=0)
    return call(sum_kernel, (F, F))(every, log_scale)


def solution(mesh):
    return jax.shard_map(
        local,
        mesh=mesh,
        in_specs=(
            P("gx", "gy", None),
            P("gx", "gy", None),
            P("shot", "gx", "gy", None),
            P("shot", "gx", "gy", None),
            P("shot", "gx", "gy", None),
            P("shot", "gx", "gy", None),
            P("shot", "gx", "gy", None),
            P("shot", None),
            P("shot"),
            P("shot", None),
            P("shot", None, ("gx", "gy")),
            P(),
        ),
        out_specs=(P("gx", "gy", None), P("gx", "gy", None)),
        check_vma=False,
    )
```

```python
import functools

import jax
import jax.numpy as jnp
from jax import lax
from jax.experimental import pallas as pl
from jax.experimental.pallas import tpu as pltpu
from jax.sharding import PartitionSpec as P

STEPS = 4
SRC_DEPTH = 6
REC_DEPTH = 3
NX, NY, NZ = 8, 32, 128
W = 4
SLAB = 16

C0, C1, C2, C3, C4 = (-205.0 / 72.0, 8.0 / 5.0, -1.0 / 5.0, 8.0 / 315.0, -1.0 / 560.0)
CK = (C0, C1, C2, C3, C4)
courant_sq = 0.0625
prior_var = 0.01

f32 = jnp.float32
VM = pl.BlockSpec(memory_space=pltpu.VMEM)
SM = pl.BlockSpec(memory_space=pltpu.SMEM)


def sds(*shape):
    return jax.ShapeDtypeStruct(shape, f32)


def lanes(rows=1):
    return lax.broadcasted_iota(jnp.int32, (rows, 128), 1)


def roll(x, k):
    k = k % 128
    return x if k == 0 else pltpu.roll(x, k, 1)


def pack(rows):
    part = lanes() // SLAB
    out = jnp.where(part == 0, rows[0], 0.0)
    for x in range(1, NX):
        out = jnp.where(part == x, roll(rows[x], SLAB * x), out)
    return out


def put_strips(i, p, s, xlo, xhi, ylo, yhi):
    out, j = (xlo, i) if i < W else (xhi, i - W)
    out[NY * j : NY * (j + 1)] = p
    out[NY * (W + j) : NY * (W + j + 1)] = s
    ylo[8 * i : 8 * i + 4] = p[:W]
    ylo[8 * i + 4 : 8 * i + 8] = s[:W]
    yhi[8 * i : 8 * i + 4] = p[NY - W :]
    yhi[8 * i + 4 : 8 * i + 8] = s[NY - W :]


def first_kernel(c, s, p, obs, xlo, xhi, ylo, yhi, oc):
    oc[...] = jnp.zeros((16, 128), f32)
    oc[0:4, 0:64] = obs[...]
    for y in (ylo, yhi):
        y[80:88] = jnp.zeros((8, 128), f32)
        y[80:84, 0:64] = obs[...]
    for i in range(NX):
        put_strips(i, p[i], s[i], xlo, xhi, ylo, yhi)
    slab = pack([c[i] for i in range(NX)])
    ylo[64:80] = slab[:16]
    yhi[64:80] = slab[16:]


def fill(buf, field, rows_l, rows_r, md, mu, at, keep_d, keep_u):
    for i in range(NX):
        buf[W + i, 8:40] = field[i]
        buf[W + i, 4:8] = jnp.where(keep_d, md[8 * i + at : 8 * i + at + 4], 0.0)
        buf[W + i, 40:44] = jnp.where(keep_u, mu[8 * i + at : 8 * i + at + 4], 0.0)
    for j in range(W):
        buf[j, 8:40] = rows_l[j]
        buf[W + NX + j, 8:40] = rows_r[j]


def laplace(buf, i, wz):
    here = buf[W + i, 8:40]
    out = (3.0 * C0) * here
    for k in range(1, W + 1):
        beside = buf[W + i + k, 8:40] + buf[W + i - k, 8:40]
        beside = beside + buf[W + i, 8 + k : 40 + k] + buf[W + i, 8 - k : 40 - k]
        out = out + CK[k] * beside
        out = out + wz[k][0] * roll(here, -k) + wz[k][1] * roll(here, k)
    return out


def depth_weights():
    lane = lanes()
    return [None] + [
        (jnp.where(lane < NZ - k, CK[k], 0.0), jnp.where(lane >= k, CK[k], 0.0))
        for k in range(1, W + 1)
    ]


def edges():
    iy = lax.axis_index("gy")
    return iy > 0, iy < lax.axis_size("gy") - 1


def strip(m, at):
    return [m[at + NY * j : at + NY * (j + 1)] for j in range(W)]


def add_source(n, source, start, wavelet, field):
    width = NY * lax.axis_size("gy")
    sx = source[0] // width - lax.axis_index("gx") * NX
    sy = source[0] % width - lax.axis_index("gy") * NY

    @pl.when((sx >= 0) & (sx < NX) & (sy >= 0) & (sy < NY))
    def _():
        row = field[sx, pl.ds(sy, 1), :]
        add = jnp.where(lanes() == SRC_DEPTH, wavelet[0, start[0] + n], 0.0)
        field[sx, pl.ds(sy, 1), :] = row + add


def collect(n, md, mu, oc, oc_out):
    at = 80 if n == 0 else 64
    got_d, got_u = md[at : at + 8], mu[at : at + 8]
    oc_out[...] = oc[...]
    up, turn_u, down, turn_d = ((0, 64, 12, 64), (4, 0, 12, 0), (4, 64, 8, 64), (8, 0, None, 0))[n]
    oc_out[up : up + 4] = oc_out[up : up + 4] + roll(got_u, turn_u)[:4]
    if down is not None:
        oc_out[down : down + 4] = oc_out[down : down + 4] + roll(got_d, turn_d)[:4]
    return got_d, got_u


def step_kernel(n, source, start, wavelet, c, p, pp, q, ql, ml, mr, md, mu, oc, *rest):
    if n == 0:
        lpk, oc_out, qn, pn, xlo, xhi, ylo, yhi, lap_out, cext, bufp, bufs = rest
    if n == 1:
        cext, lpk, oc_out, qn, pn, xlo, xhi, ylo, yhi, lap_out, bufp, bufs = rest
    if n == 2:
        lap_other, lpk, oc_out, qn, pn, xlo, xhi, ylo, yhi, img_out, mat, bufp, bufs = rest
    keep_d, keep_u = edges()
    lane = lanes()
    wz = depth_weights()
    fill(bufp, p, strip(ml, 0), strip(mr, 0), md, mu, 0, keep_d, keep_u)
    s = [c[i] * q[i] for i in range(NX)]
    fill(bufs, s, strip(ml, 128), strip(mr, 128), md, mu, 4, keep_d, keep_u)
    slab = jnp.zeros((NY, NZ), f32)
    for i in range(NX):
        lap = laplace(bufp, i, wz)
        slab = jnp.where(lane // SLAB == i, roll(lap, SLAB * i), slab)
        pn[i] = 2.0 * p[i] - pp[i] + c[i] * lap
        q_new = 2.0 * q[i] - ql[i] + laplace(bufs, i, wz)
        qn[i] = q_new
        if n < 2:
            lap_out[i] = lap
        else:
            img_out[i] = lap * q[i] + q_new * lap_other[i]
    lpk[...] = slab
    add_source(n, source, start, wavelet, pn)
    got_d, got_u = collect(n, md, mu, oc, oc_out)
    for i in range(NX):
        put_strips(i, pn[i], c[i] * qn[i], xlo, xhi, ylo, yhi)
    ylo[64:72] = got_u
    yhi[64:72] = got_d
    if n == 0:
        cext[0:16] = jnp.where(keep_d, md[64:80], 0.0)
        cext[16:48] = pack([c[i] for i in range(NX)])
        cext[48:64] = jnp.where(keep_u, mu[64:80], 0.0)
        xlo[256:320] = cext[...]
        xhi[256:320] = cext[...]
    if n == 2:
        new = [pn[i] for i in range(NX)]
        slab = pack(new)
        d = lane % SLAB
        deep = (3.0 * C0) * slab
        for k in range(1, W + 1):
            deep = deep + jnp.where(d < SLAB - k, CK[k], 0.0) * roll(slab, -k)
            deep = deep + jnp.where(d >= k, CK[k], 0.0) * roll(slab, k)
        out = jnp.zeros((NY, NZ), f32)
        for i in range(NX):
            for t, row, at in (
                (0, pp[i], REC_DEPTH),
                (1, p[i], REC_DEPTH),
                (2, new[i], REC_DEPTH),
                (3, deep, SLAB * i + REC_DEPTH),
            ):
                out = jnp.where(lane == 4 * i + t, roll(row, 4 * i + t - at), out)
        mat[...] = out
        ylo[72:88] = out[:16]
        yhi[72:88] = out[16:]
    if n == 1:
        xlo[256:288] = mr[272:304]
        xhi[256:288] = ml[272:304]


def final_kernel(
    c, p, q, ql, ml, mr, md, mu, lap0, q3, img, vel, noise, image_in, driven, vpk, zpk,
    own, sent, part, bufp, bufs,
):
    keep_d, keep_u = edges()
    lane = lanes()
    wz = depth_weights()
    first = lax.axis_index("shot") % 2 == 0
    fill(bufp, p, strip(ml, 0), strip(mr, 0), md, mu, 0, keep_d, keep_u)
    s = [c[i] * q[i] for i in range(NX)]
    fill(bufs, s, strip(ml, 128), strip(mr, 128), md, mu, 4, keep_d, keep_u)
    slab = jnp.zeros((NY, NZ), f32)
    for i in range(NX):
        lap = laplace(bufp, i, wz)
        slab = jnp.where(lane // SLAB == i, roll(lap, SLAB * i), slab)
        q_new = 2.0 * q[i] - ql[i] + laplace(bufs, i, wz)
        image = img[i] + lap * q3[i] + q_new * lap0[i]
        grad = (2.0 * courant_sq) * vel[i] * image
        weighted = grad * noise[i]
        own[i] = jnp.where(first, grad, weighted)
        sent[i] = jnp.where(first, weighted, grad)
    grad = (2.0 * courant_sq) * vpk[...] * (image_in[...] + driven[...] * slab)
    part[0:NY] = grad
    part[NY : 2 * NY] = grad * zpk[...]


def chunk_kernel(mat, md, mu, oc, _, out, traces):
    keep_d, keep_u = edges()
    collect(3, md, mu, oc, traces)
    packed = jnp.where(keep_d, md[72:88], 0.0) + roll(jnp.where(keep_u, mu[72:88], 0.0), 96)
    packed = packed + roll(mat[0:16], 32) + roll(mat[16:32], 64)
    for g in range(out.shape[0]):
        out[g, 0:16] = traces[...]
        out[g, 16:32] = packed


def lap_packed(buf, g, lo, hi, wz):
    lane = lanes()
    here = buf[g, lo:hi]
    before, after = buf[g - 1, lo:hi], buf[g + 1, lo:hi]
    out = (3.0 * C0) * here
    for k in range(1, W + 1):
        t = SLAB * k
        beside = jnp.where(lane < 128 - t, roll(here, -t), roll(after, -t))
        beside = beside + jnp.where(lane >= t, roll(here, t), roll(before, t))
        beside = beside + buf[g, lo + k : hi + k] + buf[g, lo - k : hi - k]
        out = out + CK[k] * beside
        out = out + wz[k][0] * roll(here, -k) + wz[k][1] * roll(here, k)
    return out


def table_kernel(rec, vel, noise, keyx, keyy, count, vpk, zpk, cols, rows, hot, hoty):
    ix, iy, ngy = lax.axis_index("gx"), lax.axis_index("gy"), lax.axis_size("gy")
    half = ngy // 2
    bits = (NY * ngy).bit_length() - 1
    assert 2**bits == NY * ngy
    odd = iy % 2 == 1
    low = lanes() < 64
    bf = jnp.bfloat16
    coly = lax.broadcasted_iota(jnp.int32, (64, 128), 0).astype(f32).astype(bf)
    row4 = (lax.broadcasted_iota(jnp.int32, (128, 128), 0) // 4).astype(f32).astype(bf)
    one, none = jnp.ones((), bf), jnp.zeros((), bf)
    kx = jnp.clip((rec[...] >> bits) - ix * NX + 12, -1, 32).astype(f32)
    ky = jnp.clip((rec[...] & (NY * ngy - 1)) - iy * NY + 16, -1, 64).astype(f32)
    for ref, k in ((rows, kx), (cols, ky)):
        ref[0] = jnp.where(odd, roll(k, 64), k)
    for g in range(rec.shape[0]):
        first = (iy + 2 * (g % half)) % ngy
        a = pl.ds((g // half) * half + first // 2, 1)
        b = pl.ds((g // half) * half + ((first + 1) % ngy) // 2, 1)
        key = jnp.where(low, rows[0, a, :], rows[0, b, :])
        keyx[g : g + 1] = key
        hot[:, 128 * g : 128 * (g + 1)] = jnp.where(row4 == key.astype(bf), one, none)
        key = jnp.where(low, cols[0, a, :], cols[0, b, :])
        keyy[g : g + 1] = key
        hoty[:, 128 * g : 128 * (g + 1)] = jnp.where(coly == key.astype(bf), one, none)
    count[...] = lax.dot_general(
        hoty[...], hot[...], (((1,), (1,)), ((), ())), preferred_element_type=f32
    )
    vpk[...] = pack([vel[i] for i in range(NX)])
    zpk[...] = pack([noise[i] for i in range(NX)])


def last_kernel(
    got, keyx, keyy, count, cext, ml1, mr1, ml2, mr2, lp0, lp1, lp2, image, driven, table, hoty, x, r3, r2, r1, inj,
):
    ngx = got.shape[0]
    lane = lanes()
    ix = lax.axis_index("gx")
    c1l, c1r = ml1.at[256:320], mr1.at[256:320]
    c2l, c2r = ml2.at[256:288], mr2.at[256:288]
    bf = jnp.bfloat16
    row4 = (lax.broadcasted_iota(jnp.int32, (128, 128), 0) // 4).astype(f32).astype(bf)
    coly = lax.broadcasted_iota(jnp.int32, (64, 128), 0).astype(f32).astype(bf)
    one, none = jnp.ones((), bf), jnp.zeros((), bf)

    def build(g, carry):
        for rp in range(4):
            at = pl.ds(pl.multiple_of((4 * g + rp) * 128, 128), 128)
            val = got[g, 4 * rp : 4 * rp + 4, :]
            hi = val.astype(bf).astype(f32)
            mid = (val - hi).astype(bf).astype(f32)
            low = val - hi - mid
            here = row4 == keyx[pl.ds(4 * g + rp, 1), :].astype(bf)
            hoty[:, at] = jnp.where(coly == keyy[pl.ds(4 * g + rp, 1), :].astype(bf), one, none)
            for part, v in enumerate((hi, mid, low)):
                v16 = jnp.concatenate([v, v, v, v], 0).astype(bf)
                v128 = jnp.concatenate([v16] * 8, 0)
                table[128 * part : 128 * (part + 1), at] = jnp.where(here, v128, none)
        at = pl.ds(pl.multiple_of(g * 512, 512), 512)
        return carry + lax.dot_general(
            hoty[:, at], table[:, at], (((1,), (1,)), ((), ())), preferred_element_type=f32
        )

    sums = lax.fori_loop(0, ngx, build, jnp.zeros((64, 384), f32), unroll=ngx)
    seen = sums[:, 0:128] + sums[:, 128:256] + sums[:, 256:384]
    counts = count[...]

    k_in = lax.broadcasted_iota(jnp.int32, (128, 512), 0)
    k_out = lax.broadcasted_iota(jnp.int32, (128, 512), 1)
    spread_to = jnp.where(
        (k_in < 32) & (k_out == (k_in % 4) * 128 + (k_in // 4) * SLAB + REC_DEPTH), 1.0, 0.0
    )
    dense, raw = [], []
    for g in range(5):
        src = ix + (g - 2)
        ok = (src >= 0) & (src < ngx)
        blk = got[jnp.clip(src, 0, ngx - 1), 16:32, :]
        m = jnp.concatenate([roll(blk, -32 * t) for t in range(4)], 0)
        m = jnp.where(ok, m, 0.0)
        s_g = roll(seen, 16 - 32 * g)
        n_g = roll(counts, 16 - 32 * g)
        dense.append(jnp.where(lane % 4 == 3, 0.0, n_g * m) - s_g)
        raw.append(jnp.where(lane % 4 == 0, n_g, m))
    inj[...] = jnp.dot(
        jnp.concatenate(dense + raw, 0), spread_to,
        precision=lax.Precision.HIGHEST, preferred_element_type=f32,
    )

    def j(n, g, lo, hi):
        return inj[64 * g + lo : 64 * g + hi, 128 * n : 128 * (n + 1)]

    coef = {1: c1l, 2: cext, 3: c1r}
    pad = jnp.zeros((16, 128), f32)
    plane = [j(2, 5 + g, 0, 64) for g in range(5)]
    for g in range(5):
        x[g] = plane[g]
    for g in range(5):
        lo, hi = (16, 48) if g in (0, 4) else (4, 60)
        part = j(3, 5 + g, lo, hi)
        for k in range(1, W + 1):
            t = SLAB * k
            here = x[g, lo:hi]
            after = x[g + 1, lo:hi] if g < 4 else jnp.zeros_like(here)
            before = x[g - 1, lo:hi] if g > 0 else jnp.zeros_like(here)
            beside = jnp.where(lane < 128 - t, roll(here, -t), roll(after, -t))
            beside = beside + jnp.where(lane >= t, roll(here, t), roll(before, t))
            beside = beside + x[g, lo + k : hi + k] + x[g, lo - k : hi - k]
            part = part + CK[k] * jnp.where(lane % SLAB == REC_DEPTH, beside, 0.0)
        c_g = (c2l, c2r)[g // 4][...] if g in (0, 4) else coef[g][lo:hi]
        p4 = 2.0 * x[g, lo:hi] - j(1, 5 + g, lo, hi) + c_g * part
        r3[g] = j(3, g, 0, 64)
        r3[g, lo:hi] = r3[g, lo:hi] + j(0, 5 + g, lo, hi) * p4

    d = lane % SLAB
    wz = [None] + [
        (jnp.where(d < SLAB - k, CK[k], 0.0), jnp.where(d >= k, CK[k], 0.0))
        for k in range(1, W + 1)
    ]
    for g in coef:
        x[g] = coef[g][...] * r3[g]
    for g, far in ((0, c2l), (4, c2r)):
        x[g, 0:16] = pad
        x[g, 16:48] = far[...] * r3[g, 16:48]
        x[g, 48:64] = pad
    for g in (1, 2, 3):
        r2[g] = 2.0 * r3[g, 8:56] + lap_packed(x, g, 8, 56, wz) + j(2, g, 8, 56)
    x[0] = jnp.zeros((64, 128), f32)
    x[4] = jnp.zeros((64, 128), f32)
    for g in (1, 2, 3):
        x[g, 0:8] = pad[:8]
        x[g, 8:56] = coef[g][8:56] * r2[g]
        x[g, 56:64] = pad[:8]
    for g in (1, 2, 3):
        r1[g] = 2.0 * r2[g] - r3[g, 8:56] + lap_packed(x, g, 8, 56, wz) + j(1, g, 8, 56)
    for g in (1, 2, 3):
        x[g, 8:56] = coef[g][8:56] * r1[g]
    r0 = 2.0 * r1[2, 8:40] - r2[2, 8:40] + lap_packed(x, 2, 16, 48, wz) + j(0, 2, 16, 48)
    image[...] = r0 * lp0[...] + r1[2, 8:40] * lp1[...] + r2[2, 8:40] * lp2[...]
    driven[...] = r3[2, 16:48]


def tail_kernel(own, other, part, out):
    cells = NX * NY
    for i in range(NX):
        out[NY * i : NY * (i + 1)] = own[i] + other[i]
    out[cells : cells + 2 * NY] = part[...]


def sum_kernel(every, logs, grad_mean, grad_logs):
    lane = lanes()
    cells = NX * NY

    def packed(at):
        rows = slice(at, at + NY)
        return (every[0, rows] + every[1, rows]) + (every[2, rows] + every[3, rows])

    grad_in, weighted_in = packed(cells), packed(cells + NY)
    for i in range(NX):
        rows = slice(NY * i, NY * (i + 1))
        grad = every[0, rows] + every[2, rows]
        grad_mean[i] = grad + jnp.where(lane < SLAB, roll(grad_in, -SLAB * i), 0.0)
        weighted = every[1, rows] + every[3, rows]
        weighted = weighted + jnp.where(lane < SLAB, roll(weighted_in, -SLAB * i), 0.0)
        spread = jnp.exp(logs[i])
        grad_logs[i] = spread * weighted + jnp.exp(2.0 * logs[i]) / prior_var - 1.0


def call(kernel, outs, scratch=(), smem=0, mib=4):
    def go(*args):
        return pl.pallas_call(
            kernel,
            out_shape=outs,
            in_specs=[SM] * smem + [VM] * (len(args) - smem),
            out_specs=jax.tree.map(lambda _: VM, outs),
            scratch_shapes=list(scratch),
            compiler_params=pltpu.CompilerParams(vmem_limit_bytes=mib * 2**20),
        )(*args)

    return go


def shift(x, axis, k, wrap=False):
    n = lax.axis_size(axis)
    return lax.ppermute(x, axis, [(i, (i + k) % n) for i in range(n) if wrap or 0 <= i + k < n])


def local(
    mean_velocity,
    log_scale,
    shot_noise,
    checkpoint_prev,
    checkpoint_now,
    adjoint_next,
    adjoint_now,
    wavelet,
    source_column,
    receiver_column,
    observed,
    start_step,
):
    ngx, ngy, nshot = lax.axis_size("gx"), lax.axis_size("gy"), lax.axis_size("shot")
    noise = shot_noise[0]
    p_prev, p = checkpoint_prev[0], checkpoint_now[0]
    q_later, q = adjoint_next[0], adjoint_now[0]
    F = sds(NX, NY, NZ)
    vel = mean_velocity + jnp.exp(log_scale) * noise
    coef = courant_sq * vel * vel
    xlo, xhi, ylo, yhi, oc = call(
        first_kernel,
        (sds(256, 128), sds(256, 128), sds(88, 128), sds(88, 128), sds(16, 128)),
    )(coef, coef * q, p, observed[0])
    buf = pltpu.VMEM((NX + 2 * W, 48, NZ), f32)
    slabs, keep = [], {}
    for n in range(STEPS):
        ml, mr = shift(xhi, "gx", 1), shift(xlo, "gx", -1)
        md, mu = shift(yhi, "gy", 1, True), shift(ylo, "gy", -1, True)
        halos = (ml, mr, md, mu)
        if n == STEPS - 1:
            break
        extra = {1: (keep.get("cext"),), 2: (keep.get("lap1"),)}.get(n, ())
        rows = (320, 288, 256)[n]
        outs = [sds(NY, NZ), sds(16, 128), F, F]
        cols = (72, 72, 88)[n]
        outs += [sds(rows, 128), sds(rows, 128), sds(cols, 128), sds(cols, 128), F]
        if n != 1:
            outs.append(sds(64, 128) if n == 0 else sds(NY, NZ))
        res = call(functools.partial(step_kernel, n), tuple(outs), (buf, buf), smem=3)(
            source_column, start_step, wavelet, coef, p, p_prev, q, q_later, *halos, oc, *extra
        )
        lpk, oc, q_next, p_next, xlo, xhi, ylo, yhi = res[:8]
        slabs.append(lpk)
        if n == 0:
            keep["lap0"], keep["cext"], keep["q3"] = res[8], res[9], q_next
        if n == 1:
            keep["lap1"], keep["c"] = res[8], [ml, mr]
        if n == 2:
            img, mat = res[8], res[9]
            keep["c"] += [ml, mr]
        p_prev, p = p, p_next
        q_later, q = q, q_next

    nrec = receiver_column.shape[1]
    bf = jnp.bfloat16
    keyx, keyy, count, vpk, zpk = call(
        table_kernel,
        (
            sds(nrec // 128, 128),
            sds(nrec // 128, 128),
            sds(64, 128),
            sds(NY, NZ),
            sds(NY, NZ),
        ),
        [pltpu.VMEM((1, nrec // 128, 128), f32)] * 2
        + [pltpu.VMEM((128, nrec), bf), pltpu.VMEM((64, nrec), bf)],
        mib=12,
    )(receiver_column.reshape(-1, 128), vel, noise)
    chunk = call(chunk_kernel, sds(ngx, 32, 128), (pltpu.VMEM((16, 128), f32),))(
        mat, md, mu, oc, count
    )
    got = lax.all_to_all(chunk, "gx", 0, 0)
    g5 = pltpu.VMEM((5, 64, 128), f32)
    g48 = pltpu.VMEM((5, 48, 128), f32)
    image_in, driven = call(
        last_kernel,
        (sds(NY, NZ), sds(NY, NZ)),
        (pltpu.VMEM((384, nrec), bf), pltpu.VMEM((64, nrec), bf), g5, g5, g48, g48, pltpu.VMEM((640, 512), f32)),
        mib=24,
    )(got, keyx, keyy, count, keep["cext"], *keep["c"], *slabs)
    own, sent, part = call(final_kernel, (F, F, sds(2 * NY, NZ)), (buf, buf))(
        coef, p, q, q_later, *halos, keep["lap0"], keep["q3"], img, vel, noise,
        image_in, driven, vpk, zpk,
    )
    other = lax.ppermute(sent, "shot", [(i, i ^ 1) for i in range(nshot)])
    part = call(tail_kernel, sds(NX * NY + 2 * NY, NZ))(own, other, part)
    every = lax.all_gather(part, "shot", axis=0)
    return call(sum_kernel, (F, F))(every, log_scale)


def solution(mesh):
    return jax.shard_map(
        local,
        mesh=mesh,
        in_specs=(
            P("gx", "gy", None),
            P("gx", "gy", None),
            P("shot", "gx", "gy", None),
            P("shot", "gx", "gy", None),
            P("shot", "gx", "gy", None),
            P("shot", "gx", "gy", None),
            P("shot", "gx", "gy", None),
            P("shot", None),
            P("shot"),
            P("shot", None),
            P("shot", None, ("gx", "gy")),
            P(),
        ),
        out_specs=(P("gx", "gy", None), P("gx", "gy", None)),
        check_vma=False,
    )
```

```python
import functools

import jax
import jax.numpy as jnp
from jax import lax
from jax.experimental import pallas as pl
from jax.experimental.pallas import tpu as pltpu
from jax.sharding import PartitionSpec as P

STEPS = 4
SRC_DEPTH = 6
REC_DEPTH = 3
NX, NY, NZ = 8, 32, 128
W = 4
SLAB = 16

C0, C1, C2, C3, C4 = (-205.0 / 72.0, 8.0 / 5.0, -1.0 / 5.0, 8.0 / 315.0, -1.0 / 560.0)
CK = (C0, C1, C2, C3, C4)
courant_sq = 0.0625
prior_var = 0.01

f32 = jnp.float32
VM = pl.BlockSpec(memory_space=pltpu.VMEM)
SM = pl.BlockSpec(memory_space=pltpu.SMEM)


def sds(*shape):
    return jax.ShapeDtypeStruct(shape, f32)


def lanes(rows=1):
    return lax.broadcasted_iota(jnp.int32, (rows, 128), 1)


def roll(x, k):
    k = k % 128
    return x if k == 0 else pltpu.roll(x, k, 1)


def pack(rows):
    part = lanes() // SLAB
    out = jnp.where(part == 0, rows[0], 0.0)
    for x in range(1, NX):
        out = jnp.where(part == x, roll(rows[x], SLAB * x), out)
    return out


def put_strips(i, p, s, xlo, xhi, ylo, yhi):
    out, j = (xlo, i) if i < W else (xhi, i - W)
    out[NY * j : NY * (j + 1)] = p
    out[NY * (W + j) : NY * (W + j + 1)] = s
    ylo[8 * i : 8 * i + 4] = p[:W]
    ylo[8 * i + 4 : 8 * i + 8] = s[:W]
    yhi[8 * i : 8 * i + 4] = p[NY - W :]
    yhi[8 * i + 4 : 8 * i + 8] = s[NY - W :]


def first_kernel(c, s, p, obs, xlo, xhi, ylo, yhi, oc):
    oc[...] = jnp.zeros((16, 128), f32)
    oc[0:4, 0:64] = obs[...]
    for y in (ylo, yhi):
        y[80:88] = jnp.zeros((8, 128), f32)
        y[80:84, 0:64] = obs[...]
    for i in range(NX):
        put_strips(i, p[i], s[i], xlo, xhi, ylo, yhi)
    slab = pack([c[i] for i in range(NX)])
    ylo[64:80] = slab[:16]
    yhi[64:80] = slab[16:]


def fill(buf, field, rows_l, rows_r, md, mu, at, keep_d, keep_u):
    for i in range(NX):
        buf[W + i, 8:40] = field[i]
        buf[W + i, 4:8] = jnp.where(keep_d, md[8 * i + at : 8 * i + at + 4], 0.0)
        buf[W + i, 40:44] = jnp.where(keep_u, mu[8 * i + at : 8 * i + at + 4], 0.0)
    for j in range(W):
        buf[j, 8:40] = rows_l[j]
        buf[W + NX + j, 8:40] = rows_r[j]


def laplace(buf, i, wz):
    here = buf[W + i, 8:40]
    out = (3.0 * C0) * here
    for k in range(1, W + 1):
        beside = buf[W + i + k, 8:40] + buf[W + i - k, 8:40]
        beside = beside + buf[W + i, 8 + k : 40 + k] + buf[W + i, 8 - k : 40 - k]
        out = out + CK[k] * beside
        out = out + wz[k][0] * roll(here, -k) + wz[k][1] * roll(here, k)
    return out


def depth_weights():
    lane = lanes()
    return [None] + [
        (jnp.where(lane < NZ - k, CK[k], 0.0), jnp.where(lane >= k, CK[k], 0.0))
        for k in range(1, W + 1)
    ]


def edges():
    iy = lax.axis_index("gy")
    return iy > 0, iy < lax.axis_size("gy") - 1


def strip(m, at):
    return [m[at + NY * j : at + NY * (j + 1)] for j in range(W)]


def add_source(n, source, start, wavelet, field):
    width = NY * lax.axis_size("gy")
    sx = source[0] // width - lax.axis_index("gx") * NX
    sy = source[0] % width - lax.axis_index("gy") * NY

    @pl.when((sx >= 0) & (sx < NX) & (sy >= 0) & (sy < NY))
    def _():
        row = field[sx, pl.ds(sy, 1), :]
        add = jnp.where(lanes() == SRC_DEPTH, wavelet[0, start[0] + n], 0.0)
        field[sx, pl.ds(sy, 1), :] = row + add


def collect(n, md, mu, oc, oc_out):
    at = 80 if n == 0 else 64
    got_d, got_u = md[at : at + 8], mu[at : at + 8]
    oc_out[...] = oc[...]
    up, turn_u, down, turn_d = ((0, 64, 12, 64), (4, 0, 12, 0), (4, 64, 8, 64), (8, 0, None, 0))[n]
    oc_out[up : up + 4] = oc_out[up : up + 4] + roll(got_u, turn_u)[:4]
    if down is not None:
        oc_out[down : down + 4] = oc_out[down : down + 4] + roll(got_d, turn_d)[:4]
    return got_d, got_u


def step_kernel(n, source, start, wavelet, c, p, pp, q, ql, ml, mr, md, mu, oc, *rest):
    if n == 0:
        lpk, oc_out, qn, pn, xlo, xhi, ylo, yhi, lap_out, cext, bufp, bufs = rest
    if n == 1:
        cext, lpk, oc_out, qn, pn, xlo, xhi, ylo, yhi, lap_out, bufp, bufs = rest
    if n == 2:
        lap_other, lpk, oc_out, qn, pn, xlo, xhi, ylo, yhi, img_out, mat, bufp, bufs = rest
    keep_d, keep_u = edges()
    lane = lanes()
    wz = depth_weights()
    fill(bufp, p, strip(ml, 0), strip(mr, 0), md, mu, 0, keep_d, keep_u)
    s = [c[i] * q[i] for i in range(NX)]
    fill(bufs, s, strip(ml, 128), strip(mr, 128), md, mu, 4, keep_d, keep_u)
    slab = jnp.zeros((NY, NZ), f32)
    for i in range(NX):
        lap = laplace(bufp, i, wz)
        slab = jnp.where(lane // SLAB == i, roll(lap, SLAB * i), slab)
        pn[i] = 2.0 * p[i] - pp[i] + c[i] * lap
        q_new = 2.0 * q[i] - ql[i] + laplace(bufs, i, wz)
        qn[i] = q_new
        if n < 2:
            lap_out[i] = lap
        else:
            img_out[i] = lap * q[i] + q_new * lap_other[i]
    lpk[...] = slab
    add_source(n, source, start, wavelet, pn)
    got_d, got_u = collect(n, md, mu, oc, oc_out)
    for i in range(NX):
        put_strips(i, pn[i], c[i] * qn[i], xlo, xhi, ylo, yhi)
    ylo[64:72] = got_u
    yhi[64:72] = got_d
    if n == 0:
        cext[0:16] = jnp.where(keep_d, md[64:80], 0.0)
        cext[16:48] = pack([c[i] for i in range(NX)])
        cext[48:64] = jnp.where(keep_u, mu[64:80], 0.0)
        xlo[256:320] = cext[...]
        xhi[256:320] = cext[...]
    if n == 2:
        new = [pn[i] for i in range(NX)]
        slab = pack(new)
        d = lane % SLAB
        deep = (3.0 * C0) * slab
        for k in range(1, W + 1):
            deep = deep + jnp.where(d < SLAB - k, CK[k], 0.0) * roll(slab, -k)
            deep = deep + jnp.where(d >= k, CK[k], 0.0) * roll(slab, k)
        out = jnp.zeros((NY, NZ), f32)
        for i in range(NX):
            for t, row, at in (
                (0, pp[i], REC_DEPTH),
                (1, p[i], REC_DEPTH),
                (2, new[i], REC_DEPTH),
                (3, deep, SLAB * i + REC_DEPTH),
            ):
                out = jnp.where(lane == 4 * i + t, roll(row, 4 * i + t - at), out)
        mat[...] = out
        ylo[72:88] = out[:16]
        yhi[72:88] = out[16:]
    if n == 1:
        xlo[256:288] = mr[272:304]
        xhi[256:288] = ml[272:304]


def final_kernel(
    c, p, q, ql, ml, mr, md, mu, lap0, q3, img, vel, noise, image_in, driven, vpk, zpk,
    own, sent, part, bufp, bufs,
):
    keep_d, keep_u = edges()
    lane = lanes()
    wz = depth_weights()
    first = lax.axis_index("shot") % 2 == 0
    fill(bufp, p, strip(ml, 0), strip(mr, 0), md, mu, 0, keep_d, keep_u)
    s = [c[i] * q[i] for i in range(NX)]
    fill(bufs, s, strip(ml, 128), strip(mr, 128), md, mu, 4, keep_d, keep_u)
    slab = jnp.zeros((NY, NZ), f32)
    for i in range(NX):
        lap = laplace(bufp, i, wz)
        slab = jnp.where(lane // SLAB == i, roll(lap, SLAB * i), slab)
        q_new = 2.0 * q[i] - ql[i] + laplace(bufs, i, wz)
        image = img[i] + lap * q3[i] + q_new * lap0[i]
        grad = (2.0 * courant_sq) * vel[i] * image
        weighted = grad * noise[i]
        own[i] = jnp.where(first, grad, weighted)
        sent[i] = jnp.where(first, weighted, grad)
    grad = (2.0 * courant_sq) * vpk[...] * (image_in[...] + driven[...] * slab)
    part[0:NY] = grad
    part[NY : 2 * NY] = grad * zpk[...]


def chunk_kernel(mat, md, mu, oc, _, out, traces):
    keep_d, keep_u = edges()
    collect(3, md, mu, oc, traces)
    packed = jnp.where(keep_d, md[72:88], 0.0) + roll(jnp.where(keep_u, mu[72:88], 0.0), 96)
    packed = packed + roll(mat[0:16], 32) + roll(mat[16:32], 64)
    for g in range(out.shape[0]):
        out[g, 0:16] = traces[...]
        out[g, 16:32] = packed


def lap_packed(buf, g, lo, hi, wz):
    lane = lanes()
    here = buf[g, lo:hi]
    before, after = buf[g - 1, lo:hi], buf[g + 1, lo:hi]
    out = (3.0 * C0) * here
    for k in range(1, W + 1):
        t = SLAB * k
        beside = jnp.where(lane < 128 - t, roll(here, -t), roll(after, -t))
        beside = beside + jnp.where(lane >= t, roll(here, t), roll(before, t))
        beside = beside + buf[g, lo + k : hi + k] + buf[g, lo - k : hi - k]
        out = out + CK[k] * beside
        out = out + wz[k][0] * roll(here, -k) + wz[k][1] * roll(here, k)
    return out


def table_kernel(rec, vel, noise, keyx, keyy, count, vpk, zpk, cols, rows, hot, hoty):
    ix, iy, ngy = lax.axis_index("gx"), lax.axis_index("gy"), lax.axis_size("gy")
    half = ngy // 2
    bits = (NY * ngy).bit_length() - 1
    assert 2**bits == NY * ngy
    odd = iy % 2 == 1
    low = lanes() < 64
    bf = jnp.bfloat16
    coly = lax.broadcasted_iota(jnp.int32, (64, 128), 0).astype(f32).astype(bf)
    row4 = (lax.broadcasted_iota(jnp.int32, (128, 128), 0) // 4).astype(f32).astype(bf)
    one, none = jnp.ones((), bf), jnp.zeros((), bf)
    kx = jnp.clip((rec[...] >> bits) - ix * NX + 12, -1, 32).astype(f32)
    ky = jnp.clip((rec[...] & (NY * ngy - 1)) - iy * NY + 16, -1, 64).astype(f32)
    for ref, k in ((rows, kx), (cols, ky)):
        ref[0] = jnp.where(odd, roll(k, 64), k)
    for g in range(rec.shape[0]):
        first = (iy + 2 * (g % half)) % ngy
        a = pl.ds((g // half) * half + first // 2, 1)
        b = pl.ds((g // half) * half + ((first + 1) % ngy) // 2, 1)
        key = jnp.where(low, rows[0, a, :], rows[0, b, :])
        keyx[g : g + 1] = key
        hot[:, 128 * g : 128 * (g + 1)] = jnp.where(row4 == key.astype(bf), one, none)
        key = jnp.where(low, cols[0, a, :], cols[0, b, :])
        keyy[g : g + 1] = key
        hoty[:, 128 * g : 128 * (g + 1)] = jnp.where(coly == key.astype(bf), one, none)
    count[...] = lax.dot_general(
        hoty[...], hot[...], (((1,), (1,)), ((), ())), preferred_element_type=f32
    )
    vpk[...] = pack([vel[i] for i in range(NX)])
    zpk[...] = pack([noise[i] for i in range(NX)])


def last_kernel(
    got, keyx, keyy, count, cext, ml1, mr1, ml2, mr2, lp0, lp1, lp2, image, driven, table, hoty, x, r3, r2, r1, inj,
):
    ngx = got.shape[0]
    lane = lanes()
    ix = lax.axis_index("gx")
    c1l, c1r = ml1.at[256:320], mr1.at[256:320]
    c2l, c2r = ml2.at[256:288], mr2.at[256:288]
    bf = jnp.bfloat16
    row4 = (lax.broadcasted_iota(jnp.int32, (128, 128), 0) // 4).astype(f32).astype(bf)
    coly = lax.broadcasted_iota(jnp.int32, (64, 128), 0).astype(f32).astype(bf)
    one, none = jnp.ones((), bf), jnp.zeros((), bf)

    def build(g, carry):
        for rp in range(4):
            at = pl.ds(pl.multiple_of((4 * g + rp) * 128, 128), 128)
            val = got[g, 4 * rp : 4 * rp + 4, :]
            hi = val.astype(bf).astype(f32)
            mid = (val - hi).astype(bf).astype(f32)
            low = val - hi - mid
            here = row4 == keyx[pl.ds(4 * g + rp, 1), :].astype(bf)
            hoty[:, at] = jnp.where(coly == keyy[pl.ds(4 * g + rp, 1), :].astype(bf), one, none)
            for part, v in enumerate((hi, mid, low)):
                v16 = jnp.concatenate([v, v, v, v], 0).astype(bf)
                v128 = jnp.concatenate([v16] * 8, 0)
                table[128 * part : 128 * (part + 1), at] = jnp.where(here, v128, none)
        at = pl.ds(pl.multiple_of(g * 512, 512), 512)
        return carry + lax.dot_general(
            hoty[:, at], table[:, at], (((1,), (1,)), ((), ())), preferred_element_type=f32
        )

    sums = lax.fori_loop(0, ngx, build, jnp.zeros((64, 384), f32), unroll=ngx)
    seen = sums[:, 0:128] + sums[:, 128:256] + sums[:, 256:384]
    counts = count[...]

    k_in = lax.broadcasted_iota(jnp.int32, (128, 512), 0)
    k_out = lax.broadcasted_iota(jnp.int32, (128, 512), 1)
    spread_to = jnp.where(
        (k_in < 32) & (k_out == (k_in % 4) * 128 + (k_in // 4) * SLAB + REC_DEPTH), 1.0, 0.0
    )
    dense, raw = [], []
    for g in range(5):
        src = ix + (g - 2)
        ok = (src >= 0) & (src < ngx)
        blk = got[jnp.clip(src, 0, ngx - 1), 16:32, :]
        m = jnp.concatenate([roll(blk, -32 * t) for t in range(4)], 0)
        m = jnp.where(ok, m, 0.0)
        s_g = roll(seen, 16 - 32 * g)
        n_g = roll(counts, 16 - 32 * g)
        dense.append(jnp.where(lane % 4 == 3, 0.0, n_g * m) - s_g)
        raw.append(jnp.where(lane % 4 == 0, n_g, m))
    whole = jnp.concatenate(dense + raw, 0)
    hi = whole.astype(bf)
    rest = whole - hi.astype(f32)
    mid = rest.astype(bf)
    low = (rest - mid.astype(f32)).astype(bf)
    to = spread_to.astype(bf)
    inj[...] = (
        jnp.dot(hi, to, preferred_element_type=f32)
        + jnp.dot(mid, to, preferred_element_type=f32)
        + jnp.dot(low, to, preferred_element_type=f32)
    )

    def j(n, g, lo, hi):
        return inj[64 * g + lo : 64 * g + hi, 128 * n : 128 * (n + 1)]

    coef = {1: c1l, 2: cext, 3: c1r}
    pad = jnp.zeros((16, 128), f32)
    plane = [j(2, 5 + g, 0, 64) for g in range(5)]
    for g in range(5):
        x[g] = plane[g]
    for g in range(5):
        lo, hi = (16, 48) if g in (0, 4) else (4, 60)
        part = j(3, 5 + g, lo, hi)
        for k in range(1, W + 1):
            t = SLAB * k
            here = x[g, lo:hi]
            after = x[g + 1, lo:hi] if g < 4 else jnp.zeros_like(here)
            before = x[g - 1, lo:hi] if g > 0 else jnp.zeros_like(here)
            beside = jnp.where(lane < 128 - t, roll(here, -t), roll(after, -t))
            beside = beside + jnp.where(lane >= t, roll(here, t), roll(before, t))
            beside = beside + x[g, lo + k : hi + k] + x[g, lo - k : hi - k]
            part = part + CK[k] * jnp.where(lane % SLAB == REC_DEPTH, beside, 0.0)
        c_g = (c2l, c2r)[g // 4][...] if g in (0, 4) else coef[g][lo:hi]
        p4 = 2.0 * x[g, lo:hi] - j(1, 5 + g, lo, hi) + c_g * part
        r3[g] = j(3, g, 0, 64)
        r3[g, lo:hi] = r3[g, lo:hi] + j(0, 5 + g, lo, hi) * p4

    d = lane % SLAB
    wz = [None] + [
        (jnp.where(d < SLAB - k, CK[k], 0.0), jnp.where(d >= k, CK[k], 0.0))
        for k in range(1, W + 1)
    ]
    for g in coef:
        x[g] = coef[g][...] * r3[g]
    for g, far in ((0, c2l), (4, c2r)):
        x[g, 0:16] = pad
        x[g, 16:48] = far[...] * r3[g, 16:48]
        x[g, 48:64] = pad
    for g in (1, 2, 3):
        r2[g] = 2.0 * r3[g, 8:56] + lap_packed(x, g, 8, 56, wz) + j(2, g, 8, 56)
    x[0] = jnp.zeros((64, 128), f32)
    x[4] = jnp.zeros((64, 128), f32)
    for g in (1, 2, 3):
        x[g, 0:8] = pad[:8]
        x[g, 8:56] = coef[g][8:56] * r2[g]
        x[g, 56:64] = pad[:8]
    for g in (1, 2, 3):
        r1[g] = 2.0 * r2[g] - r3[g, 8:56] + lap_packed(x, g, 8, 56, wz) + j(1, g, 8, 56)
    for g in (1, 2, 3):
        x[g, 8:56] = coef[g][8:56] * r1[g]
    r0 = 2.0 * r1[2, 8:40] - r2[2, 8:40] + lap_packed(x, 2, 16, 48, wz) + j(0, 2, 16, 48)
    image[...] = r0 * lp0[...] + r1[2, 8:40] * lp1[...] + r2[2, 8:40] * lp2[...]
    driven[...] = r3[2, 16:48]


def tail_kernel(own, other, part, out):
    cells = NX * NY
    for i in range(NX):
        out[NY * i : NY * (i + 1)] = own[i] + other[i]
    out[cells : cells + 2 * NY] = part[...]


def sum_kernel(every, logs, grad_mean, grad_logs):
    lane = lanes()
    cells = NX * NY

    def packed(at):
        rows = slice(at, at + NY)
        return (every[0, rows] + every[1, rows]) + (every[2, rows] + every[3, rows])

    grad_in, weighted_in = packed(cells), packed(cells + NY)
    for i in range(NX):
        rows = slice(NY * i, NY * (i + 1))
        grad = every[0, rows] + every[2, rows]
        grad_mean[i] = grad + jnp.where(lane < SLAB, roll(grad_in, -SLAB * i), 0.0)
        weighted = every[1, rows] + every[3, rows]
        weighted = weighted + jnp.where(lane < SLAB, roll(weighted_in, -SLAB * i), 0.0)
        spread = jnp.exp(logs[i])
        grad_logs[i] = spread * weighted + jnp.exp(2.0 * logs[i]) / prior_var - 1.0


def call(kernel, outs, scratch=(), smem=0, mib=4):
    def go(*args):
        return pl.pallas_call(
            kernel,
            out_shape=outs,
            in_specs=[SM] * smem + [VM] * (len(args) - smem),
            out_specs=jax.tree.map(lambda _: VM, outs),
            scratch_shapes=list(scratch),
            compiler_params=pltpu.CompilerParams(vmem_limit_bytes=mib * 2**20),
        )(*args)

    return go


def shift(x, axis, k, wrap=False):
    n = lax.axis_size(axis)
    return lax.ppermute(x, axis, [(i, (i + k) % n) for i in range(n) if wrap or 0 <= i + k < n])


def local(
    mean_velocity,
    log_scale,
    shot_noise,
    checkpoint_prev,
    checkpoint_now,
    adjoint_next,
    adjoint_now,
    wavelet,
    source_column,
    receiver_column,
    observed,
    start_step,
):
    ngx, ngy, nshot = lax.axis_size("gx"), lax.axis_size("gy"), lax.axis_size("shot")
    noise = shot_noise[0]
    p_prev, p = checkpoint_prev[0], checkpoint_now[0]
    q_later, q = adjoint_next[0], adjoint_now[0]
    F = sds(NX, NY, NZ)
    vel = mean_velocity + jnp.exp(log_scale) * noise
    coef = courant_sq * vel * vel
    xlo, xhi, ylo, yhi, oc = call(
        first_kernel,
        (sds(256, 128), sds(256, 128), sds(88, 128), sds(88, 128), sds(16, 128)),
    )(coef, coef * q, p, observed[0])
    buf = pltpu.VMEM((NX + 2 * W, 48, NZ), f32)
    slabs, keep = [], {}
    for n in range(STEPS):
        ml, mr = shift(xhi, "gx", 1), shift(xlo, "gx", -1)
        md, mu = shift(yhi, "gy", 1, True), shift(ylo, "gy", -1, True)
        halos = (ml, mr, md, mu)
        if n == STEPS - 1:
            break
        extra = {1: (keep.get("cext"),), 2: (keep.get("lap1"),)}.get(n, ())
        rows = (320, 288, 256)[n]
        outs = [sds(NY, NZ), sds(16, 128), F, F]
        cols = (72, 72, 88)[n]
        outs += [sds(rows, 128), sds(rows, 128), sds(cols, 128), sds(cols, 128), F]
        if n != 1:
            outs.append(sds(64, 128) if n == 0 else sds(NY, NZ))
        res = call(functools.partial(step_kernel, n), tuple(outs), (buf, buf), smem=3)(
            source_column, start_step, wavelet, coef, p, p_prev, q, q_later, *halos, oc, *extra
        )
        lpk, oc, q_next, p_next, xlo, xhi, ylo, yhi = res[:8]
        slabs.append(lpk)
        if n == 0:
            keep["lap0"], keep["cext"], keep["q3"] = res[8], res[9], q_next
        if n == 1:
            keep["lap1"], keep["c"] = res[8], [ml, mr]
        if n == 2:
            img, mat = res[8], res[9]
            keep["c"] += [ml, mr]
        p_prev, p = p, p_next
        q_later, q = q, q_next

    nrec = receiver_column.shape[1]
    bf = jnp.bfloat16
    keyx, keyy, count, vpk, zpk = call(
        table_kernel,
        (
            sds(nrec // 128, 128),
            sds(nrec // 128, 128),
            sds(64, 128),
            sds(NY, NZ),
            sds(NY, NZ),
        ),
        [pltpu.VMEM((1, nrec // 128, 128), f32)] * 2
        + [pltpu.VMEM((128, nrec), bf), pltpu.VMEM((64, nrec), bf)],
        mib=12,
    )(receiver_column.reshape(-1, 128), vel, noise)
    chunk = call(chunk_kernel, sds(ngx, 32, 128), (pltpu.VMEM((16, 128), f32),))(
        mat, md, mu, oc, count
    )
    got = lax.all_to_all(chunk, "gx", 0, 0)
    g5 = pltpu.VMEM((5, 64, 128), f32)
    g48 = pltpu.VMEM((5, 48, 128), f32)
    image_in, driven = call(
        last_kernel,
        (sds(NY, NZ), sds(NY, NZ)),
        (pltpu.VMEM((384, nrec), bf), pltpu.VMEM((64, nrec), bf), g5, g5, g48, g48, pltpu.VMEM((640, 512), f32)),
        mib=24,
    )(got, keyx, keyy, count, keep["cext"], *keep["c"], *slabs)
    own, sent, part = call(final_kernel, (F, F, sds(2 * NY, NZ)), (buf, buf))(
        coef, p, q, q_later, *halos, keep["lap0"], keep["q3"], img, vel, noise,
        image_in, driven, vpk, zpk,
    )
    other = lax.ppermute(sent, "shot", [(i, i ^ 1) for i in range(nshot)])
    part = call(tail_kernel, sds(NX * NY + 2 * NY, NZ))(own, other, part)
    every = lax.all_gather(part, "shot", axis=0)
    return call(sum_kernel, (F, F))(every, log_scale)


def solution(mesh):
    return jax.shard_map(
        local,
        mesh=mesh,
        in_specs=(
            P("gx", "gy", None),
            P("gx", "gy", None),
            P("shot", "gx", "gy", None),
            P("shot", "gx", "gy", None),
            P("shot", "gx", "gy", None),
            P("shot", "gx", "gy", None),
            P("shot", "gx", "gy", None),
            P("shot", None),
            P("shot"),
            P("shot", None),
            P("shot", None, ("gx", "gy")),
            P(),
        ),
        out_specs=(P("gx", "gy", None), P("gx", "gy", None)),
        check_vma=False,
    )
```
